32 devices in a mesh: narrow: 4 (over x, core), wide: 8 (over z, y).
Axes of the slice: x: 2, y: 2, z: 4, core: 2. Of those that a mesh axis runs over, the one named last changes fastest.
Arguments:
- inputs: bfloat16 [4, 3136, 2048], P(None, 'wide', 'narrow'), may hold values from -12 to 12
- sides: int32 [4, 64], P(None, 'wide'), may hold values from 5 to 7, as said below
- w_first: bfloat16 [2048, 512], P('wide', 'narrow'), may hold values from -0.125 to 0.125
- w_middle: bfloat16 [3, 3, 512, 512], P(None, None, 'wide', 'narrow'), may hold values from -0.09375 to 0.09375
- w_last: bfloat16 [512, 2048], P('wide', 'narrow'), may hold values from -0.25 to 0.25
- gain_first: float32 [512], P('narrow'), may hold values from 0.25 to 1.75
- shift_first: float32 [512], P('narrow'), may hold values from -1.2 to 1.2
- gain_middle: float32 [512], P('narrow'), may hold values from 0.25 to 1.75
- shift_middle: float32 [512], P('narrow'), may hold values from -1.2 to 1.2
- gain_last: float32 [2048], P('narrow'), may hold values from 0.25 to 1.75
- shift_last: float32 [2048], P('narrow'), may hold values from -1.2 to 1.2
- cotangent: bfloat16 [4, 3136, 2048], P(None, 'wide', 'narrow'), may hold values from -6 to 6
Outputs:
- block_out: bfloat16 [4, 3136, 2048], P(None, 'wide', 'narrow')
- input_grad: float32 [4, 3136, 2048], P(None, 'wide', 'narrow')
- grad_first: float32 [2048, 512], P('wide', 'narrow')
- grad_middle: float32 [3, 3, 512, 512], P(None, None, 'wide', 'narrow')
- grad_last: float32 [512, 2048], P('wide', 'narrow')
- grad_gain_first: float32 [512], P('narrow')
- grad_shift_first: float32 [512], P('narrow')
- grad_gain_middle: float32 [512], P('narrow')
- grad_shift_middle: float32 [512], P('narrow')
- grad_gain_last: float32 [2048], P('narrow')
- grad_shift_last: float32 [2048], P('narrow')
The draws below stay inside these ranges and needn't reach their ends.
Inputs may be any that keep to these rules, and one draw needn't show every extreme that they name: `sides`: each micro-batch of each index of wide holds at least one image of side 7 and one of side 5.
All inputs are finite; a program needn't handle non-finite values.
Results may differ from the reference program's by a relative error of at most 0.022.
Values may be sent and summed in bfloat16 or wider, within the bound.
No kernel may reach another device: no remote copies, remote signals or barrier semaphores. Data moves between devices by JAX's collectives and lax.ppermute only.
A program may use at most 192 MiB of HBM per device.

```python
import jax
import jax.numpy as jnp
from jax import lax

C = 2048
M = 512
IMG = 8
MICRO = 4
IMAGES = 64
PIXELS = 3136


def draw_inputs(key, part):
    key = jax.random.fold_in(key, 11)
    noise_key, scale_key = jax.random.split(key, 2)
    position = jnp.arange(IMAGES, dtype=jnp.float32) / (IMAGES - 1)
    rising = 0.6 * jnp.exp(position * jnp.log(3.0))
    rough = jax.random.uniform(scale_key, (MICRO, IMAGES, 1, 1), jnp.float32, 0.7, 1.4)
    noise = jax.random.normal(noise_key, (MICRO, IMAGES, 49, C), jnp.float32)
    values = jnp.clip(noise * rough * rising[None, :, None, None], -12.0, 12.0)
    return values.reshape(MICRO, IMAGES * 49, C).astype(jnp.bfloat16)


def draw_sides(key, part):
    key = jax.random.fold_in(key, 23)
    side_key, order_key = jax.random.split(key)
    drawn = jax.random.randint(side_key, (MICRO, IMAGES), 5, 8, dtype=jnp.int32)
    within = jnp.arange(IMAGES, dtype=jnp.int32) % IMG
    drawn = jnp.where(within == 0, 7, jnp.where(within == 1, 5, drawn))
    scores = jax.random.randint(order_key, (MICRO, IMAGES), 0, 1 << 20, dtype=jnp.int32) * IMAGES + jnp.arange(IMAGES, dtype=jnp.int32)
    blocks = IMAGES // IMG
    order = jnp.argsort(scores.reshape(MICRO, blocks, IMG), axis=-1)
    placed = jnp.take_along_axis(drawn.reshape(MICRO, blocks, IMG), order, axis=-1)
    return placed.reshape(MICRO, IMAGES).astype(jnp.int32)


def steps_of(stream_key, extent, pieces, least, largest):
    level = 1.0
    for dim, parts in pieces:
        heights = jax.random.uniform(jax.random.fold_in(jax.random.fold_in(stream_key, 6), dim), (parts,), jnp.float32, least / len(pieces), largest / len(pieces))
        level = level * jnp.repeat(jnp.exp(heights), extent[dim] // parts).reshape((-1,) + (1,) * (len(extent) - 1 - dim))
    return level


def gaussian(rng, dims, deviation, most, cuts=(), held_as=jnp.bfloat16):
    result = jax.random.normal(rng, dims, jnp.float32) * deviation
    if len(cuts) > 0:
        result = steps_of(rng, dims, cuts, -0.22, 0.18) * result
    return jnp.clip(result, min=-most, max=most).astype(held_as)


def setup_inputs(seed: int = 0) -> dict:
    key_list = jax.random.split(jax.random.key(seed), 13)
    return {
        "inputs": draw_inputs(jax.random.fold_in(key_list[12], 71), 0),
        "sides": draw_sides(jax.random.fold_in(key_list[12], 71), 0),
        "w_first": gaussian(key_list[2], (C, M), C ** -0.5, 0.125, ((0, 8), (1, 4))),
        "w_middle": gaussian(key_list[3], (3, 3, M, M), (9 * M) ** -0.5, 0.09375, ((2, 8), (3, 4))),
        "w_last": gaussian(key_list[4], (M, C), M ** -0.5, 0.25, ((0, 8), (1, 4))),
        "gain_first": jnp.clip(1.0 + 0.15 * jax.random.normal(key_list[5], (M,), jnp.float32), 0.25, 1.75),
        "shift_first": gaussian(key_list[6], (M,), 0.3, 1.2, ((0, 4),), jnp.float32),
        "gain_middle": jnp.clip(1.0 + 0.15 * jax.random.normal(key_list[7], (M,), jnp.float32), 0.25, 1.75),
        "shift_middle": gaussian(key_list[8], (M,), 0.3, 1.2, ((0, 4),), jnp.float32),
        "gain_last": jnp.clip(1.0 + 0.15 * jax.random.normal(key_list[9], (C,), jnp.float32), 0.25, 1.75),
        "shift_last": gaussian(key_list[10], (C,), 0.3, 1.2, ((0, 4),), jnp.float32),
        "cotangent": gaussian(key_list[11], (MICRO, PIXELS, C), 1.0, 6.0, ((1, 8), (2, 4))),
    }


@jax.custom_vjp
def low(v):
    return lax.optimization_barrier(v.astype(jnp.bfloat16)).astype(jnp.float32)

@jax.custom_vjp
def low_back(v):
    return v

def low_keep(v):
    return (low(v), None)

def low_pass(kept, grad):
    return (grad,)

def back_keep(v):
    return (v, None)

def back_low(kept, grad):
    return (low(grad),)
low.defvjp(low_keep, low_pass)
low_back.defvjp(back_keep, back_low)

def masks_of(sides):
    places = jnp.arange(7, dtype=jnp.int32)
    limit = sides[:, :, None, None]
    inside = (places[None, None, :, None] < limit) & (places[None, None, None, :] < limit)
    return inside.astype(jnp.float32).reshape(sides.shape[0], sides.shape[1] * 49, 1)

def normalize(values, mask, gain, shift):
    count = jnp.sum(mask)
    mean = lax.optimization_barrier(jnp.sum(mask * values, axis=0)) / count
    spread = lax.optimization_barrier(jnp.sum(mask * values * values, axis=0)) / count - mean * mean
    return gain * (values - mean) * lax.rsqrt(spread + 1e-05) + shift

def reference(inputs, sides, w_first, w_middle, w_last, gain_first, shift_first, gain_middle, shift_middle, gain_last, shift_last, cotangent):
    masks = masks_of(sides)
    highest = lax.Precision.HIGHEST

    def forward(inputs_f, first, middle, last, gain_one, shift_one, gain_two, shift_two, gain_three, shift_three):
        first_low = low(first)
        middle_low = low(middle)
        last_low = low(last)

        def one_batch(carry, pair):
            rows, mask = pair
            pre_first = low_back(jnp.dot(low(rows), first_low, precision=highest, preferred_element_type=jnp.float32))
            hidden_one = low(mask * jax.nn.silu(normalize(pre_first, mask, gain_one, shift_one)))
            canvas = hidden_one.reshape(IMAGES, 7, 7, M)
            convolved = lax.conv_general_dilated(canvas, middle_low, (1, 1), 'SAME', dimension_numbers=('NHWC', 'HWIO', 'NHWC'), precision=highest)
            pre_middle = low_back(convolved.reshape(IMAGES * 49, M))
            hidden_two = low(mask * jax.nn.silu(normalize(pre_middle, mask, gain_two, shift_two)))
            pre_last = low_back(jnp.dot(hidden_two, last_low, precision=highest, preferred_element_type=jnp.float32))
            summed = normalize(pre_last, mask, gain_three, shift_three) + rows
            return (carry, mask * jax.nn.silu(summed))
        start = jnp.zeros((), jnp.float32)
        _, outputs = lax.scan(jax.checkpoint(one_batch), start, (inputs_f, masks))
        return outputs
    outputs, pullback = jax.vjp(forward, inputs.astype(jnp.float32), w_first.astype(jnp.float32), w_middle.astype(jnp.float32), w_last.astype(jnp.float32), gain_first, shift_first, gain_middle, shift_middle, gain_last, shift_last)
    grads = pullback(cotangent.astype(jnp.float32))
    return (outputs.astype(jnp.bfloat16), grads[0], grads[1], grads[2], grads[3], grads[4], grads[5], grads[6], grads[7], grads[8], grads[9])
```

```python
import jax
import jax.numpy as jnp
from jax import lax
from jax.experimental import pallas as pl
from jax.experimental.pallas import tpu as pltpu
from jax.sharding import PartitionSpec as P


F32 = jnp.float32
BF = jnp.bfloat16
EPS = 1e-05
SIDE = 7
PITCH = 8
TAPS = 9
NARROW = 4
BOTH = ("wide", "narrow")
MESH = ("narrow", "wide")
VMEM_BYTES = 40 * 2**20


def dot(left, right):
    return jnp.dot(left, right, preferred_element_type=F32)


def dot_nt(left, right):
    return lax.dot_general(left, right, (((1,), (1,)), ((), ())), preferred_element_type=F32)


def dot_tn(left, right):
    return lax.dot_general(left, right, (((0,), (0,)), ((), ())), preferred_element_type=F32)


def run(kernel, scalars, operands, outs, scratch=(), flops=0):
    moved = sum(o.size * o.dtype.itemsize for o in (*operands, *outs))
    return pl.pallas_call(
        kernel,
        out_shape=outs,
        in_specs=[pl.BlockSpec(memory_space=pltpu.SMEM)] * len(scalars)
        + [pl.BlockSpec(memory_space=pltpu.VMEM)] * len(operands),
        out_specs=[pl.BlockSpec(memory_space=pltpu.VMEM)] * len(outs),
        scratch_shapes=list(scratch),
        cost_estimate=pl.CostEstimate(flops=flops, bytes_accessed=moved, transcendentals=0),
        compiler_params=pltpu.CompilerParams(vmem_limit_bytes=VMEM_BYTES),
    )(*scalars, *operands)


def arr(shape, dtype):
    return jax.ShapeDtypeStruct(shape, dtype)


def by_rows(rows, body, carry, size=16):
    full = rows // size
    carry = lax.fori_loop(
        0, full, lambda i, c: body(pl.ds(pl.multiple_of(i * size, size), size), c), carry
    )
    if rows % size:
        carry = body(pl.ds(full * size, rows % size), carry)
    return carry


def fold(values):
    total = values[0:8]
    for start in range(8, values.shape[0], 8):
        total = total + values[start : start + 8]
    return total


def zeros_acc(channels):
    return (jnp.zeros((8, channels), F32), jnp.zeros((8, channels), F32))


def column_sum(acc):
    return jnp.sum(acc, axis=0, keepdims=True)


def sigmoid(values):
    return 0.5 * jnp.tanh(0.5 * values) + 0.5


def coefficients(total, squares, inverse, gain, shift):
    mean = total * inverse
    spread = squares * inverse - mean * mean
    scale = lax.rsqrt(spread + EPS)
    slope = gain * scale
    return mean, scale, slope, shift - mean * slope


def total_of(parts, index, wide):
    acc = parts[index]
    for place in range(1, wide):
        acc = acc + parts[place * NARROW + index]
    return acc


def total_wide(parts):
    acc = parts[0]
    for place in range(1, parts.shape[0]):
        acc = acc + parts[place]
    return acc


def wide_row(block, first, count=NARROW):
    return jnp.concatenate([block[first + k : first + k + 1] for k in range(count)], axis=1)


def row_of(block, first, index):
    rows = [jnp.where(index == k, block[first + k : first + k + 1], 0.0) for k in range(NARROW)]
    return rows[0] + rows[1] + rows[2] + rows[3]


def lane_block(index):
    return pl.ds(pl.multiple_of(index * 128, 128), 128)


def send_stats(message, first, second):
    for k in range(NARROW):
        message[0, k : k + 1, :] = first[:, 128 * k : 128 * k + 128]
        message[0, NARROW + k : NARROW + k + 1, :] = second[:, 128 * k : 128 * k + 128]
    repeat_first(message)


def repeat_first(message):
    block = message[0]
    for place in range(1, message.shape[0]):
        message[place] = block


def first_product(idx, x, *refs):
    pieces, (w_first, send_far, own_far, send_near, own_near) = refs[:-5], refs[-5:]
    n, z, y = idx[0], idx[1], idx[2]
    if len(pieces) == 1:
        w_first[...] = pieces[0][...]
    else:
        rows, cols = pieces[0].shape
        for place, piece in enumerate(pieces):
            half = y ^ (place // NARROW)
            block = (z - place % NARROW) & 3
            w_first[pl.ds(pl.multiple_of(half * rows, rows), rows), lane_block(block)] = piece[...]
    for ref, m in ((send_far, 3), (own_far, 2), (send_near, 1), (own_near, 0)):
        ref[...] = dot(x[n ^ m], w_first[...]).astype(ref.dtype)


def first_join(idx, own, near, far, mask, pre, message):
    b = idx[0]

    def body(ds, acc):
        values = own[ds, :] + near[ds, :].astype(F32) + far[ds, :].astype(F32)
        pre[ds, :] = values.astype(BF)
        kept = mask[b, ds, :] * values
        return acc[0] + fold(kept), acc[1] + fold(kept * values)

    sums = by_rows(own.shape[0], body, zeros_acc(own.shape[1]))
    send_stats(message, column_sum(sums[0]), column_sum(sums[1]))


def middle_forward(idx, inverse, pre0, pre1, pre2, pre3, parts, params, mask, to_canvas, to_rows, weight,
                   hidden, pre, coef, message, active, spread, joined):
    n = idx[0]
    wide = parts.shape[0] // NARROW
    rows, places = pre0.shape[0], to_canvas.shape[0]
    img = places // (SIDE * PITCH)
    margin = img * (PITCH + 1)
    gain = jnp.concatenate([params[k, 0:1, :] for k in range(NARROW)], axis=1)
    shift = jnp.concatenate([params[k, 1:2, :] for k in range(NARROW)], axis=1)
    spread[0:margin, :] = jnp.zeros((margin, spread.shape[1]), F32)
    spread[margin + places :, :] = jnp.zeros((margin, spread.shape[1]), F32)
    line = img * PITCH
    for m, source in enumerate((pre0, pre1, pre2, pre3)):
        b = n ^ m
        block = total_of(parts, b, wide)
        mean, scale, slope, offset = coefficients(
            wide_row(block, 0), wide_row(block, NARROW), inverse[b], gain, shift
        )
        for k, row in enumerate((mean, scale, slope, offset)):
            coef[m, k : k + 1, :] = row

        def activate(ds, carry):
            act = source[ds, :].astype(F32) * slope + offset
            active[ds, :] = (mask[b, ds, :] * act * sigmoid(act)).astype(BF)
            return carry

        by_rows(rows, activate, 0)
        hidden[m] = dot(to_canvas[...], active[...]).astype(BF)
        spread[margin : margin + places, :] = dot(hidden[m], weight[...])
        for top in range(SIDE):
            acc = None
            for tap in range(TAPS):
                start = margin + top * line + ((tap // 3 - 1) * PITCH + tap % 3 - 1) * img
                part = spread[start : start + line, 128 * tap : 128 * tap + 128]
                acc = part if acc is None else acc + part
            joined[top * line : (top + 1) * line, :] = acc.astype(BF)
        pre[m] = dot(to_rows[...], joined[...]).astype(BF)

        def collect(ds, acc):
            values = pre[m, ds, :].astype(F32)
            kept = mask[b, ds, :] * values
            return acc[0] + fold(kept), acc[1] + fold(kept * values)

        sums = by_rows(rows, collect, zeros_acc(128))
        message[0, 2 * m : 2 * m + 1, :] = column_sum(sums[0])
        message[0, 2 * m + 1 : 2 * m + 2, :] = column_sum(sums[1])
    repeat_first(message)


def last_forward(idx, inverse, src0, src1, src2, src3, parts, params, mask, weight,
                 hidden, own, coef, pre, message):
    n = idx[0]
    wide = parts.shape[0] // NARROW
    rows = own.shape[0]
    sources = (src0, src1, src2, src3)
    blocks = [total_of(parts, n ^ i, wide) for i in range(NARROW)]
    for m in range(NARROW):
        b = n ^ m
        for i in range(NARROW):
            j = m ^ i
            here = lane_block(n ^ i)
            mean, scale, slope, offset = coefficients(
                blocks[i][2 * j : 2 * j + 1], blocks[i][2 * j + 1 : 2 * j + 2], inverse[b],
                params[n ^ i, 2:3, :], params[n ^ i, 3:4, :],
            )
            if m == 0:
                own[:, here] = sources[i][j]
                for k, row in enumerate((mean, scale, slope, offset)):
                    coef[k : k + 1, here] = row

            def activate(ds, carry):
                act = sources[i][j, ds, :].astype(F32) * slope + offset
                hidden[m, ds, here] = (mask[b, ds, :] * act * sigmoid(act)).astype(BF)
                return carry

            by_rows(rows, activate, 0, 32)
        pre[m] = dot(hidden[m], weight[...])

        def collect(ds, acc):
            values = pre[m, ds, :]
            kept = mask[b, ds, :] * values
            return acc[0] + fold(kept), acc[1] + fold(kept * values)

        sums = by_rows(rows, collect, zeros_acc(pre.shape[2]))
        message[0, 2 * m : 2 * m + 1, :] = column_sum(sums[0])
        message[0, 2 * m + 1 : 2 * m + 2, :] = column_sum(sums[1])
    repeat_first(message)


def block_output(idx, inverse, pre, x, cotangent, parts, gain, shift, mask, out, grad, coef, message):
    n = idx[0]
    rows, channels = pre.shape[1:]
    block = total_wide(parts)
    for m in range(NARROW):
        b = n ^ m
        mean, scale, slope, offset = coefficients(
            block[2 * m : 2 * m + 1], block[2 * m + 1 : 2 * m + 2], inverse[b], gain[...], shift[...]
        )
        for k, row in enumerate((mean, scale, slope, offset)):
            coef[m, k : k + 1, :] = row
        back = mean * scale

        def body(ds, acc):
            values = pre[m, ds, :]
            inside = mask[b, ds, :]
            summed = values * slope + offset + x[b, ds, :].astype(F32)
            gate = sigmoid(summed)
            value = summed * gate
            out[b, ds, :] = (inside * value).astype(BF)
            local = inside * cotangent[b, ds, :].astype(F32) * (gate + value * (1.0 - gate))
            grad[m, ds, :] = local
            return acc[0] + fold(local), acc[1] + fold(local * (values * scale - back))

        sums = by_rows(rows, body, zeros_acc(channels))
        message[0, 2 * m : 2 * m + 1, :] = column_sum(sums[0])
        message[0, 2 * m + 1 : 2 * m + 2, :] = column_sum(sums[1])
    repeat_first(message)


def last_backward(idx, inverse, pre, grad, parts, coef, mask, weight,
                  grad_pre, send_far, own_far, send_near, own_near, sums):
    n = idx[0]
    rows = pre.shape[1]
    block = total_wide(parts)
    for s in range(2):
        acc = block[s : s + 1]
        for m in range(1, NARROW):
            acc = acc + block[2 * m + s : 2 * m + s + 1]
        sums[s : s + 1, :] = acc
    for m, ref in ((3, send_far), (2, own_far), (1, send_near), (0, own_near)):
        b = n ^ m
        mean, scale, slope = (coef[m, k : k + 1, :] for k in range(3))
        level = block[2 * m : 2 * m + 1] * inverse[b]
        tilt = block[2 * m + 1 : 2 * m + 2] * inverse[b]
        level, tilt = level - mean * scale * tilt, scale * tilt

        def body(ds, carry):
            away = mask[b, ds, :] * (level + pre[m, ds, :] * tilt)
            grad_pre[m, ds, :] = (slope * (grad[m, ds, :] - away)).astype(BF)
            return carry

        by_rows(rows, body, 0)
        ref[...] = dot_nt(grad_pre[m], weight[...]).astype(ref.dtype)


def middle_join(idx, own, near, far, pre, coef, mask, grad, message):
    b = idx[0]
    mean, scale, slope, offset = (coef[k : k + 1, :] for k in range(4))
    back = mean * scale

    def body(ds, acc):
        values = pre[ds, :].astype(F32)
        act = values * slope + offset
        gate = sigmoid(act)
        total = own[ds, :] + near[ds, :].astype(F32) + far[ds, :].astype(F32)
        local = total * mask[b, ds, :] * (gate * (1.0 + act * (1.0 - gate)))
        grad[ds, :] = local
        return acc[0] + fold(local), acc[1] + fold(local * (values * scale - back))

    sums = by_rows(own.shape[0], body, zeros_acc(own.shape[1]))
    send_stats(message, column_sum(sums[0]), column_sum(sums[1]))


def middle_backward(idx, inverse, grad, pre, parts, coef, mask, first_pre, first_coef, to_canvas, to_rows,
                    w0, w1, w2, w3, own, near, far, grad_first, sums, message,
                    grad_pre, weight, gathered, canvas):
    n = idx[0]
    wide = parts.shape[0] // NARROW
    rows, places = grad.shape[0], to_canvas.shape[0]
    img = places // (SIDE * PITCH)
    margin = img * (PITCH + 1)
    every = total_of(parts, 0, wide)
    for b in range(1, NARROW):
        every = every + total_of(parts, b, wide)
    sums[0:1, :] = row_of(every, 0, n)
    sums[1:2, :] = row_of(every, NARROW, n)
    block = total_of(parts, n, wide)
    mean, scale, slope = (coef[k : k + 1, :] for k in range(3))
    level = wide_row(block, 0) * inverse[n]
    tilt = wide_row(block, NARROW) * inverse[n]
    level, tilt = level - mean * scale * tilt, scale * tilt

    def body(ds, carry):
        away = mask[n, ds, :] * (level + pre[ds, :].astype(F32) * tilt)
        grad_pre[ds, :] = (slope * (grad[ds, :] - away)).astype(BF)
        return carry

    by_rows(rows, body, 0)
    own[...] = grad_pre[:, lane_block(n)]
    near[...] = grad_pre[:, lane_block(n ^ 1)]
    far[0] = grad_pre[:, lane_block(n ^ 2)]
    far[1] = grad_pre[:, lane_block(n ^ 3)]
    for j, piece in enumerate((w0, w1, w2, w3)):
        for tap in range(TAPS):
            weight[tap, :, lane_block(n ^ j)] = piece[:, 128 * tap : 128 * tap + 128]
    canvas[...] = dot(to_canvas[...], grad_pre[...]).astype(BF).astype(F32)
    gathered[...] = jnp.zeros_like(gathered)
    for tap in range(TAPS):
        start = margin + ((tap // 3 - 1) * PITCH + tap % 3 - 1) * img
        gathered[start : start + places, :] += dot_nt(canvas[...].astype(BF), weight[tap])
    canvas[...] = gathered[margin : margin + places, :]
    grad_pre[...] = dot(to_rows[...], canvas[...].astype(BF)).astype(BF)
    mean, scale, slope, offset = (first_coef[0, k : k + 1, :] for k in range(4))
    back = mean * scale

    def finish(ds, acc):
        values = first_pre[ds, :].astype(F32)
        act = values * slope + offset
        gate = sigmoid(act)
        local = grad_pre[ds, :].astype(F32) * mask[n, ds, :] * (gate * (1.0 + act * (1.0 - gate)))
        grad_first[ds, :] = local.astype(BF)
        return acc[0] + fold(local), acc[1] + fold(local * (values * scale - back))

    sums2 = by_rows(rows, finish, zeros_acc(grad.shape[1]))
    send_stats(message, column_sum(sums2[0]), column_sum(sums2[1]))


def first_backward(idx, inverse, g0, g1, g2, g3, p0, p1, p2, p3, parts, coef, mask, x, grad, weight,
                   grad_input, sums, out, grad_pre, acc):
    n, z, y = idx[0], idx[1], idx[2]
    wide = parts.shape[0] // NARROW
    rows, channels = g0.shape
    every = None
    for m, (g, pre) in enumerate(((g0, p0), (g1, p1), (g2, p2), (g3, p3))):
        b = n ^ m
        block = total_of(parts, b, wide)
        every = block if every is None else every + block
        mean, scale, slope = (coef[m, k : k + 1, :] for k in range(3))
        level = wide_row(block, 0) * inverse[b]
        tilt = wide_row(block, NARROW) * inverse[b]
        level, tilt = level - mean * scale * tilt, scale * tilt

        def body(ds, carry):
            away = mask[b, ds, :] * (level + pre[ds, :].astype(F32) * tilt)
            grad_pre[m, ds, :] = (slope * (g[ds, :].astype(F32) - away)).astype(BF)
            return carry

        by_rows(rows, body, 0)
        product = dot_tn(x[b], grad_pre[m])
        if m == 0:
            acc[...] = product
        else:
            acc[...] += product
    if len(out.shape) == 2:
        out[...] = acc[...]
    else:
        half, cols = out.shape[1:]
        for place in range(out.shape[0]):
            top = pl.multiple_of((y ^ (place // NARROW)) * half, half)
            out[place] = acc[pl.ds(top, half), lane_block((z - place % NARROW) & 3)].astype(BF)
    for m in range(NARROW):
        grad_input[n ^ m] = dot_nt(grad_pre[m], weight[...]) + grad[m]
    sums[0:1, :] = row_of(every, 0, n)
    sums[1:2, :] = row_of(every, NARROW, n)


def last_weight(idx, hidden, grad_pre, *refs):
    acc = refs[-1]
    for m in range(NARROW):
        product = dot_tn(hidden[m], grad_pre[m])
        if m == 0:
            acc[...] = product
        else:
            acc[...] += product
    hand_out(idx, acc, refs[:-1])


def hand_out(idx, acc, outs):
    if len(outs) == 1:
        outs[0][...] = acc[...]
        return
    z, y = idx[1], idx[2]
    own, away = outs
    rows = acc.shape[0] // 8
    for j in range(4):
        place = pl.ds(j * rows, rows)
        for ref, dy in ((own, 0), (away, 1)):
            top = ((z ^ j) * 2 + (y ^ dy)) * rows
            ref[place, :] = acc[pl.ds(pl.multiple_of(top, rows), rows), :].astype(ref.dtype)


def middle_weight(idx, hidden, q0, q1, q2, q3, to_canvas, *refs):
    outs, (acc, shifted, canvas) = refs[:-3], refs[-3:]
    places = to_canvas.shape[0]
    img = places // (SIDE * PITCH)
    margin = img * (PITCH + 1)
    canvas[0:margin, :] = jnp.zeros((margin, 128), F32)
    canvas[margin + places :, :] = jnp.zeros((margin, 128), F32)
    for m, piece in enumerate((q0, q1, q2, q3)):
        canvas[margin : margin + places, :] = dot(to_canvas[...], piece[...])
        for tap in range(TAPS):
            start = margin - ((tap // 3 - 1) * PITCH + tap % 3 - 1) * img
            shifted[:, 128 * tap : 128 * tap + 128] = canvas[start : start + places, :].astype(BF)
        product = dot_tn(hidden[m], shifted[...])
        if m == 0:
            acc[...] = product
        else:
            acc[...] += product
    hand_out(idx, acc, outs)


def gather_weights(idx, *refs):
    pieces, (w_middle, w_last) = refs[:-2], refs[-2:]
    z, y = idx[1], idx[2]
    rows = w_last.shape[0] // 8
    for place, piece in enumerate(pieces):
        for dy in range(2):
            top = pl.multiple_of(((z ^ place) * 2 + (y ^ dy)) * rows, rows)
            here = pl.ds(top, rows)
            for tap in range(TAPS):
                w_middle[here, 128 * tap : 128 * tap + 128] = piece[dy, tap * rows : (tap + 1) * rows, :]
            for k in range(NARROW):
                w_last[here, 128 * k : 128 * k + 128] = piece[dy, (TAPS + k) * rows : (TAPS + k + 1) * rows, :]


def sum_pieces(pieces, out):
    acc = pieces[0][...].astype(F32)
    for piece in pieces[1:]:
        acc = acc + piece[...].astype(F32)
    out[...] = acc


def swap_core(values):
    return lax.ppermute(values, "narrow", [(i, i ^ 1) for i in range(NARROW)])


def swap_chip(values):
    return lax.ppermute(values, "narrow", [(i, i ^ 2) for i in range(NARROW)])


def swap_wide(values, step, wide):
    return lax.ppermute(values, "wide", [(i, i ^ step) for i in range(wide)])


def from_all(values):
    far = swap_chip(values)
    near = swap_core(values)
    return values, near, far, swap_core(far)


def reduce_narrow(send_far, own_far, send_near, own_near):
    got_far = swap_core(send_far)
    got_near = swap_core(send_near)
    joined = (own_far + got_far.astype(F32)).astype(BF)
    return own_near, got_near, swap_chip(joined)


def exchange(message, axes):
    return lax.all_to_all(message, axes, 0, 0, tiled=True)


def reduce_wide(own, away, wide):
    rows = own.shape[0] // 4
    total = own + swap_wide(away, 1, wide).astype(F32)
    parts = [
        swap_wide(total[j * rows : (j + 1) * rows].astype(BF), 2 * j, wide).astype(F32)
        for j in range(1, 4)
    ]
    return total[0:rows] + parts[0] + parts[1] + parts[2]


def transposed_steps():
    steps = []
    for dy in range(2):
        for j in range(NARROW):
            pairs = []
            for k in range(NARROW):
                for z in range(4):
                    for y in range(2):
                        pairs.append((k * 8 + 2 * z + y, z * 8 + 2 * ((k + j) % 4) + (y ^ dy)))
            steps.append(pairs)
    return steps


def on_device(inputs, sides, w_first, w_middle, w_last, gain_first, shift_first, gain_middle, shift_middle,
              gain_last, shift_last, cotangent, *, wide):
    micro, rows, low = inputs.shape
    img = sides.shape[1]
    mid = w_last.shape[0] * wide
    cols = w_first.shape[1]
    places = img * SIDE * PITCH
    direct = wide == 8
    n = lax.axis_index("narrow")
    w = lax.axis_index("wide")
    idx = jnp.stack([n, w // 2, w % 2]).astype(jnp.int32)

    spots = jnp.arange(rows, dtype=jnp.int32)
    spot_y, spot_x, spot_img = spots % 49 // 7, spots % 7, spots // 49
    limit = jnp.repeat(sides, 49, axis=1)
    mask = ((spot_y[None] < limit) & (spot_x[None] < limit)).astype(F32)[:, :, None]
    place = (spot_y * PITCH + spot_x) * img + spot_img
    to_canvas = (jnp.arange(places, dtype=jnp.int32)[:, None] == place[None, :]).astype(BF)
    to_rows = (place[:, None] == jnp.arange(places, dtype=jnp.int32)[None, :]).astype(BF)

    if direct:
        steps = transposed_steps()
        first_pieces = [lax.ppermute(w_first, MESH, pairs) for pairs in steps]
    else:
        first_all = lax.all_gather(lax.all_gather(w_first, "narrow", axis=1, tiled=True), "wide", axis=0, tiled=True)
        first_pieces = [lax.dynamic_slice_in_dim(first_all, n * low, low, 0)]

    counts = jnp.sum((sides * sides).astype(F32), axis=1)
    small = jnp.concatenate(
        [gain_first[None], shift_first[None], gain_middle[None], shift_middle[None],
         jnp.broadcast_to(jnp.pad(counts, (0, 128 - micro))[None], (4, 128))], axis=0
    )
    smalls = exchange(jnp.broadcast_to(small[None], (wide * NARROW, 8, 128)), BOTH)
    params = smalls[0:NARROW]
    inverse = 1.0 / jnp.sum(smalls[::NARROW, 4, 0:micro], axis=0)

    if direct:
        share = w_last.shape[0]
        packed = jnp.concatenate(
            [w_middle.reshape(TAPS * share, 128)] + [w_last[:, 128 * k : 128 * k + 128] for k in range(NARROW)], axis=0
        )
        pair = jnp.stack([packed, swap_wide(packed, 1, wide)])
        pieces = [pair] + [swap_wide(pair, 2 * j, wide) for j in range(1, 4)]
        middle_slice, last_slice = run(
            gather_weights, (idx,), pieces, [arr((mid, TAPS * 128), BF), arr((mid, low), BF)]
        )
    else:
        middle_slice = lax.all_gather(w_middle, "wide", axis=2, tiled=True)
        middle_slice = middle_slice.reshape(TAPS, mid, 128).transpose(1, 0, 2).reshape(mid, TAPS * 128)
        last_slice = lax.all_gather(w_last, "wide", axis=0, tiled=True)

    everyone = arr((wide * NARROW, 8, 128), F32)
    across = arr((wide, 8, low), F32)
    flat = arr((rows, mid), BF)
    flat32 = arr((rows, mid), F32)

    w_rows, send_far, own_far, send_near, own_near = run(
        first_product, (idx,), (inputs, *first_pieces),
        [arr((low, mid), BF), flat, flat32, flat, flat32], flops=2 * micro * rows * low * mid,
    )
    joined = reduce_narrow(send_far, own_far, send_near, own_near)
    pre_one, message = run(first_join, (idx,), (*joined, mask), [flat, everyone])
    pre_ones = from_all(pre_one)
    parts_one = exchange(message, BOTH)

    hidden_one, pre_two, coef_one, message = run(
        middle_forward, (idx, inverse), (*pre_ones, parts_one, params, mask, to_canvas, to_rows, middle_slice),
        [arr((micro, places, mid), BF), arr((micro, rows, 128), BF), arr((micro, 8, mid), F32), everyone],
        [pltpu.VMEM((rows, mid), BF), pltpu.VMEM((places + 2 * img * (PITCH + 1), TAPS * 128), F32), pltpu.VMEM((places, 128), BF)],
        flops=2 * micro * places * mid * TAPS * 128,
    )
    pre_twos = from_all(pre_two)
    parts_two = exchange(message, BOTH)

    hidden_two, own_two, coef_two, pre_three, message = run(
        last_forward, (idx, inverse), (*pre_twos, parts_two, params, mask, last_slice),
        [arr((micro, rows, mid), BF), flat, arr((8, mid), F32), arr((micro, rows, low), F32), across],
        flops=2 * micro * rows * low * mid,
    )
    parts_three = exchange(message, "wide")
    block_out, grad_sum, coef_three, message = run(
        block_output, (idx, inverse),
        (pre_three, inputs, cotangent, parts_three, gain_last[None], shift_last[None], mask),
        [arr(inputs.shape, BF), arr((micro, rows, low), F32), arr((micro, 8, low), F32), across],
    )
    parts_four = exchange(message, "wide")

    grad_three, send_far, own_far, send_near, own_near, sums_three = run(
        last_backward, (idx, inverse), (pre_three, grad_sum, parts_four, coef_three, mask, last_slice),
        [arr((micro, rows, low), BF), flat, flat32, flat, flat32, arr((2, low), F32)],
        flops=2 * micro * rows * low * mid,
    )
    joined = reduce_narrow(send_far, own_far, send_near, own_near)
    grad_two, message = run(middle_join, (idx,), (*joined, own_two, coef_two, mask), [flat32, everyone])
    parts_five = exchange(message, BOTH)

    middle_slices = from_all(middle_slice)
    own_q, near_q, far_q, grad_one, sums_two, message = run(
        middle_backward, (idx, inverse),
        (grad_two, own_two, parts_five, coef_two, mask, pre_one, coef_one, to_canvas, to_rows, *middle_slices),
        [arr((rows, 128), BF), arr((rows, 128), BF), arr((2, rows, 128), BF), flat, arr((2, 128), F32), everyone],
        [pltpu.VMEM((rows, mid), BF), pltpu.VMEM((TAPS, mid, mid), BF),
         pltpu.VMEM((places + 2 * img * (PITCH + 1), mid), F32), pltpu.VMEM((places, mid), F32)],
        flops=2 * places * mid * TAPS * mid,
    )
    grad_ones = from_all(grad_one)
    parts_six = exchange(message, BOTH)
    got_near = swap_core(near_q)
    got_far = swap_chip(far_q)
    got_last = swap_core(got_far[1])

    out_first = arr((8, 2 * low // NARROW, cols), BF) if direct else arr((low, mid), F32)
    input_grad, sums_one, first_sum = run(
        first_backward, (idx, inverse),
        (*grad_ones, *pre_ones, parts_six, coef_one, mask, inputs, grad_sum, w_rows),
        [arr((micro, rows, low), F32), arr((2, 128), F32), out_first],
        [pltpu.VMEM((micro, rows, mid), BF), pltpu.VMEM((low, mid), F32)],
        flops=4 * micro * rows * low * mid,
    )

    def handed(channels):
        if direct:
            return [arr((mid // 2, channels), F32), arr((mid // 2, channels), BF)]
        return [arr((mid, channels), F32)]

    last_sum = run(
        last_weight, (idx,), (hidden_two, grad_three), handed(low), [pltpu.VMEM((mid, low), F32)],
        flops=2 * micro * rows * low * mid,
    )
    middle_sum = run(
        middle_weight, (idx,), (hidden_one, own_q, got_near, got_far[0], got_last, to_canvas), handed(TAPS * 128),
        [pltpu.VMEM((mid, TAPS * 128), F32), pltpu.VMEM((places, TAPS * 128), BF),
         pltpu.VMEM((places + 2 * img * (PITCH + 1), 128), F32)],
        flops=2 * micro * places * mid * TAPS * 128,
    )
    if direct:
        grad_last = reduce_wide(*last_sum, wide)
        grad_middle = reduce_wide(*middle_sum, wide)
        arrived = [
            lax.ppermute(first_sum[k], MESH, [(dst, src) for src, dst in pairs]) for k, pairs in enumerate(steps)
        ]
        grad_first = arrived[0].astype(F32)
        for piece in arrived[1:]:
            grad_first = grad_first + piece.astype(F32)
    else:
        grad_last = lax.psum_scatter(last_sum[0], "wide", scatter_dimension=0, tiled=True)
        grad_middle = lax.psum_scatter(middle_sum[0], "wide", scatter_dimension=0, tiled=True)
        whole = lax.psum(first_sum, "wide")
        whole = lax.all_gather(whole, "narrow", axis=0, tiled=True)
        share = whole.shape[0] // wide
        grad_first = lax.dynamic_slice(whole, (w * share, n * cols), (share, cols))
    share = grad_middle.shape[0]
    grad_middle = grad_middle.reshape(share, TAPS, 128).transpose(1, 0, 2).reshape(3, 3, share, 128)
    return (
        block_out, input_grad, grad_first, grad_middle, grad_last,
        sums_one[1], sums_one[0], sums_two[1], sums_two[0], sums_three[1], sums_three[0],
    )


def solution(mesh):
    wide = mesh.shape["wide"]
    placed = (
        P(None, "wide", "narrow"),
        P(None, "wide"),
        P("wide", "narrow"),
        P(None, None, "wide", "narrow"),
        P("wide", "narrow"),
        P("narrow"),
        P("narrow"),
        P("narrow"),
        P("narrow"),
        P("narrow"),
        P("narrow"),
        P(None, "wide", "narrow"),
    )
    return jax.shard_map(
        lambda *arrays: on_device(*arrays, wide=wide),
        mesh=mesh,
        in_specs=placed,
        out_specs=(
            P(None, "wide", "narrow"),
            P(None, "wide", "narrow"),
            P("wide", "narrow"),
            P(None, None, "wide", "narrow"),
            P("wide", "narrow"),
            P("narrow"),
            P("narrow"),
            P("narrow"),
            P("narrow"),
            P("narrow"),
            P("narrow"),
        ),
        check_vma=False,
    )
```

```python
import jax
import jax.numpy as jnp
from jax import lax
from jax.experimental import pallas as pl
from jax.experimental.pallas import tpu as pltpu
from jax.sharding import PartitionSpec as P


F32 = jnp.float32
BF = jnp.bfloat16
EPS = 1e-05
SIDE = 7
PITCH = 8
TAPS = 9
NARROW = 4
MESH = ("narrow", "wide")
VMEM_BYTES = 20 * 2**20


def dot(left, right):
    return jnp.dot(left, right, preferred_element_type=F32)


def dot_nt(left, right):
    return lax.dot_general(left, right, (((1,), (1,)), ((), ())), preferred_element_type=F32)


def dot_tn(left, right):
    return lax.dot_general(left, right, (((0,), (0,)), ((), ())), preferred_element_type=F32)


def position():
    n, w = lax.axis_index("narrow"), lax.axis_index("wide")
    return n, w // 2, w % 2


def run(kernel, operands, outs, scratch=(), flops=0):
    moved = sum(o.size * o.dtype.itemsize for o in (*operands, *outs))
    return pl.pallas_call(
        kernel,
        out_shape=outs,
        name=kernel.__name__,
        in_specs=[pl.BlockSpec(memory_space=pltpu.VMEM)] * len(operands),
        out_specs=[pl.BlockSpec(memory_space=pltpu.VMEM)] * len(outs),
        scratch_shapes=list(scratch),
        cost_estimate=pl.CostEstimate(flops=flops, bytes_accessed=moved, transcendentals=0),
        compiler_params=pltpu.CompilerParams(vmem_limit_bytes=VMEM_BYTES),
    )(*operands)


def arr(shape, dtype):
    return jax.ShapeDtypeStruct(shape, dtype)


def by_rows(rows, body, carry):
    return body(pl.ds(0, rows), carry)


def fold(values):
    total = values[0:8]
    for start in range(8, values.shape[0], 8):
        total = total + values[start : start + 8]
    return total


def zeros_acc(channels):
    return (jnp.zeros((8, channels), F32), jnp.zeros((8, channels), F32))


def column_sum(acc):
    return jnp.sum(acc, axis=0, keepdims=True)


def sigmoid(values):
    return 0.5 * jnp.tanh(0.5 * values) + 0.5


def coefficients(total, squares, inverse, gain, shift):
    mean = total * inverse
    spread = squares * inverse - mean * mean
    scale = lax.rsqrt(spread + EPS)
    slope = gain * scale
    return mean, scale, slope, shift - mean * slope


def wide_row(block, first, count=NARROW):
    return jnp.concatenate([block[first + k : first + k + 1] for k in range(count)], axis=1)


def row_of(block, first, index):
    rows = [jnp.where(index == k, block[first + k : first + k + 1], 0.0) for k in range(NARROW)]
    return rows[0] + rows[1] + rows[2] + rows[3]


def inverse_count(params, b, channels):
    row = params[b, 4:5, :]
    return row if channels == 128 else jnp.concatenate([row] * (channels // 128), axis=1)


def lane_block(index):
    return pl.ds(pl.multiple_of(index * 128, 128), 128)


def send_stats(message, first, second):
    for k in range(NARROW):
        message[k : k + 1, :] = first[:, 128 * k : 128 * k + 128]
        message[NARROW + k : NARROW + k + 1, :] = second[:, 128 * k : 128 * k + 128]


def first_product(x, *refs):
    pieces, (w_first, send_far, own_far, send_near, own_near) = refs[:-5], refs[-5:]
    n, z, y = position()
    if len(pieces) == 1:
        w_first[...] = pieces[0][...]
    else:
        rows, cols = pieces[0].shape
        for place, piece in enumerate(pieces):
            half = y ^ (place // NARROW)
            block = (z - place % NARROW) & 3
            w_first[pl.ds(pl.multiple_of(half * rows, rows), rows), lane_block(block)] = piece[...]
    for ref, m in ((send_far, 3), (own_far, 2), (send_near, 1), (own_near, 0)):
        ref[...] = dot(x[n ^ m], w_first[...]).astype(ref.dtype)


def first_join(own, near, far, mask, small, pre, message):
    b = position()[0]

    def body(ds, acc):
        values = own[ds, :] + near[ds, :].astype(F32) + far[ds, :].astype(F32)
        pre[ds, :] = values.astype(BF)
        kept = mask[b, ds, :] * values
        return acc[0] + fold(kept), acc[1] + fold(kept * values)

    sums = by_rows(own.shape[0], body, zeros_acc(own.shape[1]))
    send_stats(message, column_sum(sums[0]), column_sum(sums[1]))
    message[8:16, :] = small[...]


def middle_forward(pre0, pre1, pre2, pre3, sum0, sum1, sum2, sum3, mask, to_canvas, to_rows, weight,
                   hidden, pre, coef, message, params, active, spread, joined):
    n = position()[0]
    blocks = (sum0[...], sum1[...], sum2[...], sum3[...])
    for m, block in enumerate(blocks):
        params[n ^ m, 0:4, :] = block[8:12]
    for b in range(NARROW):
        params[b, 4:5, :] = 1.0 / blocks[0][12 + b : 13 + b]
        params[b, 5:8, :] = jnp.zeros((3, 128), F32)
    rows, places = pre0.shape[0], to_canvas.shape[0]
    img = places // (SIDE * PITCH)
    margin = img * (PITCH + 1)
    gain = jnp.concatenate([params[k, 0:1, :] for k in range(NARROW)], axis=1)
    shift = jnp.concatenate([params[k, 1:2, :] for k in range(NARROW)], axis=1)
    spread[0:margin, :] = jnp.zeros((margin, spread.shape[1]), F32)
    spread[margin + places :, :] = jnp.zeros((margin, spread.shape[1]), F32)
    line = img * PITCH
    for m, source in enumerate((pre0, pre1, pre2, pre3)):
        b = n ^ m
        block = blocks[m]
        mean, scale, slope, offset = coefficients(
            wide_row(block, 0), wide_row(block, NARROW), inverse_count(params, b, gain.shape[1]), gain, shift
        )
        for k, row in enumerate((mean, scale, slope, offset)):
            coef[m, k : k + 1, :] = row

        def activate(ds, carry):
            act = source[ds, :].astype(F32) * slope + offset
            active[ds, :] = (mask[b, ds, :] * act * sigmoid(act)).astype(BF)
            return carry

        by_rows(rows, activate, 0)
        hidden[m] = dot(to_canvas[...], active[...]).astype(BF)
        spread[margin : margin + places, :] = dot(hidden[m], weight[...])
        for top in range(SIDE):
            acc = None
            for tap in range(TAPS):
                start = margin + top * line + ((tap // 3 - 1) * PITCH + tap % 3 - 1) * img
                part = spread[start : start + line, 128 * tap : 128 * tap + 128]
                acc = part if acc is None else acc + part
            joined[top * line : (top + 1) * line, :] = acc.astype(BF)
        pre[m] = dot(to_rows[...], joined[...]).astype(BF)

        def collect(ds, acc):
            values = pre[m, ds, :].astype(F32)
            kept = mask[b, ds, :] * values
            return acc[0] + fold(kept), acc[1] + fold(kept * values)

        sums = by_rows(rows, collect, zeros_acc(128))
        message[2 * m : 2 * m + 1, :] = column_sum(sums[0])
        message[2 * m + 1 : 2 * m + 2, :] = column_sum(sums[1])


def last_forward(src0, src1, src2, src3, sum0, sum1, sum2, sum3, params, mask, weight,
                 hidden, own, coef, pre, message):
    n = position()[0]
    rows = own.shape[0]
    sources = (src0, src1, src2, src3)
    blocks = (sum0[...], sum1[...], sum2[...], sum3[...])
    for m in range(NARROW):
        b = n ^ m
        for i in range(NARROW):
            j = m ^ i
            here = lane_block(n ^ i)
            mean, scale, slope, offset = coefficients(
                blocks[i][2 * j : 2 * j + 1], blocks[i][2 * j + 1 : 2 * j + 2], inverse_count(params, b, 128),
                params[n ^ i, 2:3, :], params[n ^ i, 3:4, :],
            )
            if m == 0:
                own[:, here] = sources[i][j]
                for k, row in enumerate((mean, scale, slope, offset)):
                    coef[k : k + 1, here] = row

            def activate(ds, carry):
                act = sources[i][j, ds, :].astype(F32) * slope + offset
                hidden[m, ds, here] = (mask[b, ds, :] * act * sigmoid(act)).astype(BF)
                return carry

            by_rows(rows, activate, 0)
        pre[m] = dot(hidden[m], weight[...])

        def collect(ds, acc):
            values = pre[m, ds, :]
            kept = mask[b, ds, :] * values
            return acc[0] + fold(kept), acc[1] + fold(kept * values)

        sums = by_rows(rows, collect, zeros_acc(pre.shape[2]))
        message[2 * m : 2 * m + 1, :] = column_sum(sums[0])
        message[2 * m + 1 : 2 * m + 2, :] = column_sum(sums[1])


def block_output(pre, x, cotangent, parts, params, gain, shift, mask, out, grad, coef, message):
    n = position()[0]
    rows, channels = pre.shape[1:]
    block = parts[...]
    for m in range(NARROW):
        b = n ^ m
        mean, scale, slope, offset = coefficients(
            block[2 * m : 2 * m + 1], block[2 * m + 1 : 2 * m + 2], inverse_count(params, b, channels), gain[...], shift[...]
        )
        for k, row in enumerate((mean, scale, slope, offset)):
            coef[m, k : k + 1, :] = row
        back = mean * scale

        def body(ds, acc):
            values = pre[m, ds, :]
            inside = mask[b, ds, :]
            summed = values * slope + offset + x[b, ds, :].astype(F32)
            gate = sigmoid(summed)
            value = summed * gate
            out[b, ds, :] = (inside * value).astype(BF)
            local = inside * cotangent[b, ds, :].astype(F32) * (gate + value * (1.0 - gate))
            grad[m, ds, :] = local
            return acc[0] + fold(local), acc[1] + fold(local * (values * scale - back))

        sums = by_rows(rows, body, zeros_acc(channels))
        message[2 * m : 2 * m + 1, :] = column_sum(sums[0])
        message[2 * m + 1 : 2 * m + 2, :] = column_sum(sums[1])


def last_backward(pre, grad, parts, params, coef, mask, weight,
                  grad_pre, send_far, own_far, send_near, own_near, level_sum, tilt_sum):
    n = position()[0]
    rows = pre.shape[1]
    block = parts[...]
    for s, ref in enumerate((level_sum, tilt_sum)):
        acc = block[s : s + 1]
        for m in range(1, NARROW):
            acc = acc + block[2 * m + s : 2 * m + s + 1]
        ref[...] = acc
    for m, ref in ((3, send_far), (2, own_far), (1, send_near), (0, own_near)):
        b = n ^ m
        mean, scale, slope = (coef[m, k : k + 1, :] for k in range(3))
        inverse = inverse_count(params, b, block.shape[1])
        level = block[2 * m : 2 * m + 1] * inverse
        tilt = block[2 * m + 1 : 2 * m + 2] * inverse
        level, tilt = level - mean * scale * tilt, scale * tilt

        def body(ds, carry):
            away = mask[b, ds, :] * (level + pre[m, ds, :] * tilt)
            grad_pre[m, ds, :] = (slope * (grad[m, ds, :] - away)).astype(BF)
            return carry

        by_rows(rows, body, 0)
        ref[...] = dot_nt(grad_pre[m], weight[...]).astype(ref.dtype)


def middle_join(own, near, far, pre, coef, mask, grad, own_q, near_q, far_q, last_q, message):
    b = position()[0]
    mean, scale, slope, offset = (coef[k : k + 1, :] for k in range(4))
    back = mean * scale

    def body(ds, acc):
        values = pre[ds, :].astype(F32)
        act = values * slope + offset
        gate = sigmoid(act)
        total = own[ds, :] + near[ds, :].astype(F32) + far[ds, :].astype(F32)
        local = total * mask[b, ds, :] * (gate * (1.0 + act * (1.0 - gate)))
        grad[ds, :] = local
        return acc[0] + fold(local), acc[1] + fold(local * (values * scale - back))

    sums = by_rows(own.shape[0], body, zeros_acc(own.shape[1]))
    send_stats(message, column_sum(sums[0]), column_sum(sums[1]))
    own_q[...] = grad[:, lane_block(b)].astype(BF)
    near_q[...] = grad[:, lane_block(b ^ 1)].astype(BF)
    far_q[...] = grad[:, lane_block(b ^ 2)].astype(BF)
    last_q[...] = grad[:, lane_block(b ^ 3)].astype(BF)


def middle_backward(grad, pre, parts, params, coef, mask, first_pre, first_coef, to_canvas, to_rows,
                    w0, w1, w2, w3, grad_first, message,
                    grad_pre, weight, gathered, canvas):
    n = position()[0]
    rows, places = grad.shape[0], to_canvas.shape[0]
    img = places // (SIDE * PITCH)
    margin = img * (PITCH + 1)
    block = parts[...]
    mean, scale, slope = (coef[k : k + 1, :] for k in range(3))
    inverse = inverse_count(params, n, grad.shape[1])
    level = wide_row(block, 0) * inverse
    tilt = wide_row(block, NARROW) * inverse
    level, tilt = level - mean * scale * tilt, scale * tilt

    def body(ds, carry):
        away = mask[n, ds, :] * (level + pre[ds, :].astype(F32) * tilt)
        grad_pre[ds, :] = (slope * (grad[ds, :] - away)).astype(BF)
        return carry

    by_rows(rows, body, 0)
    for j, piece in enumerate((w0, w1, w2, w3)):
        for tap in range(TAPS):
            weight[tap, :, lane_block(n ^ j)] = piece[:, 128 * tap : 128 * tap + 128]
    canvas[...] = dot(to_canvas[...], grad_pre[...]).astype(BF).astype(F32)
    gathered[...] = jnp.zeros_like(gathered)
    for tap in range(TAPS):
        start = margin + ((tap // 3 - 1) * PITCH + tap % 3 - 1) * img
        gathered[start : start + places, :] += dot_nt(canvas[...].astype(BF), weight[tap])
    canvas[...] = gathered[margin : margin + places, :]
    grad_pre[...] = dot(to_rows[...], canvas[...].astype(BF)).astype(BF)
    mean, scale, slope, offset = (first_coef[0, k : k + 1, :] for k in range(4))
    back = mean * scale

    def finish(ds, acc):
        values = first_pre[ds, :].astype(F32)
        act = values * slope + offset
        gate = sigmoid(act)
        local = grad_pre[ds, :].astype(F32) * mask[n, ds, :] * (gate * (1.0 + act * (1.0 - gate)))
        grad_first[ds, :] = local.astype(BF)
        return acc[0] + fold(local), acc[1] + fold(local * (values * scale - back))

    sums2 = by_rows(rows, finish, zeros_acc(grad.shape[1]))
    send_stats(message, column_sum(sums2[0]), column_sum(sums2[1]))


def first_backward(g0, g1, g2, g3, p0, p1, p2, p3, sum0, sum1, sum2, sum3, params, coef, mask, x, grad, weight,
                   grad_input, level_sum, tilt_sum, out, grad_pre, acc):
    n, z, y = position()
    rows, channels = g0.shape
    blocks = (sum0[...], sum1[...], sum2[...], sum3[...])
    every = blocks[0] + blocks[1] + blocks[2] + blocks[3]
    for m, (g, pre) in enumerate(((g0, p0), (g1, p1), (g2, p2), (g3, p3))):
        b = n ^ m
        block = blocks[m]
        mean, scale, slope = (coef[m, k : k + 1, :] for k in range(3))
        inverse = inverse_count(params, b, channels)
        level = wide_row(block, 0) * inverse
        tilt = wide_row(block, NARROW) * inverse
        level, tilt = level - mean * scale * tilt, scale * tilt

        def body(ds, carry):
            away = mask[b, ds, :] * (level + pre[ds, :].astype(F32) * tilt)
            grad_pre[m, ds, :] = (slope * (g[ds, :].astype(F32) - away)).astype(BF)
            return carry

        by_rows(rows, body, 0)
        product = dot_tn(x[b], grad_pre[m])
        if m == 0:
            acc[...] = product
        else:
            acc[...] += product
    if len(out.shape) == 2:
        out[...] = acc[...]
    else:
        half, cols = out.shape[1:]
        for place in range(out.shape[0]):
            top = pl.multiple_of((y ^ (place // NARROW)) * half, half)
            out[place] = acc[pl.ds(top, half), lane_block((z - place % NARROW) & 3)].astype(BF)
    for m in range(NARROW):
        grad_input[n ^ m] = dot_nt(grad_pre[m], weight[...]) + grad[m]
    level_sum[...] = row_of(every, 0, n)
    tilt_sum[...] = row_of(every, NARROW, n)


def last_weight(hidden, grad_pre, *refs):
    acc = refs[-1]
    for m in range(NARROW):
        product = dot_tn(hidden[m], grad_pre[m])
        if m == 0:
            acc[...] = product
        else:
            acc[...] += product
    hand_out(acc, refs[:-1])


def hand_out(acc, outs):
    if len(outs) == 1:
        outs[0][...] = acc[...]
        return
    _, z, y = position()
    own, away = outs
    rows = acc.shape[0] // 8
    for j in range(4):
        place = pl.ds(j * rows, rows)
        for ref, dy in ((own, 0), (away, 1)):
            top = ((z ^ j) * 2 + (y ^ dy)) * rows
            ref[place, :] = acc[pl.ds(pl.multiple_of(top, rows), rows), :].astype(ref.dtype)


def middle_weight(hidden, q0, q1, q2, q3, pre, sum0, sum1, sum2, sum3, norm, params, mask, to_canvas,
                  level_sum, tilt_sum, *refs):
    outs, (acc, shifted, canvas) = refs[:-3], refs[-3:]
    n = position()[0]
    places = to_canvas.shape[0]
    img = places // (SIDE * PITCH)
    margin = img * (PITCH + 1)
    canvas[0:margin, :] = jnp.zeros((margin, 128), F32)
    canvas[margin + places :, :] = jnp.zeros((margin, 128), F32)
    norms = norm[...]
    blocks = (sum0[...], sum1[...], sum2[...], sum3[...])
    every = blocks[0] + blocks[1] + blocks[2] + blocks[3]
    level_sum[...] = row_of(every, 0, n)
    tilt_sum[...] = row_of(every, NARROW, n)
    for m, piece in enumerate((q0, q1, q2, q3)):
        b = n ^ m
        inverse = inverse_count(params, b, 128)
        mean, scale, slope, _ = coefficients(
            norms[2 * m : 2 * m + 1], norms[2 * m + 1 : 2 * m + 2], inverse, params[n, 2:3, :], params[n, 3:4, :]
        )
        block = blocks[m]
        level = row_of(block, 0, n) * inverse
        tilt = row_of(block, NARROW, n) * inverse
        level, tilt = level - mean * scale * tilt, scale * tilt
        away = mask[b] * (level + pre[m].astype(F32) * tilt)
        grad_pre = (slope * (piece[...].astype(F32) - away)).astype(BF)
        canvas[margin : margin + places, :] = dot(to_canvas[...], grad_pre)
        for tap in range(TAPS):
            start = margin - ((tap // 3 - 1) * PITCH + tap % 3 - 1) * img
            shifted[:, 128 * tap : 128 * tap + 128] = canvas[start : start + places, :].astype(BF)
        product = dot_tn(hidden[m], shifted[...])
        if m == 0:
            acc[...] = product
        else:
            acc[...] += product
    hand_out(acc, outs)


def gather_middle(near, far, out):
    _, z, y = position()
    rows = out.shape[0] // 8
    for dy, stack in enumerate((near, far)):
        for j in range(4):
            here = pl.ds(pl.multiple_of(((z ^ j) * 2 + (y ^ dy)) * rows, rows), rows)
            for tap in range(TAPS):
                top = (j * TAPS + tap) * rows
                out[here, 128 * tap : 128 * tap + 128] = stack[top : top + rows, :]


def gather_last(*refs):
    pieces, out = refs[:-1], refs[-1]
    _, z, y = position()
    rows = out.shape[0] // 8
    for j, pair in enumerate(pieces):
        for dy in range(2):
            here = pl.ds(pl.multiple_of(((z ^ j) * 2 + (y ^ dy)) * rows, rows), rows)
            out[here, :] = pair[dy * rows : (dy + 1) * rows, :]


def add_tiles(*refs):
    total = refs[0][...]
    for ref in refs[1:-1]:
        total = total + ref[...]
    refs[-1][...] = total


def merge_wide(own, away, own_last, away_last, keep, keep_last, *sends):
    rows, middle = keep.shape
    keep[...] = own[0:rows, :] + away[0:rows, :].astype(F32)
    keep_last[...] = own_last[0:rows, :] + away_last[0:rows, :].astype(F32)
    for j, send in enumerate(sends):
        here = slice((j + 1) * rows, (j + 2) * rows)
        send[:, 0:middle] = (own[here, :] + away[here, :].astype(F32)).astype(BF)
        send[:, middle:] = (own_last[here, :] + away_last[here, :].astype(F32)).astype(BF)


def finish_wide(keep, keep_last, p1, p2, p3, out, out_last):
    middle = keep.shape[1]
    for tap in range(TAPS):
        here = slice(128 * tap, 128 * tap + 128)
        out[tap] = keep[:, here] + p1[:, here].astype(F32) + p2[:, here].astype(F32) + p3[:, here].astype(F32)
    out_last[...] = (
        keep_last[...] + p1[:, middle:].astype(F32) + p2[:, middle:].astype(F32) + p3[:, middle:].astype(F32)
    )


def swap_core(values):
    return lax.ppermute(values, "narrow", [(i, i ^ 1) for i in range(NARROW)])


def swap_chip(values):
    return lax.ppermute(values, "narrow", [(i, i ^ 2) for i in range(NARROW)])


def swap_wide(values, step, wide):
    return lax.ppermute(values, "wide", [(i, i ^ step) for i in range(wide)])


def after(value, *others):
    return lax.optimization_barrier((value, *others))[0]


def from_all(values, *others):
    far = swap_chip(values)
    if others:
        return values, swap_core(after(values, *others)), far, swap_core(after(far, *others))
    return values, swap_core(values), far, swap_core(far)


def add(*tiles):
    return run(add_tiles, tiles, [arr(tiles[0].shape, F32)])[0]


def sum_wide(values, wide, *beside):
    if wide == 8:
        values = add(after(values, *beside) if beside else values, swap_wide(values, 1, wide))
        if beside:
            return values, add(values, *(swap_wide(values, step, wide) for step in (2, 4, 6)))
        return add(values, *(swap_wide(values, step, wide) for step in (2, 4, 6)))
    step = 1
    while step < wide:
        values = add(values, swap_wide(values, step, wide))
        step *= 2
    return (values, values) if beside else values


def reduce_narrow(send_far, own_far, send_near, own_near, *others):
    got_far = swap_core(send_far)
    got_near = swap_core(send_near)
    joined = (own_far + got_far.astype(F32)).astype(BF)
    if others:
        joined = after(joined, *others)
    return (own_near, got_near, swap_chip(joined)), joined


def transposed_steps():
    steps = []
    for dy in range(2):
        for j in range(NARROW):
            pairs = []
            for k in range(NARROW):
                for z in range(4):
                    for y in range(2):
                        pairs.append((k * 8 + 2 * z + y, z * 8 + 2 * ((k + j) % 4) + (y ^ dy)))
            steps.append(pairs)
    return steps


def on_device(inputs, sides, w_first, w_middle, w_last, gain_first, shift_first, gain_middle, shift_middle,
              gain_last, shift_last, cotangent, *, wide):
    micro, rows, low = inputs.shape
    img = sides.shape[1]
    mid = w_last.shape[0] * wide
    cols = w_first.shape[1]
    places = img * SIDE * PITCH
    direct = wide == 8
    n = lax.axis_index("narrow")
    w = lax.axis_index("wide")

    spots = jnp.arange(rows, dtype=jnp.int32)
    spot_y, spot_x, spot_img = spots % 49 // 7, spots % 7, spots // 49
    limit = jnp.repeat(sides, 49, axis=1)
    mask = ((spot_y[None] < limit) & (spot_x[None] < limit)).astype(F32)[:, :, None]
    place = (spot_y * PITCH + spot_x) * img + spot_img
    to_canvas = (jnp.arange(places, dtype=jnp.int32)[:, None] == place[None, :]).astype(BF)
    to_rows = (place[:, None] == jnp.arange(places, dtype=jnp.int32)[None, :]).astype(BF)

    if direct:
        steps = transposed_steps()
        share = w_last.shape[0]
        first_pieces = [lax.ppermute(w_first, MESH, pairs) for pairs in steps]
    else:
        first_all = lax.all_gather(lax.all_gather(w_first, "narrow", axis=1, tiled=True), "wide", axis=0, tiled=True)
        first_pieces = [lax.dynamic_slice_in_dim(first_all, n * low, low, 0)]
        middle_slice = lax.all_gather(w_middle, "wide", axis=2, tiled=True)
        middle_slice = middle_slice.reshape(TAPS, mid, 128).transpose(1, 0, 2).reshape(mid, TAPS * 128)
        last_slice = lax.all_gather(w_last, "wide", axis=0, tiled=True)

    counts = jnp.sum((sides * sides).astype(F32), axis=1)
    small = jnp.concatenate(
        [jnp.stack([gain_first, shift_first, gain_middle, shift_middle]) * (1.0 / wide),
         jnp.broadcast_to(counts[:, None], (micro, 128))], axis=0
    )

    tile = arr((8, 128), F32)
    across = arr((8, low), F32)
    flat = arr((rows, mid), BF)
    flat32 = arr((rows, mid), F32)

    w_rows, send_far, own_far, send_near, own_near = run(
        first_product, (inputs, *first_pieces),
        [arr((low, mid), BF), flat, flat32, flat, flat32], flops=2 * micro * rows * low * mid,
    )
    joined, begun = reduce_narrow(send_far, own_far, send_near, own_near)
    if direct:
        flat_middle = after(w_middle.reshape(TAPS * share, 128), begun)
        middle_near = jnp.concatenate([flat_middle] + [swap_wide(flat_middle, 2 * j, wide) for j in range(1, 4)], axis=0)
        middle_far = swap_wide(middle_near, 1, wide)
        held = after(w_last, begun)
        last_pair = jnp.concatenate([held, swap_wide(held, 1, wide)], axis=0)
        last_pieces = [last_pair] + [swap_wide(last_pair, 2 * j, wide) for j in range(1, 4)]
        joined = (after(joined[0], middle_near, last_pair), *joined[1:])
    pre_one, message = run(first_join, (*joined, mask, small), [flat, arr((16, 128), F32)])
    total = sum_wide(message, wide)
    pre_ones = from_all(pre_one, total, *((middle_far,) if direct else ()))
    sums_one = from_all(total)
    if direct:
        middle_slice = run(gather_middle, (middle_near, middle_far), [arr((mid, TAPS * 128), BF)])[0]
        last_slice = run(gather_last, last_pieces, [arr((mid, low), BF)])[0]
        middle_slice = after(middle_slice, *last_pieces)

    hidden_one, pre_two, coef_one, message, params = run(
        middle_forward, (*pre_ones, *sums_one, mask, to_canvas, to_rows, middle_slice),
        [arr((micro, places, mid), BF), arr((micro, rows, 128), BF), arr((micro, 8, mid), F32), tile, arr((NARROW, 8, 128), F32)],
        [pltpu.VMEM((rows, mid), BF), pltpu.VMEM((places + 2 * img * (PITCH + 1), TAPS * 128), F32), pltpu.VMEM((places, 128), BF)],
        flops=2 * micro * places * mid * TAPS * 128,
    )
    total = sum_wide(message, wide)
    pre_twos = from_all(pre_two, total)
    sums_two = from_all(total)
    held = after(middle_slice, pre_twos[3], sums_two[3])
    middle_away = swap_chip(held)

    hidden_two, own_two, coef_two, pre_three, message = run(
        last_forward, (*pre_twos, *sums_two, params, mask, last_slice),
        [arr((micro, rows, mid), BF), flat, arr((8, mid), F32), arr((micro, rows, low), F32), across],
        flops=2 * micro * rows * low * mid,
    )
    parts_three = sum_wide(message, wide)
    block_out, grad_sum, coef_three, message = run(
        block_output,
        (pre_three, inputs, cotangent, parts_three, params, gain_last[None], shift_last[None], mask),
        [arr(inputs.shape, BF), arr((micro, rows, low), F32), arr((micro, 8, low), F32), across],
    )
    parts_four = sum_wide(message, wide)

    grad_three, send_far, own_far, send_near, own_near, level_three, tilt_three = run(
        last_backward, (pre_three, grad_sum, parts_four, params, coef_three, mask, last_slice),
        [arr((micro, rows, low), BF), flat, flat32, flat, flat32, arr((1, low), F32), arr((1, low), F32)],
        flops=2 * micro * rows * low * mid,
    )
    joined, _ = reduce_narrow(send_far, own_far, send_near, own_near, middle_away)

    def handed(channels):
        if direct:
            return [arr((mid // 2, channels), F32), arr((mid // 2, channels), BF)]
        return [arr((mid, channels), F32)]

    last_sum = run(
        last_weight, (hidden_two, grad_three), handed(low), [pltpu.VMEM((mid, low), F32)],
        flops=2 * micro * rows * low * mid,
    )
    slim = arr((rows, 128), BF)
    row = arr((1, 128), F32)
    if direct:
        got_last_sum = swap_wide(last_sum[1], 1, wide)
        joined = (after(joined[0], got_last_sum), *joined[1:])
    grad_two, own_q, near_q, far_q, last_q, message = run(
        middle_join, (*joined, own_two, coef_two, mask), [flat32, slim, slim, slim, slim, tile]
    )
    total_five = sum_wide(message, wide)
    got_far, got_last, got_near = swap_chip(far_q), swap_core(swap_chip(last_q)), swap_core(near_q)
    middle_slices = (middle_slice, swap_core(held), middle_away, swap_core(middle_away))
    sums_five = from_all(total_five)

    grad_one, message = run(
        middle_backward,
        (grad_two, own_two, total_five, params, coef_two, mask, pre_one, coef_one, to_canvas, to_rows, *middle_slices),
        [flat, tile],
        [pltpu.VMEM((rows, mid), BF), pltpu.VMEM((TAPS, mid, mid), BF),
         pltpu.VMEM((places + 2 * img * (PITCH + 1), mid), F32), pltpu.VMEM((places, mid), F32)],
        flops=2 * places * mid * TAPS * mid,
    )
    level_two, tilt_two, *middle_sum = run(
        middle_weight,
        (hidden_one, own_q, got_near, got_far, got_last, pre_two, *sums_five, sums_two[0], params, mask, to_canvas),
        [row, row, *handed(TAPS * 128)],
        [pltpu.VMEM((mid, TAPS * 128), F32), pltpu.VMEM((places, TAPS * 128), BF),
         pltpu.VMEM((places + 2 * img * (PITCH + 1), 128), F32)],
        flops=2 * micro * places * mid * TAPS * 128,
    )
    begun, total = sum_wide(message, wide, *middle_sum)
    grad_ones = from_all(after(grad_one, sums_five[2]), total)
    sums_six = from_all(total)
    if direct:
        got_middle = swap_wide(after(middle_sum[1], begun), 1, wide)

    out_first = arr((8, 2 * low // NARROW, cols), BF) if direct else arr((low, mid), F32)
    input_grad, level_one, tilt_one, first_sum = run(
        first_backward,
        (*grad_ones, *pre_ones, *sums_six, params, coef_one, mask, inputs, grad_sum, w_rows),
        [arr((micro, rows, low), F32), row, row, out_first],
        [pltpu.VMEM((micro, rows, mid), BF), pltpu.VMEM((low, mid), F32)],
        flops=4 * micro * rows * low * mid,
    )

    if direct:
        arrived = [
            lax.ppermute(first_sum[k], MESH, [(dst, src) for src, dst in pairs]) for k, pairs in enumerate(steps)
        ]
        channels = TAPS * 128
        keep, keep_last, *sends = run(
            merge_wide, (middle_sum[0], after(got_middle, first_sum), last_sum[0], got_last_sum),
            [arr((share, channels), F32), arr((share, low), F32)] + [arr((share, channels + low), BF)] * 3,
        )
        parts = [swap_wide(send, 2 * j + 2, wide) for j, send in enumerate(sends)]
        grad_middle, grad_last = run(
            finish_wide, (after(keep, arrived[0]), keep_last, *parts),
            [arr((TAPS, share, 128), F32), arr((share, low), F32)],
        )
        grad_middle = grad_middle.reshape(3, 3, share, 128)
        grad_first = arrived[0].astype(F32)
        for piece in arrived[1:]:
            grad_first = grad_first + piece.astype(F32)
    else:
        grad_last = lax.psum_scatter(last_sum[0], "wide", scatter_dimension=0, tiled=True)
        grad_middle = lax.psum_scatter(middle_sum[0], "wide", scatter_dimension=0, tiled=True)
        share = grad_middle.shape[0]
        grad_middle = grad_middle.reshape(share, TAPS, 128).transpose(1, 0, 2).reshape(3, 3, share, 128)
        whole = lax.psum(first_sum, "wide")
        whole = lax.all_gather(whole, "narrow", axis=0, tiled=True)
        share = whole.shape[0] // wide
        grad_first = lax.dynamic_slice(whole, (w * share, n * cols), (share, cols))
    return (
        block_out, input_grad, grad_first, grad_middle, grad_last,
        tilt_one[0], level_one[0], tilt_two[0], level_two[0], tilt_three[0], level_three[0],
    )


def solution(mesh):
    wide = mesh.shape["wide"]
    placed = (
        P(None, "wide", "narrow"),
        P(None, "wide"),
        P("wide", "narrow"),
        P(None, None, "wide", "narrow"),
        P("wide", "narrow"),
        P("narrow"),
        P("narrow"),
        P("narrow"),
        P("narrow"),
        P("narrow"),
        P("narrow"),
        P(None, "wide", "narrow"),
    )
    return jax.shard_map(
        lambda *arrays: on_device(*arrays, wide=wide),
        mesh=mesh,
        in_specs=placed,
        out_specs=(
            P(None, "wide", "narrow"),
            P(None, "wide", "narrow"),
            P("wide", "narrow"),
            P(None, None, "wide", "narrow"),
            P("wide", "narrow"),
            P("narrow"),
            P("narrow"),
            P("narrow"),
            P("narrow"),
            P("narrow"),
            P("narrow"),
        ),
        check_vma=False,
    )
```

```python
import jax
import jax.numpy as jnp
from jax import lax
from jax.experimental import pallas as pl
from jax.experimental.pallas import tpu as pltpu
from jax.sharding import PartitionSpec as P


F32 = jnp.float32
BF = jnp.bfloat16
EPS = 1e-05
SIDE = 7
PITCH = 8
TAPS = 9
NARROW = 4
MESH = ("narrow", "wide")
VMEM_BYTES = 20 * 2**20


def dot(left, right):
    return jnp.dot(left, right, preferred_element_type=F32)


def dot_nt(left, right):
    return lax.dot_general(left, right, (((1,), (1,)), ((), ())), preferred_element_type=F32)


def dot_tn(left, right):
    return lax.dot_general(left, right, (((0,), (0,)), ((), ())), preferred_element_type=F32)


def position():
    n, w = lax.axis_index("narrow"), lax.axis_index("wide")
    return n, w // 2, w % 2


def run(kernel, operands, outs, scratch=(), flops=0):
    moved = sum(o.size * o.dtype.itemsize for o in (*operands, *outs))
    return pl.pallas_call(
        kernel,
        out_shape=outs,
        name=kernel.__name__,
        in_specs=[pl.BlockSpec(memory_space=pltpu.VMEM)] * len(operands),
        out_specs=[pl.BlockSpec(memory_space=pltpu.VMEM)] * len(outs),
        scratch_shapes=list(scratch),
        cost_estimate=pl.CostEstimate(flops=flops, bytes_accessed=moved, transcendentals=0),
        compiler_params=pltpu.CompilerParams(vmem_limit_bytes=VMEM_BYTES),
    )(*operands)


def arr(shape, dtype):
    return jax.ShapeDtypeStruct(shape, dtype)


def by_rows(rows, body, carry):
    return body(pl.ds(0, rows), carry)


def fold(values):
    total = values[0:8]
    for start in range(8, values.shape[0], 8):
        total = total + values[start : start + 8]
    return total


def zeros_acc(channels):
    return (jnp.zeros((8, channels), F32), jnp.zeros((8, channels), F32))


def column_sum(acc):
    return jnp.sum(acc, axis=0, keepdims=True)


def sigmoid(values):
    return 0.5 * jnp.tanh(0.5 * values) + 0.5


def coefficients(total, squares, inverse, gain, shift):
    mean = total * inverse
    spread = squares * inverse - mean * mean
    scale = lax.rsqrt(spread + EPS)
    slope = gain * scale
    return mean, scale, slope, shift - mean * slope


def wide_row(block, first, count=NARROW):
    return jnp.concatenate([block[first + k : first + k + 1] for k in range(count)], axis=1)


def row_of(block, first, index):
    rows = [jnp.where(index == k, block[first + k : first + k + 1], 0.0) for k in range(NARROW)]
    return rows[0] + rows[1] + rows[2] + rows[3]


def inverse_count(params, b, channels):
    row = params[b, 4:5, :]
    return row if channels == 128 else jnp.concatenate([row] * (channels // 128), axis=1)


def lane_block(index):
    return pl.ds(pl.multiple_of(index * 128, 128), 128)


def send_stats(message, first, second):
    for k in range(NARROW):
        message[k : k + 1, :] = first[:, 128 * k : 128 * k + 128]
        message[NARROW + k : NARROW + k + 1, :] = second[:, 128 * k : 128 * k + 128]


def repeat_first(message):
    block = message[0]
    for place in range(1, message.shape[0]):
        message[place] = block


def sum_parts(parts):
    total = parts[0]
    for place in range(1, parts.shape[0]):
        total = total + parts[place]
    return total


def first_product(x, *refs):
    pieces, (w_first, send_far, own_far, send_near, own_near) = refs[:-5], refs[-5:]
    n, z, y = position()
    if len(pieces) == 1:
        w_first[...] = pieces[0][...]
    else:
        rows = pieces[0].shape[0] // 2
        for j, piece in enumerate(pieces):
            for dy in range(2):
                here = pl.ds(pl.multiple_of((y ^ dy) * rows, rows), rows)
                w_first[here, lane_block((z - j) & 3)] = piece[dy * rows : (dy + 1) * rows, :]
    for ref, m in ((send_far, 3), (own_far, 2), (send_near, 1), (own_near, 0)):
        ref[...] = dot(x[n ^ m], w_first[...]).astype(ref.dtype)


def first_join(own, near, far, mask, small, pre, message):
    b = position()[0]

    def body(ds, acc):
        values = own[ds, :] + near[ds, :].astype(F32) + far[ds, :].astype(F32)
        pre[ds, :] = values.astype(BF)
        kept = mask[b, ds, :] * values
        return acc[0] + fold(kept), acc[1] + fold(kept * values)

    sums = by_rows(own.shape[0], body, zeros_acc(own.shape[1]))
    send_stats(message, column_sum(sums[0]), column_sum(sums[1]))
    message[8:16, :] = small[...]


def middle_forward(pre0, pre1, pre2, pre3, sum0, sum1, sum2, sum3, mask, to_canvas, to_rows, weight,
                   hidden, pre, coef, message, params, active, spread, joined):
    n = position()[0]
    blocks = (sum0[...], sum1[...], sum2[...], sum3[...])
    for m, block in enumerate(blocks):
        params[n ^ m, 0:4, :] = block[8:12]
    for b in range(NARROW):
        params[b, 4:5, :] = 1.0 / blocks[0][12 + b : 13 + b]
        params[b, 5:8, :] = jnp.zeros((3, 128), F32)
    rows, places = pre0.shape[0], to_canvas.shape[0]
    img = places // (SIDE * PITCH)
    margin = img * (PITCH + 1)
    gain = jnp.concatenate([params[k, 0:1, :] for k in range(NARROW)], axis=1)
    shift = jnp.concatenate([params[k, 1:2, :] for k in range(NARROW)], axis=1)
    spread[0:margin, :] = jnp.zeros((margin, spread.shape[1]), F32)
    spread[margin + places :, :] = jnp.zeros((margin, spread.shape[1]), F32)
    line = img * PITCH
    for m, source in enumerate((pre0, pre1, pre2, pre3)):
        b = n ^ m
        block = blocks[m]
        mean, scale, slope, offset = coefficients(
            wide_row(block, 0), wide_row(block, NARROW), inverse_count(params, b, gain.shape[1]), gain, shift
        )
        for k, row in enumerate((mean, scale, slope, offset)):
            coef[m, k : k + 1, :] = row

        def activate(ds, carry):
            act = source[ds, :].astype(F32) * slope + offset
            active[ds, :] = (mask[b, ds, :] * act * sigmoid(act)).astype(BF)
            return carry

        by_rows(rows, activate, 0)
        hidden[m] = dot(to_canvas[...], active[...]).astype(BF)
        spread[margin : margin + places, :] = dot(hidden[m], weight[...])
        for top in range(SIDE):
            acc = None
            for tap in range(TAPS):
                start = margin + top * line + ((tap // 3 - 1) * PITCH + tap % 3 - 1) * img
                part = spread[start : start + line, 128 * tap : 128 * tap + 128]
                acc = part if acc is None else acc + part
            joined[top * line : (top + 1) * line, :] = acc.astype(BF)
        pre[m] = dot(to_rows[...], joined[...]).astype(BF)

        def collect(ds, acc):
            values = pre[m, ds, :].astype(F32)
            kept = mask[b, ds, :] * values
            return acc[0] + fold(kept), acc[1] + fold(kept * values)

        sums = by_rows(rows, collect, zeros_acc(128))
        message[2 * m : 2 * m + 1, :] = column_sum(sums[0])
        message[2 * m + 1 : 2 * m + 2, :] = column_sum(sums[1])


def last_forward(src0, src1, src2, src3, sum0, sum1, sum2, sum3, params, mask, weight,
                 hidden, own, coef, pre, message):
    n = position()[0]
    rows = own.shape[0]
    sources = (src0, src1, src2, src3)
    blocks = (sum0[...], sum1[...], sum2[...], sum3[...])
    for m in range(NARROW):
        b = n ^ m
        for i in range(NARROW):
            j = m ^ i
            here = lane_block(n ^ i)
            mean, scale, slope, offset = coefficients(
                blocks[i][2 * j : 2 * j + 1], blocks[i][2 * j + 1 : 2 * j + 2], inverse_count(params, b, 128),
                params[n ^ i, 2:3, :], params[n ^ i, 3:4, :],
            )
            if m == 0:
                own[:, here] = sources[i][j]
                for k, row in enumerate((mean, scale, slope, offset)):
                    coef[k : k + 1, here] = row

            def activate(ds, carry):
                act = sources[i][j, ds, :].astype(F32) * slope + offset
                hidden[m, ds, here] = (mask[b, ds, :] * act * sigmoid(act)).astype(BF)
                return carry

            by_rows(rows, activate, 0)
        pre[m] = dot(hidden[m], weight[...])

        def collect(ds, acc):
            values = pre[m, ds, :]
            kept = mask[b, ds, :] * values
            return acc[0] + fold(kept), acc[1] + fold(kept * values)

        sums = by_rows(rows, collect, zeros_acc(pre.shape[2]))
        message[0, 2 * m : 2 * m + 1, :] = column_sum(sums[0])
        message[0, 2 * m + 1 : 2 * m + 2, :] = column_sum(sums[1])
    repeat_first(message)


def block_output(pre, x, cotangent, parts, params, gain, shift, mask, out, grad, coef, message):
    n = position()[0]
    rows, channels = pre.shape[1:]
    block = sum_parts(parts)
    for m in range(NARROW):
        b = n ^ m
        mean, scale, slope, offset = coefficients(
            block[2 * m : 2 * m + 1], block[2 * m + 1 : 2 * m + 2], inverse_count(params, b, channels), gain[...], shift[...]
        )
        for k, row in enumerate((mean, scale, slope, offset)):
            coef[m, k : k + 1, :] = row
        back = mean * scale

        def body(ds, acc):
            values = pre[m, ds, :]
            inside = mask[b, ds, :]
            summed = values * slope + offset + x[b, ds, :].astype(F32)
            gate = sigmoid(summed)
            value = summed * gate
            out[b, ds, :] = (inside * value).astype(BF)
            local = inside * cotangent[b, ds, :].astype(F32) * (gate + value * (1.0 - gate))
            grad[m, ds, :] = local
            return acc[0] + fold(local), acc[1] + fold(local * (values * scale - back))

        sums = by_rows(rows, body, zeros_acc(channels))
        message[0, 2 * m : 2 * m + 1, :] = column_sum(sums[0])
        message[0, 2 * m + 1 : 2 * m + 2, :] = column_sum(sums[1])
    repeat_first(message)


def last_backward(pre, grad, parts, params, coef, mask, weight,
                  grad_pre, send_far, own_far, send_near, own_near, level_sum, tilt_sum):
    n = position()[0]
    rows = pre.shape[1]
    block = sum_parts(parts)
    for s, ref in enumerate((level_sum, tilt_sum)):
        acc = block[s : s + 1]
        for m in range(1, NARROW):
            acc = acc + block[2 * m + s : 2 * m + s + 1]
        ref[...] = acc
    for m, ref in ((3, send_far), (2, own_far), (1, send_near), (0, own_near)):
        b = n ^ m
        mean, scale, slope = (coef[m, k : k + 1, :] for k in range(3))
        inverse = inverse_count(params, b, block.shape[1])
        level = block[2 * m : 2 * m + 1] * inverse
        tilt = block[2 * m + 1 : 2 * m + 2] * inverse
        level, tilt = level - mean * scale * tilt, scale * tilt

        def body(ds, carry):
            away = mask[b, ds, :] * (level + pre[m, ds, :] * tilt)
            grad_pre[m, ds, :] = (slope * (grad[m, ds, :] - away)).astype(BF)
            return carry

        by_rows(rows, body, 0)
        ref[...] = dot_nt(grad_pre[m], weight[...]).astype(ref.dtype)


def middle_join(own, near, far, pre, coef, mask, grad, own_q, near_q, far_q, message):
    b = position()[0]
    mean, scale, slope, offset = (coef[k : k + 1, :] for k in range(4))
    back = mean * scale

    def body(ds, acc):
        values = pre[ds, :].astype(F32)
        act = values * slope + offset
        gate = sigmoid(act)
        total = own[ds, :] + near[ds, :].astype(F32) + far[ds, :].astype(F32)
        local = total * mask[b, ds, :] * (gate * (1.0 + act * (1.0 - gate)))
        grad[ds, :] = local
        return acc[0] + fold(local), acc[1] + fold(local * (values * scale - back))

    sums = by_rows(own.shape[0], body, zeros_acc(own.shape[1]))
    send_stats(message, column_sum(sums[0]), column_sum(sums[1]))
    own_q[...] = grad[:, lane_block(b)].astype(BF)
    near_q[...] = grad[:, lane_block(b ^ 1)].astype(BF)
    far_q[0] = grad[:, lane_block(b ^ 2)].astype(BF)
    far_q[1] = grad[:, lane_block(b ^ 3)].astype(BF)


def middle_backward(grad, pre, parts, params, coef, mask, first_pre, first_coef, to_canvas, to_rows,
                    w0, w1, w2, w3, grad_first, message,
                    grad_pre, weight, gathered, canvas):
    n = position()[0]
    rows, places = grad.shape[0], to_canvas.shape[0]
    img = places // (SIDE * PITCH)
    margin = img * (PITCH + 1)
    block = parts[...]
    mean, scale, slope = (coef[k : k + 1, :] for k in range(3))
    inverse = inverse_count(params, n, grad.shape[1])
    level = wide_row(block, 0) * inverse
    tilt = wide_row(block, NARROW) * inverse
    level, tilt = level - mean * scale * tilt, scale * tilt

    def body(ds, carry):
        away = mask[n, ds, :] * (level + pre[ds, :].astype(F32) * tilt)
        grad_pre[ds, :] = (slope * (grad[ds, :] - away)).astype(BF)
        return carry

    by_rows(rows, body, 0)
    for j, piece in enumerate((w0, w1, w2, w3)):
        for tap in range(TAPS):
            weight[tap, :, lane_block(n ^ j)] = piece[:, 128 * tap : 128 * tap + 128]
    canvas[...] = dot(to_canvas[...], grad_pre[...]).astype(BF).astype(F32)
    gathered[...] = jnp.zeros_like(gathered)
    for tap in range(TAPS):
        start = margin + ((tap // 3 - 1) * PITCH + tap % 3 - 1) * img
        gathered[start : start + places, :] += dot_nt(canvas[...].astype(BF), weight[tap])
    canvas[...] = gathered[margin : margin + places, :]
    grad_pre[...] = dot(to_rows[...], canvas[...].astype(BF)).astype(BF)
    mean, scale, slope, offset = (first_coef[0, k : k + 1, :] for k in range(4))
    back = mean * scale

    def finish(ds, acc):
        values = first_pre[ds, :].astype(F32)
        act = values * slope + offset
        gate = sigmoid(act)
        local = grad_pre[ds, :].astype(F32) * mask[n, ds, :] * (gate * (1.0 + act * (1.0 - gate)))
        grad_first[ds, :] = local.astype(BF)
        return acc[0] + fold(local), acc[1] + fold(local * (values * scale - back))

    sums2 = by_rows(rows, finish, zeros_acc(grad.shape[1]))
    send_stats(message, column_sum(sums2[0]), column_sum(sums2[1]))


def first_weight(g0, g1, g2, g3, p0, p1, p2, p3, sum0, sum1, sum2, sum3, params, coef, mask, x,
                 level_sum, tilt_sum, grad_pre, *refs):
    outs, acc = refs[:-1], refs[-1]
    n, z, y = position()
    rows, channels = g0.shape
    blocks = (sum0[...], sum1[...], sum2[...], sum3[...])
    every = blocks[0] + blocks[1] + blocks[2] + blocks[3]
    for m, (g, pre) in enumerate(((g0, p0), (g1, p1), (g2, p2), (g3, p3))):
        b = n ^ m
        block = blocks[m]
        mean, scale, slope = (coef[m, k : k + 1, :] for k in range(3))
        inverse = inverse_count(params, b, channels)
        level = wide_row(block, 0) * inverse
        tilt = wide_row(block, NARROW) * inverse
        level, tilt = level - mean * scale * tilt, scale * tilt
        away = mask[b] * (level + pre[...].astype(F32) * tilt)
        grad_pre[m] = (slope * (g[...].astype(F32) - away)).astype(BF)
        product = dot_tn(x[b], grad_pre[m])
        if m == 0:
            acc[...] = product
        else:
            acc[...] += product
    if len(outs) == 1:
        outs[0][...] = acc[...]
    else:
        half = acc.shape[0] // 2
        for ref, h in zip(outs, (y, 1 - y)):
            top = pl.multiple_of(h * half, half)
            for j in range(NARROW):
                block = acc[pl.ds(top, half), lane_block((z - j) & 3)]
                ref[:, 128 * j : 128 * j + 128] = block.astype(ref.dtype)
    level_sum[...] = row_of(every, 0, n)
    tilt_sum[...] = row_of(every, NARROW, n)


def input_gradient(grad_pre, weight, grad, out):
    n = position()[0]
    for m in range(NARROW):
        out[n ^ m] = dot_nt(grad_pre[m], weight[...]) + grad[m]


def last_weight(hidden, grad_pre, *refs):
    acc = refs[-1]
    for m in range(NARROW):
        product = dot_tn(hidden[m], grad_pre[m])
        if m == 0:
            acc[...] = product
        else:
            acc[...] += product
    hand_out(acc, refs[:-1])


def hand_out(acc, outs):
    if len(outs) == 1:
        outs[0][...] = acc[...]
        return
    _, z, y = position()
    own, away = outs
    rows = acc.shape[0] // 8
    for j in range(4):
        place = pl.ds(j * rows, rows)
        for ref, dy in ((own, 0), (away, 1)):
            top = ((z ^ j) * 2 + (y ^ dy)) * rows
            ref[place, :] = acc[pl.ds(pl.multiple_of(top, rows), rows), :].astype(ref.dtype)


def middle_weight(hidden, q0, q1, far, last, pre, sum0, sum1, sum2, sum3, norm, params, mask, to_canvas,
                  level_sum, tilt_sum, *refs):
    outs, (acc, shifted, canvas) = refs[:-3], refs[-3:]
    n = position()[0]
    places = to_canvas.shape[0]
    img = places // (SIDE * PITCH)
    margin = img * (PITCH + 1)
    canvas[0:margin, :] = jnp.zeros((margin, 128), F32)
    canvas[margin + places :, :] = jnp.zeros((margin, 128), F32)
    norms = norm[...]
    blocks = (sum0[...], sum1[...], sum2[...], sum3[...])
    every = blocks[0] + blocks[1] + blocks[2] + blocks[3]
    level_sum[...] = row_of(every, 0, n)
    tilt_sum[...] = row_of(every, NARROW, n)
    for m, piece in enumerate((q0[...], q1[...], far[0], last[1])):
        b = n ^ m
        inverse = inverse_count(params, b, 128)
        mean, scale, slope, _ = coefficients(
            norms[2 * m : 2 * m + 1], norms[2 * m + 1 : 2 * m + 2], inverse, params[n, 2:3, :], params[n, 3:4, :]
        )
        block = blocks[m]
        level = row_of(block, 0, n) * inverse
        tilt = row_of(block, NARROW, n) * inverse
        level, tilt = level - mean * scale * tilt, scale * tilt
        away = mask[b] * (level + pre[m].astype(F32) * tilt)
        grad_pre = (slope * (piece.astype(F32) - away)).astype(BF)
        canvas[margin : margin + places, :] = dot(to_canvas[...], grad_pre)
        for tap in range(TAPS):
            start = margin - ((tap // 3 - 1) * PITCH + tap % 3 - 1) * img
            shifted[:, 128 * tap : 128 * tap + 128] = canvas[start : start + places, :].astype(BF)
        product = dot_tn(hidden[m], shifted[...])
        if m == 0:
            acc[...] = product
        else:
            acc[...] += product
    hand_out(acc, outs)


def gather_middle(near, far, out):
    _, z, y = position()
    rows = out.shape[0] // 8
    for dy, stack in enumerate((near, far)):
        for j in range(4):
            here = pl.ds(pl.multiple_of(((z ^ j) * 2 + (y ^ dy)) * rows, rows), rows)
            for tap in range(TAPS):
                top = (j * TAPS + tap) * rows
                out[here, 128 * tap : 128 * tap + 128] = stack[top : top + rows, :]


def gather_last(near, far, out):
    _, z, y = position()
    rows = out.shape[0] // 8
    for dy, stack in enumerate((near, far)):
        for j in range(4):
            here = pl.ds(pl.multiple_of(((z ^ j) * 2 + (y ^ dy)) * rows, rows), rows)
            out[here, :] = stack[j * rows : (j + 1) * rows, :]


def merge_first(own, away, *sends):
    for j, send in enumerate(sends):
        here = slice(128 * j, 128 * j + 128)
        send[...] = (own[:, here] + away[:, here].astype(F32)).astype(BF)


def add_tiles(*refs):
    total = refs[0][...]
    for ref in refs[1:-1]:
        total = total + ref[...]
    refs[-1][...] = total


def merge_wide(own, away, own_last, away_last, keep, keep_last, *sends):
    rows, middle = keep.shape
    keep[...] = own[0:rows, :] + away[0:rows, :].astype(F32)
    keep_last[...] = own_last[0:rows, :] + away_last[0:rows, :].astype(F32)
    for j, send in enumerate(sends):
        here = slice((j + 1) * rows, (j + 2) * rows)
        send[:, 0:middle] = (own[here, :] + away[here, :].astype(F32)).astype(BF)
        send[:, middle:] = (own_last[here, :] + away_last[here, :].astype(F32)).astype(BF)


def finish_wide(keep, keep_last, p1, p2, p3, out, out_last):
    middle = keep.shape[1]
    for tap in range(TAPS):
        here = slice(128 * tap, 128 * tap + 128)
        out[tap] = keep[:, here] + p1[:, here].astype(F32) + p2[:, here].astype(F32) + p3[:, here].astype(F32)
    out_last[...] = (
        keep_last[...] + p1[:, middle:].astype(F32) + p2[:, middle:].astype(F32) + p3[:, middle:].astype(F32)
    )


def swap_core(values):
    return lax.ppermute(values, "narrow", [(i, i ^ 1) for i in range(NARROW)])


def swap_chip(values):
    return lax.ppermute(values, "narrow", [(i, i ^ 2) for i in range(NARROW)])


def swap_wide(values, step, wide):
    return lax.ppermute(values, "wide", [(i, i ^ step) for i in range(wide)])


def after(value, *others):
    return lax.optimization_barrier((value, *others))[0]


def from_all(values, *others):
    far = swap_chip(values)
    if others:
        return values, swap_core(after(values, *others)), far, swap_core(after(far, *others))
    return values, swap_core(values), far, swap_core(far)


def add(*tiles):
    return run(add_tiles, tiles, [arr(tiles[0].shape, F32)])[0]


def sum_wide(values, wide, beside=(), late=()):
    if wide == 8:
        values = add(after(values, *beside) if beside else values, swap_wide(values, 1, wide))
        parts = [swap_wide(values, step, wide) for step in (2, 4, 6)]
        total = add(after(values, *late) if late else values, *parts)
        return values, total
    step = 1
    while step < wide:
        values = add(values, swap_wide(values, step, wide))
        step *= 2
    return values, values


def reduce_narrow(send_far, own_far, send_near, own_near, *others):
    got_far = swap_core(send_far)
    got_near = swap_core(send_near)
    joined = (own_far + got_far.astype(F32)).astype(BF)
    if others:
        joined = after(joined, *others)
    return (own_near, got_near, swap_chip(joined)), joined


def transposed_steps():
    steps = []
    for j in range(NARROW):
        pairs = []
        for k in range(NARROW):
            for z in range(4):
                for y in range(2):
                    pairs.append((k * 8 + 2 * z + y, z * 8 + 2 * ((k + j) % 4) + y))
        steps.append(pairs)
    return steps


def on_device(inputs, sides, w_first, w_middle, w_last, gain_first, shift_first, gain_middle, shift_middle,
              gain_last, shift_last, cotangent, *, wide):
    micro, rows, low = inputs.shape
    img = sides.shape[1]
    mid = w_last.shape[0] * wide
    cols = w_first.shape[1]
    places = img * SIDE * PITCH
    direct = wide == 8
    n = lax.axis_index("narrow")
    w = lax.axis_index("wide")

    spots = jnp.arange(rows, dtype=jnp.int32)
    spot_y, spot_x, spot_img = spots % 49 // 7, spots % 7, spots // 49

    def mask_of(limits):
        limits = jnp.repeat(limits, 49, axis=1)
        return ((spot_y[None] < limits) & (spot_x[None] < limits)).astype(F32)[:, :, None]

    place = (spot_y * PITCH + spot_x) * img + spot_img
    to_canvas = (jnp.arange(places, dtype=jnp.int32)[:, None] == place[None, :]).astype(BF)
    to_rows = (place[:, None] == jnp.arange(places, dtype=jnp.int32)[None, :]).astype(BF)

    if direct:
        steps = transposed_steps()
        share = w_last.shape[0]
        packed = w_middle.reshape(TAPS * share, 128)
        middle_near = [packed] + [swap_wide(packed, 2 * j, wide) for j in range(1, 4)]
        first_pair = jnp.concatenate([w_first, swap_wide(w_first, 1, wide)], axis=0)
        first_pieces = [lax.ppermute(first_pair, MESH, pairs) for pairs in steps]
        first_pieces[0] = after(first_pieces[0], *middle_near)
    else:
        first_all = lax.all_gather(lax.all_gather(w_first, "narrow", axis=1, tiled=True), "wide", axis=0, tiled=True)
        first_pieces = [lax.dynamic_slice_in_dim(first_all, n * low, low, 0)]
        middle_slice = lax.all_gather(w_middle, "wide", axis=2, tiled=True)
        middle_slice = middle_slice.reshape(TAPS, mid, 128).transpose(1, 0, 2).reshape(mid, TAPS * 128)
        last_slice = lax.all_gather(w_last, "wide", axis=0, tiled=True)

    counts = jnp.sum((sides * sides).astype(F32), axis=1)
    small = jnp.concatenate(
        [jnp.stack([gain_first, shift_first, gain_middle, shift_middle]) * (1.0 / wide),
         jnp.broadcast_to(counts[:, None], (micro, 128))], axis=0
    )

    tile = arr((8, 128), F32)
    across = arr((wide, 8, low), F32)
    flat = arr((rows, mid), BF)
    flat32 = arr((rows, mid), F32)

    w_rows, send_far, own_far, send_near, own_near = run(
        first_product, (inputs, *first_pieces),
        [arr((low, mid), BF), flat, flat32, flat, flat32], flops=2 * micro * rows * low * mid,
    )
    joined, begun = reduce_narrow(send_far, own_far, send_near, own_near)
    if direct:
        middle_near = jnp.concatenate([after(middle_near[0], begun)] + middle_near[1:], axis=0)
        middle_far = swap_wide(middle_near, 1, wide)
    mask = mask_of(after(sides, begun))
    beside = ()
    if direct:
        held = after(w_last, mask)
        last_near = jnp.concatenate([held] + [swap_wide(held, 2 * j, wide) for j in range(1, 4)], axis=0)
        beside = (middle_far, last_near)
    pre_one, message = run(first_join, (*joined, mask, small), [flat, arr((16, 128), F32)])
    begun, total = sum_wide(message, wide, beside=beside)
    if direct:
        last_far = swap_wide(after(last_near, begun), 1, wide)
    pre_ones = from_all(pre_one, total)
    sums_one = from_all(total)
    if direct:
        middle_slice = run(gather_middle, (middle_near, middle_far), [arr((mid, TAPS * 128), BF)])[0]
        middle_slice = after(middle_slice, last_far)

    hidden_one, pre_two, coef_one, message, params = run(
        middle_forward, (*pre_ones, *sums_one, mask, to_canvas, to_rows, middle_slice),
        [arr((micro, places, mid), BF), arr((micro, rows, 128), BF), arr((micro, 8, mid), F32), tile, arr((NARROW, 8, 128), F32)],
        [pltpu.VMEM((rows, mid), BF), pltpu.VMEM((places + 2 * img * (PITCH + 1), TAPS * 128), F32), pltpu.VMEM((places, 128), BF)],
        flops=2 * micro * places * mid * TAPS * 128,
    )
    if direct:
        last_slice = run(gather_last, (last_near, last_far), [arr((mid, low), BF)])[0]
    _, total = sum_wide(message, wide)
    pre_twos = from_all(pre_two, total)
    sums_two = from_all(total)
    held = after(middle_slice, pre_twos[3], sums_two[3])
    middle_away = swap_chip(held)

    hidden_two, own_two, coef_two, pre_three, message = run(
        last_forward, (*pre_twos, *sums_two, params, mask, last_slice),
        [arr((micro, rows, mid), BF), flat, arr((8, mid), F32), arr((micro, rows, low), F32), across],
        flops=2 * micro * rows * low * mid,
    )
    parts_three = lax.all_to_all(message, "wide", 0, 0, tiled=True)
    block_out, grad_sum, coef_three, message = run(
        block_output,
        (pre_three, inputs, cotangent, parts_three, params, gain_last[None], shift_last[None], mask),
        [arr(inputs.shape, BF), arr((micro, rows, low), F32), arr((micro, 8, low), F32), across],
    )
    parts_four = lax.all_to_all(message, "wide", 0, 0, tiled=True)

    grad_three, send_far, own_far, send_near, own_near, level_three, tilt_three = run(
        last_backward, (pre_three, grad_sum, parts_four, params, coef_three, mask, last_slice),
        [arr((micro, rows, low), BF), flat, flat32, flat, flat32, arr((1, low), F32), arr((1, low), F32)],
        flops=2 * micro * rows * low * mid,
    )
    joined, begun = reduce_narrow(send_far, own_far, send_near, own_near, middle_away)
    grad_three = after(grad_three, begun)

    def handed(channels):
        if direct:
            return [arr((mid // 2, channels), F32), arr((mid // 2, channels), BF)]
        return [arr((mid, channels), F32)]

    last_sum = run(
        last_weight, (hidden_two, grad_three), handed(low), [pltpu.VMEM((mid, low), F32)],
        flops=2 * micro * rows * low * mid,
    )
    slim = arr((rows, 128), BF)
    row = arr((1, 128), F32)
    if direct:
        got_last_sum = swap_wide(last_sum[1], 1, wide)
        joined = (after(joined[0], got_last_sum), *joined[1:])
    grad_two, own_q, near_q, far_q, message = run(
        middle_join, (*joined, own_two, coef_two, mask), [flat32, slim, slim, arr((2, rows, 128), BF), tile]
    )
    got_far = swap_chip(far_q)
    _, total_five = sum_wide(message, wide, late=(got_far,))
    near_q, got_far = lax.optimization_barrier((near_q, got_far, total_five))[:2]
    got_near, got_last = swap_core(near_q), swap_core(got_far)
    middle_slices = (middle_slice, swap_core(held), middle_away, swap_core(middle_away))
    sums_five = from_all(total_five)

    grad_one, message = run(
        middle_backward,
        (grad_two, own_two, total_five, params, coef_two, mask, pre_one, coef_one, to_canvas, to_rows, *middle_slices),
        [flat, tile],
        [pltpu.VMEM((rows, mid), BF), pltpu.VMEM((TAPS, mid, mid), BF),
         pltpu.VMEM((places + 2 * img * (PITCH + 1), mid), F32), pltpu.VMEM((places, mid), F32)],
        flops=2 * places * mid * TAPS * mid,
    )
    level_two, tilt_two, *middle_sum = run(
        middle_weight,
        (hidden_one, own_q, got_near, got_far, got_last, pre_two, *sums_five, sums_two[0], params, mask, to_canvas),
        [row, row, *handed(TAPS * 128)],
        [pltpu.VMEM((mid, TAPS * 128), F32), pltpu.VMEM((places, TAPS * 128), BF),
         pltpu.VMEM((places + 2 * img * (PITCH + 1), 128), F32)],
        flops=2 * micro * places * mid * TAPS * 128,
    )
    begun, total = sum_wide(message, wide, beside=middle_sum)
    grad_ones = from_all(after(grad_one, sums_five[2]), total)
    sums_six = from_all(total)
    if direct:
        got_middle = swap_wide(after(middle_sum[1], begun), 1, wide)

    out_first = [arr((low // 2, mid), F32), arr((low // 2, mid), BF)] if direct else [arr((low, mid), F32)]
    level_one, tilt_one, grad_pre_one, *first_sum = run(
        first_weight,
        (*grad_ones, *pre_ones, *sums_six, after(params, got_middle) if direct else params, coef_one, mask, inputs),
        [row, row, arr((micro, rows, mid), BF), *out_first], [pltpu.VMEM((low, mid), F32)],
        flops=2 * micro * rows * low * mid,
    )
    input_grad = run(
        input_gradient, (grad_pre_one, w_rows, grad_sum), [arr((micro, rows, low), F32)],
        flops=2 * micro * rows * low * mid,
    )[0]

    if direct:
        got_first = swap_wide(first_sum[1], 1, wide)
        channels = TAPS * 128
        keep, keep_last, *sends = run(
            merge_wide, (middle_sum[0], after(got_middle, first_sum[1]), last_sum[0], got_last_sum),
            [arr((share, channels), F32), arr((share, low), F32)] + [arr((share, channels + low), BF)] * 3,
        )
        parts = [swap_wide(send, 2 * j + 2, wide) for j, send in enumerate(sends)]
        sends = run(merge_first, (first_sum[0], after(got_first, *parts[0:2])), [arr((low // 2, cols), BF)] * NARROW)
        arrived = [
            lax.ppermute(send, MESH, [(dst, src) for src, dst in pairs]) for send, pairs in zip(sends, steps)
        ]
        grad_middle, grad_last = run(
            finish_wide, (after(keep, arrived[0]), keep_last, *parts),
            [arr((TAPS, share, 128), F32), arr((share, low), F32)],
        )
        grad_middle = grad_middle.reshape(3, 3, share, 128)
        grad_first = arrived[0].astype(F32)
        for piece in arrived[1:]:
            grad_first = grad_first + piece.astype(F32)
    else:
        grad_last = lax.psum_scatter(last_sum[0], "wide", scatter_dimension=0, tiled=True)
        grad_middle = lax.psum_scatter(middle_sum[0], "wide", scatter_dimension=0, tiled=True)
        share = grad_middle.shape[0]
        grad_middle = grad_middle.reshape(share, TAPS, 128).transpose(1, 0, 2).reshape(3, 3, share, 128)
        whole = lax.psum(first_sum[0], "wide")
        whole = lax.all_gather(whole, "narrow", axis=0, tiled=True)
        share = whole.shape[0] // wide
        grad_first = lax.dynamic_slice(whole, (w * share, n * cols), (share, cols))
    return (
        block_out, input_grad, grad_first, grad_middle, grad_last,
        tilt_one[0], level_one[0], tilt_two[0], level_two[0], tilt_three[0], level_three[0],
    )


def solution(mesh):
    wide = mesh.shape["wide"]
    placed = (
        P(None, "wide", "narrow"),
        P(None, "wide"),
        P("wide", "narrow"),
        P(None, None, "wide", "narrow"),
        P("wide", "narrow"),
        P("narrow"),
        P("narrow"),
        P("narrow"),
        P("narrow"),
        P("narrow"),
        P("narrow"),
        P(None, "wide", "narrow"),
    )
    return jax.shard_map(
        lambda *arrays: on_device(*arrays, wide=wide),
        mesh=mesh,
        in_specs=placed,
        out_specs=(
            P(None, "wide", "narrow"),
            P(None, "wide", "narrow"),
            P("wide", "narrow"),
            P(None, None, "wide", "narrow"),
            P("wide", "narrow"),
            P("narrow"),
            P("narrow"),
            P("narrow"),
            P("narrow"),
            P("narrow"),
            P("narrow"),
        ),
        check_vma=False,
    )
```

```python
import jax
import jax.numpy as jnp
from jax import lax
from jax.experimental import pallas as pl
from jax.experimental.pallas import tpu as pltpu
from jax.sharding import PartitionSpec as P


F32 = jnp.float32
BF = jnp.bfloat16
EPS = 1e-05
SIDE = 7
PITCH = 8
TAPS = 9
NARROW = 4
MESH = ("narrow", "wide")
VMEM_BYTES = 20 * 2**20


def dot(left, right):
    return jnp.dot(left, right, preferred_element_type=F32)


def dot_nt(left, right):
    return lax.dot_general(left, right, (((1,), (1,)), ((), ())), preferred_element_type=F32)


def dot_tn(left, right):
    return lax.dot_general(left, right, (((0,), (0,)), ((), ())), preferred_element_type=F32)


def position():
    n, w = lax.axis_index("narrow"), lax.axis_index("wide")
    return n, w // 2, w % 2


def run(kernel, operands, outs, scratch=(), flops=0):
    moved = sum(o.size * o.dtype.itemsize for o in (*operands, *outs))
    return pl.pallas_call(
        kernel,
        out_shape=outs,
        name=kernel.__name__,
        in_specs=[pl.BlockSpec(memory_space=pltpu.VMEM)] * len(operands),
        out_specs=[pl.BlockSpec(memory_space=pltpu.VMEM)] * len(outs),
        scratch_shapes=list(scratch),
        cost_estimate=pl.CostEstimate(flops=flops, bytes_accessed=moved, transcendentals=0),
        compiler_params=pltpu.CompilerParams(vmem_limit_bytes=VMEM_BYTES),
    )(*operands)


def arr(shape, dtype):
    return jax.ShapeDtypeStruct(shape, dtype)


def by_rows(rows, body, carry):
    return body(pl.ds(0, rows), carry)


def fold(values):
    total = values[0:8]
    for start in range(8, values.shape[0], 8):
        total = total + values[start : start + 8]
    return total


def zeros_acc(channels):
    return (jnp.zeros((8, channels), F32), jnp.zeros((8, channels), F32))


def column_sum(acc):
    return jnp.sum(acc, axis=0, keepdims=True)


def sigmoid(values):
    return 0.5 * jnp.tanh(0.5 * values) + 0.5


def coefficients(total, squares, inverse, gain, shift):
    mean = total * inverse
    spread = squares * inverse - mean * mean
    scale = lax.rsqrt(spread + EPS)
    slope = gain * scale
    return mean, scale, slope, shift - mean * slope


def wide_row(block, first, count=NARROW):
    return jnp.concatenate([block[first + k : first + k + 1] for k in range(count)], axis=1)


def row_of(block, first, index):
    rows = [jnp.where(index == k, block[first + k : first + k + 1], 0.0) for k in range(NARROW)]
    return rows[0] + rows[1] + rows[2] + rows[3]


def inverse_count(params, b, channels):
    row = params[b, 4:5, :]
    return row if channels == 128 else jnp.concatenate([row] * (channels // 128), axis=1)


def lane_block(index):
    return pl.ds(pl.multiple_of(index * 128, 128), 128)


def send_stats(message, first, second):
    for k in range(NARROW):
        message[k : k + 1, :] = first[:, 128 * k : 128 * k + 128]
        message[NARROW + k : NARROW + k + 1, :] = second[:, 128 * k : 128 * k + 128]


def repeat_first(message):
    block = message[0]
    for place in range(1, message.shape[0]):
        message[place] = block


def total_of(parts, index):
    total = parts[index]
    for place in range(NARROW, parts.shape[0], NARROW):
        total = total + parts[place + index]
    return total


def sum_parts(parts):
    total = parts[0]
    for place in range(1, parts.shape[0]):
        total = total + parts[place]
    return total


def first_product(x, *refs):
    pieces, (w_first, send_far, own_far, send_near, own_near) = refs[:-5], refs[-5:]
    n, z, y = position()
    if len(pieces) == 1:
        w_first[...] = pieces[0][...]
    else:
        rows = pieces[0].shape[0] // 2
        for j, piece in enumerate(pieces):
            for dy in range(2):
                here = pl.ds(pl.multiple_of((y ^ dy) * rows, rows), rows)
                w_first[here, lane_block((z - j) & 3)] = piece[dy * rows : (dy + 1) * rows, :]
    for ref, m in ((send_far, 3), (own_far, 2), (send_near, 1), (own_near, 0)):
        ref[...] = dot(x[n ^ m], w_first[...]).astype(ref.dtype)


def first_join(own, near, far, mask, small, pre, message):
    b = position()[0]

    def body(ds, acc):
        values = own[ds, :] + near[ds, :].astype(F32) + far[ds, :].astype(F32)
        pre[ds, :] = values.astype(BF)
        kept = mask[b, ds, :] * values
        return acc[0] + fold(kept), acc[1] + fold(kept * values)

    sums = by_rows(own.shape[0], body, zeros_acc(own.shape[1]))
    send_stats(message, column_sum(sums[0]), column_sum(sums[1]))
    message[8:16, :] = small[...]


def middle_forward(pre0, pre1, pre2, pre3, sum0, sum1, sum2, sum3, mask, to_canvas, to_rows, weight,
                   hidden, pre, coef, message, params, active, spread, joined):
    n = position()[0]
    blocks = (sum0[...], sum1[...], sum2[...], sum3[...])
    for m, block in enumerate(blocks):
        params[n ^ m, 0:4, :] = block[8:12]
    for b in range(NARROW):
        params[b, 4:5, :] = 1.0 / blocks[0][12 + b : 13 + b]
        params[b, 5:8, :] = jnp.zeros((3, 128), F32)
    rows, places = pre0.shape[0], to_canvas.shape[0]
    img = places // (SIDE * PITCH)
    margin = img * (PITCH + 1)
    gain = jnp.concatenate([params[k, 0:1, :] for k in range(NARROW)], axis=1)
    shift = jnp.concatenate([params[k, 1:2, :] for k in range(NARROW)], axis=1)
    spread[0:margin, :] = jnp.zeros((margin, spread.shape[1]), F32)
    spread[margin + places :, :] = jnp.zeros((margin, spread.shape[1]), F32)
    line = img * PITCH
    for m, source in enumerate((pre0, pre1, pre2, pre3)):
        b = n ^ m
        block = blocks[m]
        mean, scale, slope, offset = coefficients(
            wide_row(block, 0), wide_row(block, NARROW), inverse_count(params, b, gain.shape[1]), gain, shift
        )
        for k, row in enumerate((mean, scale, slope, offset)):
            coef[m, k : k + 1, :] = row

        def activate(ds, carry):
            act = source[ds, :].astype(F32) * slope + offset
            active[ds, :] = (mask[b, ds, :] * act * sigmoid(act)).astype(BF)
            return carry

        by_rows(rows, activate, 0)
        hidden[m] = dot(to_canvas[...], active[...]).astype(BF)
        spread[margin : margin + places, :] = dot(hidden[m], weight[...])
        for top in range(SIDE):
            acc = None
            for tap in range(TAPS):
                start = margin + top * line + ((tap // 3 - 1) * PITCH + tap % 3 - 1) * img
                part = spread[start : start + line, 128 * tap : 128 * tap + 128]
                acc = part if acc is None else acc + part
            joined[top * line : (top + 1) * line, :] = acc.astype(BF)
        pre[m] = dot(to_rows[...], joined[...]).astype(BF)

        def collect(ds, acc):
            values = pre[m, ds, :].astype(F32)
            kept = mask[b, ds, :] * values
            return acc[0] + fold(kept), acc[1] + fold(kept * values)

        sums = by_rows(rows, collect, zeros_acc(128))
        message[0, 2 * m : 2 * m + 1, :] = column_sum(sums[0])
        message[0, 2 * m + 1 : 2 * m + 2, :] = column_sum(sums[1])
    repeat_first(message)


def last_forward(src0, src1, src2, src3, parts, params, mask, weight,
                 hidden, own, coef, pre, message):
    n = position()[0]
    rows = own.shape[0]
    sources = (src0, src1, src2, src3)
    blocks = [total_of(parts, n ^ i) for i in range(NARROW)]
    for m in range(NARROW):
        b = n ^ m
        for i in range(NARROW):
            j = m ^ i
            here = lane_block(n ^ i)
            mean, scale, slope, offset = coefficients(
                blocks[i][2 * j : 2 * j + 1], blocks[i][2 * j + 1 : 2 * j + 2], inverse_count(params, b, 128),
                params[n ^ i, 2:3, :], params[n ^ i, 3:4, :],
            )
            if m == 0:
                own[:, here] = sources[i][j]
                for k, row in enumerate((mean, scale, slope, offset)):
                    coef[k : k + 1, here] = row

            def activate(ds, carry):
                act = sources[i][j, ds, :].astype(F32) * slope + offset
                hidden[m, ds, here] = (mask[b, ds, :] * act * sigmoid(act)).astype(BF)
                return carry

            by_rows(rows, activate, 0)
        pre[m] = dot(hidden[m], weight[...])

        def collect(ds, acc):
            values = pre[m, ds, :]
            kept = mask[b, ds, :] * values
            return acc[0] + fold(kept), acc[1] + fold(kept * values)

        sums = by_rows(rows, collect, zeros_acc(pre.shape[2]))
        message[0, 2 * m : 2 * m + 1, :] = column_sum(sums[0])
        message[0, 2 * m + 1 : 2 * m + 2, :] = column_sum(sums[1])
    repeat_first(message)


def block_output(pre, x, cotangent, parts, params, gain, shift, mask, out, grad, coef, message):
    n = position()[0]
    rows, channels = pre.shape[1:]
    block = sum_parts(parts)
    for m in range(NARROW):
        b = n ^ m
        mean, scale, slope, offset = coefficients(
            block[2 * m : 2 * m + 1], block[2 * m + 1 : 2 * m + 2], inverse_count(params, b, channels), gain[...], shift[...]
        )
        for k, row in enumerate((mean, scale, slope, offset)):
            coef[m, k : k + 1, :] = row
        back = mean * scale

        def body(ds, acc):
            values = pre[m, ds, :]
            inside = mask[b, ds, :]
            summed = values * slope + offset + x[b, ds, :].astype(F32)
            gate = sigmoid(summed)
            value = summed * gate
            out[b, ds, :] = (inside * value).astype(BF)
            local = inside * cotangent[b, ds, :].astype(F32) * (gate + value * (1.0 - gate))
            grad[m, ds, :] = local
            return acc[0] + fold(local), acc[1] + fold(local * (values * scale - back))

        sums = by_rows(rows, body, zeros_acc(channels))
        message[0, 2 * m : 2 * m + 1, :] = column_sum(sums[0])
        message[0, 2 * m + 1 : 2 * m + 2, :] = column_sum(sums[1])
    repeat_first(message)


def last_backward(pre, grad, parts, params, coef, mask, weight,
                  grad_pre, send_far, own_far, send_near, own_near, level_sum, tilt_sum):
    n = position()[0]
    rows = pre.shape[1]
    block = sum_parts(parts)
    for s, ref in enumerate((level_sum, tilt_sum)):
        acc = block[s : s + 1]
        for m in range(1, NARROW):
            acc = acc + block[2 * m + s : 2 * m + s + 1]
        ref[...] = acc
    for m, ref in ((3, send_far), (2, own_far), (1, send_near), (0, own_near)):
        b = n ^ m
        mean, scale, slope = (coef[m, k : k + 1, :] for k in range(3))
        inverse = inverse_count(params, b, block.shape[1])
        level = block[2 * m : 2 * m + 1] * inverse
        tilt = block[2 * m + 1 : 2 * m + 2] * inverse
        level, tilt = level - mean * scale * tilt, scale * tilt

        def body(ds, carry):
            away = mask[b, ds, :] * (level + pre[m, ds, :] * tilt)
            grad_pre[m, ds, :] = (slope * (grad[m, ds, :] - away)).astype(BF)
            return carry

        by_rows(rows, body, 0)
        ref[...] = dot_nt(grad_pre[m], weight[...]).astype(ref.dtype)


def middle_join(own, near, far, pre, coef, mask, grad, own_q, near_q, far_q, message):
    b = position()[0]
    mean, scale, slope, offset = (coef[k : k + 1, :] for k in range(4))
    back = mean * scale

    def body(ds, acc):
        values = pre[ds, :].astype(F32)
        act = values * slope + offset
        gate = sigmoid(act)
        total = own[ds, :] + near[ds, :].astype(F32) + far[ds, :].astype(F32)
        local = total * mask[b, ds, :] * (gate * (1.0 + act * (1.0 - gate)))
        grad[ds, :] = local
        return acc[0] + fold(local), acc[1] + fold(local * (values * scale - back))

    sums = by_rows(own.shape[0], body, zeros_acc(own.shape[1]))
    send_stats(message.at[0], column_sum(sums[0]), column_sum(sums[1]))
    repeat_first(message)
    own_q[...] = grad[:, lane_block(b)].astype(BF)
    near_q[...] = grad[:, lane_block(b ^ 1)].astype(BF)
    far_q[0] = grad[:, lane_block(b ^ 2)].astype(BF)
    far_q[1] = grad[:, lane_block(b ^ 3)].astype(BF)


def middle_backward(grad, pre, parts, params, coef, mask, first_pre, first_coef, to_canvas, to_rows,
                    w0, w1, w2, w3, grad_first, message,
                    grad_pre, weight, gathered, canvas):
    n = position()[0]
    rows, places = grad.shape[0], to_canvas.shape[0]
    img = places // (SIDE * PITCH)
    margin = img * (PITCH + 1)
    block = sum_parts(parts)
    mean, scale, slope = (coef[k : k + 1, :] for k in range(3))
    inverse = inverse_count(params, n, grad.shape[1])
    level = wide_row(block, 0) * inverse
    tilt = wide_row(block, NARROW) * inverse
    level, tilt = level - mean * scale * tilt, scale * tilt

    def body(ds, carry):
        away = mask[n, ds, :] * (level + pre[ds, :].astype(F32) * tilt)
        grad_pre[ds, :] = (slope * (grad[ds, :] - away)).astype(BF)
        return carry

    by_rows(rows, body, 0)
    for j, piece in enumerate((w0, w1, w2, w3)):
        for tap in range(TAPS):
            weight[tap, :, lane_block(n ^ j)] = piece[:, 128 * tap : 128 * tap + 128]
    canvas[...] = dot(to_canvas[...], grad_pre[...]).astype(BF).astype(F32)
    gathered[...] = jnp.zeros_like(gathered)
    for tap in range(TAPS):
        start = margin + ((tap // 3 - 1) * PITCH + tap % 3 - 1) * img
        gathered[start : start + places, :] += dot_nt(canvas[...].astype(BF), weight[tap])
    canvas[...] = gathered[margin : margin + places, :]
    grad_pre[...] = dot(to_rows[...], canvas[...].astype(BF)).astype(BF)
    mean, scale, slope, offset = (first_coef[0, k : k + 1, :] for k in range(4))
    back = mean * scale

    def finish(ds, acc):
        values = first_pre[ds, :].astype(F32)
        act = values * slope + offset
        gate = sigmoid(act)
        local = grad_pre[ds, :].astype(F32) * mask[n, ds, :] * (gate * (1.0 + act * (1.0 - gate)))
        grad_first[ds, :] = local.astype(BF)
        return acc[0] + fold(local), acc[1] + fold(local * (values * scale - back))

    sums2 = by_rows(rows, finish, zeros_acc(grad.shape[1]))
    send_stats(message, column_sum(sums2[0]), column_sum(sums2[1]))


def first_weight(g0, g1, g2, g3, p0, p1, p2, p3, sum0, sum1, sum2, sum3, params, coef, mask, x,
                 level_sum, tilt_sum, grad_pre, *refs):
    outs, acc = refs[:-1], refs[-1]
    n, z, y = position()
    rows, channels = g0.shape
    blocks = (sum0[...], sum1[...], sum2[...], sum3[...])
    every = blocks[0] + blocks[1] + blocks[2] + blocks[3]
    for m, (g, pre) in enumerate(((g0, p0), (g1, p1), (g2, p2), (g3, p3))):
        b = n ^ m
        block = blocks[m]
        mean, scale, slope = (coef[m, k : k + 1, :] for k in range(3))
        inverse = inverse_count(params, b, channels)
        level = wide_row(block, 0) * inverse
        tilt = wide_row(block, NARROW) * inverse
        level, tilt = level - mean * scale * tilt, scale * tilt
        away = mask[b] * (level + pre[...].astype(F32) * tilt)
        grad_pre[m] = (slope * (g[...].astype(F32) - away)).astype(BF)
        product = dot_tn(x[b], grad_pre[m])
        if m == 0:
            acc[...] = product
        else:
            acc[...] += product
    if len(outs) == 1:
        outs[0][...] = acc[...]
    else:
        half = acc.shape[0] // 2
        for ref, h in zip(outs, (y, 1 - y)):
            top = pl.multiple_of(h * half, half)
            for j in range(NARROW):
                block = acc[pl.ds(top, half), lane_block((z - j) & 3)]
                ref[:, 128 * j : 128 * j + 128] = block.astype(ref.dtype)
    level_sum[...] = row_of(every, 0, n)
    tilt_sum[...] = row_of(every, NARROW, n)


def input_gradient(grad_pre, weight, grad, out):
    n = position()[0]
    for m in range(NARROW):
        out[n ^ m] = dot_nt(grad_pre[m], weight[...]) + grad[m]


def last_weight(hidden, grad_pre, *refs):
    acc = refs[-1]
    for m in range(NARROW):
        product = dot_tn(hidden[m], grad_pre[m])
        if m == 0:
            acc[...] = product
        else:
            acc[...] += product
    hand_out(acc, refs[:-1])


def hand_out(acc, outs):
    if len(outs) == 1:
        outs[0][...] = acc[...]
        return
    _, z, y = position()
    own, away = outs
    rows = acc.shape[0] // 8
    for j in range(4):
        place = pl.ds(j * rows, rows)
        for ref, dy in ((own, 0), (away, 1)):
            top = ((z ^ j) * 2 + (y ^ dy)) * rows
            ref[place, :] = acc[pl.ds(pl.multiple_of(top, rows), rows), :].astype(ref.dtype)


def middle_weight(hidden, q0, q1, far, last, pre, sum0, sum1, sum2, sum3, norm, params, mask, to_canvas,
                  level_sum, tilt_sum, *refs):
    outs, (acc, shifted, canvas) = refs[:-3], refs[-3:]
    n = position()[0]
    places = to_canvas.shape[0]
    img = places // (SIDE * PITCH)
    margin = img * (PITCH + 1)
    canvas[0:margin, :] = jnp.zeros((margin, 128), F32)
    canvas[margin + places :, :] = jnp.zeros((margin, 128), F32)
    norms = total_of(norm, n)
    blocks = (sum0[...], sum1[...], sum2[...], sum3[...])
    every = blocks[0] + blocks[1] + blocks[2] + blocks[3]
    level_sum[...] = row_of(every, 0, n)
    tilt_sum[...] = row_of(every, NARROW, n)
    for m, piece in enumerate((q0[...], q1[...], far[0], last[1])):
        b = n ^ m
        inverse = inverse_count(params, b, 128)
        mean, scale, slope, _ = coefficients(
            norms[2 * m : 2 * m + 1], norms[2 * m + 1 : 2 * m + 2], inverse, params[n, 2:3, :], params[n, 3:4, :]
        )
        block = blocks[m]
        level = row_of(block, 0, n) * inverse
        tilt = row_of(block, NARROW, n) * inverse
        level, tilt = level - mean * scale * tilt, scale * tilt
        away = mask[b] * (level + pre[m].astype(F32) * tilt)
        grad_pre = (slope * (piece.astype(F32) - away)).astype(BF)
        canvas[margin : margin + places, :] = dot(to_canvas[...], grad_pre)
        for tap in range(TAPS):
            start = margin - ((tap // 3 - 1) * PITCH + tap % 3 - 1) * img
            shifted[:, 128 * tap : 128 * tap + 128] = canvas[start : start + places, :].astype(BF)
        product = dot_tn(hidden[m], shifted[...])
        if m == 0:
            acc[...] = product
        else:
            acc[...] += product
    hand_out(acc, outs)


def gather_middle(near, far, out):
    _, z, y = position()
    rows = out.shape[0] // 8
    for dy, stack in enumerate((near, far)):
        for j in range(4):
            here = pl.ds(pl.multiple_of(((z ^ j) * 2 + (y ^ dy)) * rows, rows), rows)
            for tap in range(TAPS):
                top = (j * TAPS + tap) * rows
                out[here, 128 * tap : 128 * tap + 128] = stack[top : top + rows, :]


def gather_last(near, far, out):
    _, z, y = position()
    rows = out.shape[0] // 8
    for dy, stack in enumerate((near, far)):
        for j in range(4):
            here = pl.ds(pl.multiple_of(((z ^ j) * 2 + (y ^ dy)) * rows, rows), rows)
            out[here, :] = stack[j * rows : (j + 1) * rows, :]


def merge_first(own, away, *sends):
    for j, send in enumerate(sends):
        here = slice(128 * j, 128 * j + 128)
        send[...] = (own[:, here] + away[:, here].astype(F32)).astype(BF)


def add_tiles(*refs):
    total = refs[0][...]
    for ref in refs[1:-1]:
        total = total + ref[...]
    refs[-1][...] = total


def add_parts(parts, out):
    out[...] = sum_parts(parts)


def merge_wide(own, away, own_last, away_last, keep, keep_last, *sends):
    rows, middle = keep.shape
    keep[...] = own[0:rows, :] + away[0:rows, :].astype(F32)
    keep_last[...] = own_last[0:rows, :] + away_last[0:rows, :].astype(F32)
    for j, send in enumerate(sends):
        here = slice((j + 1) * rows, (j + 2) * rows)
        send[:, 0:middle] = (own[here, :] + away[here, :].astype(F32)).astype(BF)
        send[:, middle:] = (own_last[here, :] + away_last[here, :].astype(F32)).astype(BF)


def finish_wide(keep, keep_last, p1, p2, p3, out, out_last):
    middle = keep.shape[1]
    for tap in range(TAPS):
        here = slice(128 * tap, 128 * tap + 128)
        out[tap] = keep[:, here] + p1[:, here].astype(F32) + p2[:, here].astype(F32) + p3[:, here].astype(F32)
    out_last[...] = (
        keep_last[...] + p1[:, middle:].astype(F32) + p2[:, middle:].astype(F32) + p3[:, middle:].astype(F32)
    )


def exchange(message):
    return lax.all_to_all(message, ("wide", "narrow"), 0, 0, tiled=True)


def swap_core(values):
    return lax.ppermute(values, "narrow", [(i, i ^ 1) for i in range(NARROW)])


def swap_chip(values):
    return lax.ppermute(values, "narrow", [(i, i ^ 2) for i in range(NARROW)])


def swap_wide(values, step, wide):
    return lax.ppermute(values, "wide", [(i, i ^ step) for i in range(wide)])


def after(value, *others):
    return lax.optimization_barrier((value, *others))[0]


def from_all(values, *others):
    far = swap_chip(values)
    if others:
        return values, swap_core(after(values, *others)), far, swap_core(after(far, *others))
    return values, swap_core(values), far, swap_core(far)


def add(*tiles):
    return run(add_tiles, tiles, [arr(tiles[0].shape, F32)])[0]


def sum_wide(values, wide, beside=(), late=()):
    if wide == 8:
        values = add(after(values, *beside) if beside else values, swap_wide(values, 1, wide))
        parts = [swap_wide(values, step, wide) for step in (2, 4, 6)]
        total = add(after(values, *late) if late else values, *parts)
        return values, total
    step = 1
    while step < wide:
        values = add(values, swap_wide(values, step, wide))
        step *= 2
    return values, values


def reduce_narrow(send_far, own_far, send_near, own_near, *others):
    got_far = swap_core(send_far)
    got_near = swap_core(send_near)
    joined = (own_far + got_far.astype(F32)).astype(BF)
    if others:
        joined = after(joined, *others)
    return (own_near, got_near, swap_chip(joined)), joined


def transposed_steps():
    steps = []
    for j in range(NARROW):
        pairs = []
        for k in range(NARROW):
            for z in range(4):
                for y in range(2):
                    pairs.append((k * 8 + 2 * z + y, z * 8 + 2 * ((k + j) % 4) + y))
        steps.append(pairs)
    return steps


def on_device(inputs, sides, w_first, w_middle, w_last, gain_first, shift_first, gain_middle, shift_middle,
              gain_last, shift_last, cotangent, *, wide):
    micro, rows, low = inputs.shape
    img = sides.shape[1]
    mid = w_last.shape[0] * wide
    cols = w_first.shape[1]
    places = img * SIDE * PITCH
    direct = wide == 8
    n = lax.axis_index("narrow")
    w = lax.axis_index("wide")

    spots = jnp.arange(rows, dtype=jnp.int32)
    spot_y, spot_x, spot_img = spots % 49 // 7, spots % 7, spots // 49

    def mask_of(limits):
        limits = jnp.repeat(limits, 49, axis=1)
        return ((spot_y[None] < limits) & (spot_x[None] < limits)).astype(F32)[:, :, None]

    place = (spot_y * PITCH + spot_x) * img + spot_img
    to_canvas = (jnp.arange(places, dtype=jnp.int32)[:, None] == place[None, :]).astype(BF)
    to_rows = (place[:, None] == jnp.arange(places, dtype=jnp.int32)[None, :]).astype(BF)

    if direct:
        steps = transposed_steps()
        share = w_last.shape[0]
        packed = w_middle.reshape(TAPS * share, 128)
        middle_near = [packed] + [swap_wide(packed, 2 * j, wide) for j in range(1, 4)]
        first_pair = jnp.concatenate([w_first, swap_wide(w_first, 1, wide)], axis=0)
        first_pieces = [lax.ppermute(first_pair, MESH, pairs) for pairs in steps]
        first_pieces[0] = after(first_pieces[0], *middle_near)
    else:
        first_all = lax.all_gather(lax.all_gather(w_first, "narrow", axis=1, tiled=True), "wide", axis=0, tiled=True)
        first_pieces = [lax.dynamic_slice_in_dim(first_all, n * low, low, 0)]
        middle_slice = lax.all_gather(w_middle, "wide", axis=2, tiled=True)
        middle_slice = middle_slice.reshape(TAPS, mid, 128).transpose(1, 0, 2).reshape(mid, TAPS * 128)
        last_slice = lax.all_gather(w_last, "wide", axis=0, tiled=True)

    counts = jnp.sum((sides * sides).astype(F32), axis=1)
    small = jnp.concatenate(
        [jnp.stack([gain_first, shift_first, gain_middle, shift_middle]) * (1.0 / wide),
         jnp.broadcast_to(counts[:, None], (micro, 128))], axis=0
    )

    tile = arr((8, 128), F32)
    across = arr((wide, 8, low), F32)
    flat = arr((rows, mid), BF)
    flat32 = arr((rows, mid), F32)

    w_rows, send_far, own_far, send_near, own_near = run(
        first_product, (inputs, *first_pieces),
        [arr((low, mid), BF), flat, flat32, flat, flat32], flops=2 * micro * rows * low * mid,
    )
    joined, begun = reduce_narrow(send_far, own_far, send_near, own_near)
    if direct:
        middle_near = jnp.concatenate([after(middle_near[0], begun)] + middle_near[1:], axis=0)
        middle_far = swap_wide(middle_near, 1, wide)
    mask = mask_of(after(sides, begun))
    beside = ()
    if direct:
        held = after(w_last, mask)
        last_near = jnp.concatenate([held] + [swap_wide(held, 2 * j, wide) for j in range(1, 4)], axis=0)
        beside = (middle_far, last_near)
    pre_one, message = run(first_join, (*joined, mask, small), [flat, arr((16, 128), F32)])
    begun, total = sum_wide(message, wide, beside=beside)
    if direct:
        last_far = swap_wide(after(last_near, begun), 1, wide)
    pre_ones = from_all(pre_one, total)
    sums_one = from_all(total)
    if direct:
        middle_slice = run(gather_middle, (middle_near, middle_far), [arr((mid, TAPS * 128), BF)])[0]
        middle_slice = after(middle_slice, last_far)

    hidden_one, pre_two, coef_one, message, params = run(
        middle_forward, (*pre_ones, *sums_one, mask, to_canvas, to_rows, middle_slice),
        [arr((micro, places, mid), BF), arr((micro, rows, 128), BF), arr((micro, 8, mid), F32), arr((wide * NARROW, 8, 128), F32), arr((NARROW, 8, 128), F32)],
        [pltpu.VMEM((rows, mid), BF), pltpu.VMEM((places + 2 * img * (PITCH + 1), TAPS * 128), F32), pltpu.VMEM((places, 128), BF)],
        flops=2 * micro * places * mid * TAPS * 128,
    )
    if direct:
        last_slice = run(gather_last, (last_near, last_far), [arr((mid, low), BF)])[0]
    parts_two = exchange(message)
    pre_twos = from_all(pre_two, parts_two)
    held = after(middle_slice, pre_twos[3], parts_two)
    middle_away = swap_chip(held)

    hidden_two, own_two, coef_two, pre_three, message = run(
        last_forward, (*pre_twos, parts_two, params, mask, last_slice),
        [arr((micro, rows, mid), BF), flat, arr((8, mid), F32), arr((micro, rows, low), F32), across],
        flops=2 * micro * rows * low * mid,
    )
    parts_three = lax.all_to_all(message, "wide", 0, 0, tiled=True)
    block_out, grad_sum, coef_three, message = run(
        block_output,
        (pre_three, inputs, cotangent, parts_three, params, gain_last[None], shift_last[None], mask),
        [arr(inputs.shape, BF), arr((micro, rows, low), F32), arr((micro, 8, low), F32), across],
    )
    parts_four = lax.all_to_all(message, "wide", 0, 0, tiled=True)

    grad_three, send_far, own_far, send_near, own_near, level_three, tilt_three = run(
        last_backward, (pre_three, grad_sum, parts_four, params, coef_three, mask, last_slice),
        [arr((micro, rows, low), BF), flat, flat32, flat, flat32, arr((1, low), F32), arr((1, low), F32)],
        flops=2 * micro * rows * low * mid,
    )
    joined, begun = reduce_narrow(send_far, own_far, send_near, own_near, middle_away)
    grad_three = after(grad_three, begun)

    def handed(channels):
        if direct:
            return [arr((mid // 2, channels), F32), arr((mid // 2, channels), BF)]
        return [arr((mid, channels), F32)]

    last_sum = run(
        last_weight, (hidden_two, grad_three), handed(low), [pltpu.VMEM((mid, low), F32)],
        flops=2 * micro * rows * low * mid,
    )
    slim = arr((rows, 128), BF)
    row = arr((1, 128), F32)
    if direct:
        got_last_sum = swap_wide(last_sum[1], 1, wide)
        joined = (after(joined[0], got_last_sum), *joined[1:])
    grad_two, own_q, near_q, far_q, message = run(
        middle_join, (*joined, own_two, coef_two, mask), [flat32, slim, slim, arr((2, rows, 128), BF), arr((wide, 8, 128), F32)]
    )
    got_far = swap_chip(far_q)
    middle_slices = (middle_slice, swap_core(held), middle_away, swap_core(middle_away))
    parts_five = lax.all_to_all(after(message, *middle_slices), "wide", 0, 0, tiled=True)
    total_five = run(add_parts, (parts_five,), [tile])[0]
    near_q, got_far = lax.optimization_barrier((near_q, got_far, parts_five))[:2]
    got_near, got_last = swap_core(near_q), swap_core(got_far)
    sums_five = from_all(total_five)

    grad_one, message = run(
        middle_backward,
        (grad_two, own_two, parts_five, params, coef_two, mask, pre_one, coef_one, to_canvas, to_rows, *middle_slices),
        [flat, tile],
        [pltpu.VMEM((rows, mid), BF), pltpu.VMEM((TAPS, mid, mid), BF),
         pltpu.VMEM((places + 2 * img * (PITCH + 1), mid), F32), pltpu.VMEM((places, mid), F32)],
        flops=2 * places * mid * TAPS * mid,
    )
    level_two, tilt_two, *middle_sum = run(
        middle_weight,
        (hidden_one, own_q, got_near, got_far, got_last, pre_two, *sums_five, parts_two, params, mask, to_canvas),
        [row, row, *handed(TAPS * 128)],
        [pltpu.VMEM((mid, TAPS * 128), F32), pltpu.VMEM((places, TAPS * 128), BF),
         pltpu.VMEM((places + 2 * img * (PITCH + 1), 128), F32)],
        flops=2 * micro * places * mid * TAPS * 128,
    )
    begun, total = sum_wide(message, wide, beside=middle_sum)
    grad_ones = from_all(after(grad_one, sums_five[2]), total)
    sums_six = from_all(total)
    if direct:
        got_middle = swap_wide(after(middle_sum[1], begun), 1, wide)

    out_first = [arr((low // 2, mid), F32), arr((low // 2, mid), BF)] if direct else [arr((low, mid), F32)]
    level_one, tilt_one, grad_pre_one, *first_sum = run(
        first_weight,
        (*grad_ones, *pre_ones, *sums_six, after(params, got_middle) if direct else params, coef_one, mask, inputs),
        [row, row, arr((micro, rows, mid), BF), *out_first], [pltpu.VMEM((low, mid), F32)],
        flops=2 * micro * rows * low * mid,
    )
    input_grad = run(
        input_gradient, (grad_pre_one, w_rows, grad_sum), [arr((micro, rows, low), F32)],
        flops=2 * micro * rows * low * mid,
    )[0]

    if direct:
        got_first = swap_wide(first_sum[1], 1, wide)
        channels = TAPS * 128
        keep, keep_last, *sends = run(
            merge_wide, (middle_sum[0], after(got_middle, first_sum[1]), last_sum[0], got_last_sum),
            [arr((share, channels), F32), arr((share, low), F32)] + [arr((share, channels + low), BF)] * 3,
        )
        parts = [swap_wide(send, 2 * j + 2, wide) for j, send in enumerate(sends)]
        sends = run(merge_first, (first_sum[0], after(got_first, *parts[0:2])), [arr((low // 2, cols), BF)] * NARROW)
        arrived = [
            lax.ppermute(send, MESH, [(dst, src) for src, dst in pairs]) for send, pairs in zip(sends, steps)
        ]
        grad_middle, grad_last = run(
            finish_wide, (after(keep, arrived[0]), keep_last, *parts),
            [arr((TAPS, share, 128), F32), arr((share, low), F32)],
        )
        grad_middle = grad_middle.reshape(3, 3, share, 128)
        grad_first = arrived[0].astype(F32)
        for piece in arrived[1:]:
            grad_first = grad_first + piece.astype(F32)
    else:
        grad_last = lax.psum_scatter(last_sum[0], "wide", scatter_dimension=0, tiled=True)
        grad_middle = lax.psum_scatter(middle_sum[0], "wide", scatter_dimension=0, tiled=True)
        share = grad_middle.shape[0]
        grad_middle = grad_middle.reshape(share, TAPS, 128).transpose(1, 0, 2).reshape(3, 3, share, 128)
        whole = lax.psum(first_sum[0], "wide")
        whole = lax.all_gather(whole, "narrow", axis=0, tiled=True)
        share = whole.shape[0] // wide
        grad_first = lax.dynamic_slice(whole, (w * share, n * cols), (share, cols))
    return (
        block_out, input_grad, grad_first, grad_middle, grad_last,
        tilt_one[0], level_one[0], tilt_two[0], level_two[0], tilt_three[0], level_three[0],
    )


def solution(mesh):
    wide = mesh.shape["wide"]
    placed = (
        P(None, "wide", "narrow"),
        P(None, "wide"),
        P("wide", "narrow"),
        P(None, None, "wide", "narrow"),
        P("wide", "narrow"),
        P("narrow"),
        P("narrow"),
        P("narrow"),
        P("narrow"),
        P("narrow"),
        P("narrow"),
        P(None, "wide", "narrow"),
    )
    return jax.shard_map(
        lambda *arrays: on_device(*arrays, wide=wide),
        mesh=mesh,
        in_specs=placed,
        out_specs=(
            P(None, "wide", "narrow"),
            P(None, "wide", "narrow"),
            P("wide", "narrow"),
            P(None, None, "wide", "narrow"),
            P("wide", "narrow"),
            P("narrow"),
            P("narrow"),
            P("narrow"),
            P("narrow"),
            P("narrow"),
            P("narrow"),
        ),
        check_vma=False,
    )
```

```python
import jax
import jax.numpy as jnp
from jax import lax
from jax.experimental import pallas as pl
from jax.experimental.pallas import tpu as pltpu
from jax.sharding import PartitionSpec as P


F32 = jnp.float32
BF = jnp.bfloat16
EPS = 1e-05
SIDE = 7
PITCH = 8
TAPS = 9
NARROW = 4
MESH = ("narrow", "wide")
VMEM_BYTES = 20 * 2**20


def dot(left, right):
    return jnp.dot(left, right, preferred_element_type=F32)


def dot_nt(left, right):
    return lax.dot_general(left, right, (((1,), (1,)), ((), ())), preferred_element_type=F32)


def dot_tn(left, right):
    return lax.dot_general(left, right, (((0,), (0,)), ((), ())), preferred_element_type=F32)


def position():
    n, w = lax.axis_index("narrow"), lax.axis_index("wide")
    return n, w // 2, w % 2


def run(kernel, operands, outs, scratch=(), flops=0):
    moved = sum(o.size * o.dtype.itemsize for o in (*operands, *outs))
    return pl.pallas_call(
        kernel,
        out_shape=outs,
        name=kernel.__name__,
        in_specs=[pl.BlockSpec(memory_space=pltpu.VMEM)] * len(operands),
        out_specs=[pl.BlockSpec(memory_space=pltpu.VMEM)] * len(outs),
        scratch_shapes=list(scratch),
        cost_estimate=pl.CostEstimate(flops=flops, bytes_accessed=moved, transcendentals=0),
        compiler_params=pltpu.CompilerParams(vmem_limit_bytes=VMEM_BYTES),
    )(*operands)


def arr(shape, dtype):
    return jax.ShapeDtypeStruct(shape, dtype)


def by_rows(rows, body, carry):
    return body(pl.ds(0, rows), carry)


def fold(values):
    total = values[0:8]
    for start in range(8, values.shape[0], 8):
        total = total + values[start : start + 8]
    return total


def zeros_acc(channels):
    return (jnp.zeros((8, channels), F32), jnp.zeros((8, channels), F32))


def column_sum(acc):
    return jnp.sum(acc, axis=0, keepdims=True)


def sigmoid(values):
    return 0.5 * jnp.tanh(0.5 * values) + 0.5


def coefficients(total, squares, inverse, gain, shift):
    mean = total * inverse
    spread = squares * inverse - mean * mean
    scale = lax.rsqrt(spread + EPS)
    slope = gain * scale
    return mean, scale, slope, shift - mean * slope


def wide_row(block, first, count=NARROW):
    return jnp.concatenate([block[first + k : first + k + 1] for k in range(count)], axis=1)


def row_of(block, first, index):
    rows = [jnp.where(index == k, block[first + k : first + k + 1], 0.0) for k in range(NARROW)]
    return rows[0] + rows[1] + rows[2] + rows[3]


def inverse_count(params, b, channels):
    row = params[b, 4:5, :]
    return row if channels == 128 else jnp.concatenate([row] * (channels // 128), axis=1)


def lane_block(index):
    return pl.ds(pl.multiple_of(index * 128, 128), 128)


def send_stats(message, first, second):
    for k in range(NARROW):
        message[k : k + 1, :] = first[:, 128 * k : 128 * k + 128]
        message[NARROW + k : NARROW + k + 1, :] = second[:, 128 * k : 128 * k + 128]


def repeat_first(message):
    block = message[0]
    for place in range(1, message.shape[0]):
        message[place] = block


def total_of(parts, index):
    total = parts[index]
    for place in range(NARROW, parts.shape[0], NARROW):
        total = total + parts[place + index]
    return total


def sum_parts(parts):
    total = parts[0]
    for place in range(1, parts.shape[0]):
        total = total + parts[place]
    return total


def place_columns(p0, p1, p2, p3, out):
    z = position()[1]
    for j, piece in enumerate((p0, p1, p2, p3)):
        out[:, lane_block((z - j) & 3)] = piece[...]


def first_product(x, *refs):
    pieces, (w_first, send_far, own_far, send_near, own_near) = refs[:-5], refs[-5:]
    n, z, y = position()
    if len(pieces) == 1:
        w_first[...] = pieces[0][...]
    else:
        rows = pieces[0].shape[0]
        for dy, piece in enumerate(pieces):
            w_first[pl.ds(pl.multiple_of((y ^ dy) * rows, rows), rows), :] = piece[...]
    for ref, m in ((send_far, 3), (own_far, 2), (send_near, 1), (own_near, 0)):
        ref[...] = dot(x[n ^ m], w_first[...]).astype(ref.dtype)


def first_join(own, near, far, mask, small, pre, message):
    b = position()[0]

    def body(ds, acc):
        values = own[ds, :] + near[ds, :].astype(F32) + far[ds, :].astype(F32)
        pre[ds, :] = values.astype(BF)
        kept = mask[b, ds, :] * values
        return acc[0] + fold(kept), acc[1] + fold(kept * values)

    sums = by_rows(own.shape[0], body, zeros_acc(own.shape[1]))
    send_stats(message, column_sum(sums[0]), column_sum(sums[1]))
    message[8:16, :] = small[...]


def middle_forward(pre0, pre1, pre2, pre3, sum0, sum1, sum2, sum3, mask, to_canvas, to_rows, weight,
                   hidden, pre, coef, message, params, active, spread, joined):
    n = position()[0]
    blocks = (sum0[...], sum1[...], sum2[...], sum3[...])
    for m, block in enumerate(blocks):
        params[n ^ m, 0:4, :] = block[8:12]
    for b in range(NARROW):
        params[b, 4:5, :] = 1.0 / blocks[0][12 + b : 13 + b]
        params[b, 5:8, :] = jnp.zeros((3, 128), F32)
    rows, places = pre0.shape[0], to_canvas.shape[0]
    img = places // (SIDE * PITCH)
    margin = img * (PITCH + 1)
    gain = jnp.concatenate([params[k, 0:1, :] for k in range(NARROW)], axis=1)
    shift = jnp.concatenate([params[k, 1:2, :] for k in range(NARROW)], axis=1)
    spread[0:margin, :] = jnp.zeros((margin, spread.shape[1]), F32)
    spread[margin + places :, :] = jnp.zeros((margin, spread.shape[1]), F32)
    line = img * PITCH
    for m, source in enumerate((pre0, pre1, pre2, pre3)):
        b = n ^ m
        block = blocks[m]
        mean, scale, slope, offset = coefficients(
            wide_row(block, 0), wide_row(block, NARROW), inverse_count(params, b, gain.shape[1]), gain, shift
        )
        for k, row in enumerate((mean, scale, slope, offset)):
            coef[m, k : k + 1, :] = row

        def activate(ds, carry):
            act = source[ds, :].astype(F32) * slope + offset
            active[ds, :] = (mask[b, ds, :] * act * sigmoid(act)).astype(BF)
            return carry

        by_rows(rows, activate, 0)
        hidden[m] = dot(to_canvas[...], active[...]).astype(BF)
        spread[margin : margin + places, :] = dot(hidden[m], weight[...])
        for top in range(SIDE):
            acc = None
            for tap in range(TAPS):
                start = margin + top * line + ((tap // 3 - 1) * PITCH + tap % 3 - 1) * img
                part = spread[start : start + line, 128 * tap : 128 * tap + 128]
                acc = part if acc is None else acc + part
            joined[top * line : (top + 1) * line, :] = acc.astype(BF)
        pre[m] = dot(to_rows[...], joined[...]).astype(BF)

        def collect(ds, acc):
            values = pre[m, ds, :].astype(F32)
            kept = mask[b, ds, :] * values
            return acc[0] + fold(kept), acc[1] + fold(kept * values)

        sums = by_rows(rows, collect, zeros_acc(128))
        message[0, 2 * m : 2 * m + 1, :] = column_sum(sums[0])
        message[0, 2 * m + 1 : 2 * m + 2, :] = column_sum(sums[1])
    repeat_first(message)


def last_forward(src0, src1, src2, src3, parts, params, mask, weight,
                 hidden, own, coef, pre, message):
    n = position()[0]
    rows = own.shape[0]
    sources = (src0, src1, src2, src3)
    blocks = [total_of(parts, n ^ i) for i in range(NARROW)]
    for m in range(NARROW):
        b = n ^ m
        for i in range(NARROW):
            j = m ^ i
            here = lane_block(n ^ i)
            mean, scale, slope, offset = coefficients(
                blocks[i][2 * j : 2 * j + 1], blocks[i][2 * j + 1 : 2 * j + 2], inverse_count(params, b, 128),
                params[n ^ i, 2:3, :], params[n ^ i, 3:4, :],
            )
            if m == 0:
                own[:, here] = sources[i][j]
                for k, row in enumerate((mean, scale, slope, offset)):
                    coef[k : k + 1, here] = row

            def activate(ds, carry):
                act = sources[i][j, ds, :].astype(F32) * slope + offset
                hidden[m, ds, here] = (mask[b, ds, :] * act * sigmoid(act)).astype(BF)
                return carry

            by_rows(rows, activate, 0)
        pre[m] = dot(hidden[m], weight[...])

        def collect(ds, acc):
            values = pre[m, ds, :]
            kept = mask[b, ds, :] * values
            return acc[0] + fold(kept), acc[1] + fold(kept * values)

        sums = by_rows(rows, collect, zeros_acc(pre.shape[2]))
        message[0, 2 * m : 2 * m + 1, :] = column_sum(sums[0])
        message[0, 2 * m + 1 : 2 * m + 2, :] = column_sum(sums[1])
    repeat_first(message)


def block_output(pre, x, cotangent, parts, params, gain, shift, mask, out, grad, coef, message):
    n = position()[0]
    rows, channels = pre.shape[1:]
    block = sum_parts(parts)
    for m in range(NARROW):
        b = n ^ m
        mean, scale, slope, offset = coefficients(
            block[2 * m : 2 * m + 1], block[2 * m + 1 : 2 * m + 2], inverse_count(params, b, channels), gain[...], shift[...]
        )
        for k, row in enumerate((mean, scale, slope, offset)):
            coef[m, k : k + 1, :] = row

        def body(ds, acc):
            values = pre[m, ds, :]
            inside = mask[b, ds, :]
            summed = values * slope + offset + x[b, ds, :].astype(F32)
            gate = sigmoid(summed)
            value = summed * gate
            out[b, ds, :] = (inside * value).astype(BF)
            local = inside * cotangent[b, ds, :].astype(F32) * (gate + value * (1.0 - gate))
            grad[m, ds, :] = local
            return acc[0] + fold(local), acc[1] + fold(local * values)

        sums = by_rows(rows, body, zeros_acc(channels))
        first, second = column_sum(sums[0]), column_sum(sums[1])
        message[0, 2 * m : 2 * m + 1, :] = first
        message[0, 2 * m + 1 : 2 * m + 2, :] = scale * (second - mean * first)
    repeat_first(message)


def last_backward(pre, grad, parts, params, coef, mask, weight,
                  grad_pre, send_far, own_far, send_near, own_near, level_sum, tilt_sum):
    n = position()[0]
    rows = pre.shape[1]
    block = sum_parts(parts)
    for s, ref in enumerate((level_sum, tilt_sum)):
        acc = block[s : s + 1]
        for m in range(1, NARROW):
            acc = acc + block[2 * m + s : 2 * m + s + 1]
        ref[...] = acc
    for m, ref in ((3, send_far), (2, own_far), (1, send_near), (0, own_near)):
        b = n ^ m
        mean, scale, slope = (coef[m, k : k + 1, :] for k in range(3))
        inverse = inverse_count(params, b, block.shape[1])
        level = block[2 * m : 2 * m + 1] * inverse
        tilt = block[2 * m + 1 : 2 * m + 2] * inverse
        level, tilt = level - mean * scale * tilt, scale * tilt

        def body(ds, carry):
            away = mask[b, ds, :] * (level + pre[m, ds, :] * tilt)
            grad_pre[m, ds, :] = (slope * (grad[m, ds, :] - away)).astype(BF)
            return carry

        by_rows(rows, body, 0)
        ref[...] = dot_nt(grad_pre[m], weight[...]).astype(ref.dtype)


def middle_join(own, near, far, pre, coef, mask, grad, own_q, near_q, far_q, message):
    b = position()[0]
    mean, scale, slope, offset = (coef[k : k + 1, :] for k in range(4))
    back = mean * scale

    def body(ds, acc):
        values = pre[ds, :].astype(F32)
        act = values * slope + offset
        gate = sigmoid(act)
        total = own[ds, :] + near[ds, :].astype(F32) + far[ds, :].astype(F32)
        local = total * mask[b, ds, :] * (gate * (1.0 + act * (1.0 - gate)))
        grad[ds, :] = local
        return acc[0] + fold(local), acc[1] + fold(local * (values * scale - back))

    sums = by_rows(own.shape[0], body, zeros_acc(own.shape[1]))
    send_stats(message.at[0], column_sum(sums[0]), column_sum(sums[1]))
    repeat_first(message)
    own_q[...] = grad[:, lane_block(b)].astype(BF)
    near_q[...] = grad[:, lane_block(b ^ 1)].astype(BF)
    far_q[0] = grad[:, lane_block(b ^ 2)].astype(BF)
    far_q[1] = grad[:, lane_block(b ^ 3)].astype(BF)


def middle_backward(grad, pre, parts, params, coef, mask, first_pre, first_coef, to_canvas, to_rows,
                    w0, w1, w2, w3, grad_first, message,
                    grad_pre, weight, gathered, canvas):
    n = position()[0]
    rows, places = grad.shape[0], to_canvas.shape[0]
    img = places // (SIDE * PITCH)
    margin = img * (PITCH + 1)
    block = sum_parts(parts)
    mean, scale, slope = (coef[k : k + 1, :] for k in range(3))
    inverse = inverse_count(params, n, grad.shape[1])
    level = wide_row(block, 0) * inverse
    tilt = wide_row(block, NARROW) * inverse
    level, tilt = level - mean * scale * tilt, scale * tilt

    def body(ds, carry):
        away = mask[n, ds, :] * (level + pre[ds, :].astype(F32) * tilt)
        grad_pre[ds, :] = (slope * (grad[ds, :] - away)).astype(BF)
        return carry

    by_rows(rows, body, 0)
    for j, piece in enumerate((w0, w1, w2, w3)):
        for tap in range(TAPS):
            weight[tap, :, lane_block(n ^ j)] = piece[:, 128 * tap : 128 * tap + 128]
    canvas[...] = dot(to_canvas[...], grad_pre[...]).astype(BF).astype(F32)
    gathered[...] = jnp.zeros_like(gathered)
    for tap in range(TAPS):
        start = margin + ((tap // 3 - 1) * PITCH + tap % 3 - 1) * img
        gathered[start : start + places, :] += dot_nt(canvas[...].astype(BF), weight[tap])
    canvas[...] = gathered[margin : margin + places, :]
    grad_pre[...] = dot(to_rows[...], canvas[...].astype(BF)).astype(BF)
    mean, scale, slope, offset = (first_coef[0, k : k + 1, :] for k in range(4))
    back = mean * scale

    def finish(ds, acc):
        values = first_pre[ds, :].astype(F32)
        act = values * slope + offset
        gate = sigmoid(act)
        local = grad_pre[ds, :].astype(F32) * mask[n, ds, :] * (gate * (1.0 + act * (1.0 - gate)))
        grad_first[ds, :] = local.astype(BF)
        return acc[0] + fold(local), acc[1] + fold(local * (values * scale - back))

    sums2 = by_rows(rows, finish, zeros_acc(grad.shape[1]))
    send_stats(message, column_sum(sums2[0]), column_sum(sums2[1]))


def first_weight(g0, g1, g2, g3, p0, p1, p2, p3, sum0, sum1, sum2, sum3, params, coef, mask, x,
                 level_sum, tilt_sum, grad_pre, *refs):
    outs, acc = refs[:-1], refs[-1]
    n, z, y = position()
    rows, channels = g0.shape
    blocks = (sum0[...], sum1[...], sum2[...], sum3[...])
    every = blocks[0] + blocks[1] + blocks[2] + blocks[3]
    for m, (g, pre) in enumerate(((g0, p0), (g1, p1), (g2, p2), (g3, p3))):
        b = n ^ m
        block = blocks[m]
        mean, scale, slope = (coef[m, k : k + 1, :] for k in range(3))
        inverse = inverse_count(params, b, channels)
        level = wide_row(block, 0) * inverse
        tilt = wide_row(block, NARROW) * inverse
        level, tilt = level - mean * scale * tilt, scale * tilt
        away = mask[b] * (level + pre[...].astype(F32) * tilt)
        grad_pre[m] = (slope * (g[...].astype(F32) - away)).astype(BF)
    total = dot_tn(x[n], grad_pre[0])
    for m in range(1, NARROW):
        total = total + dot_tn(x[n ^ m], grad_pre[m])
    acc[...] = total
    if len(outs) == 1:
        outs[0][...] = acc[...]
    else:
        half = acc.shape[0] // 2
        for ref, h in zip(outs, (y, 1 - y)):
            top = pl.multiple_of(h * half, half)
            for j in range(NARROW):
                block = acc[pl.ds(top, half), lane_block((z - j) & 3)]
                ref[:, 128 * j : 128 * j + 128] = block.astype(ref.dtype)
    level_sum[...] = row_of(every, 0, n)
    tilt_sum[...] = row_of(every, NARROW, n)


def input_gradient(grad_pre, weight, grad, out):
    n = position()[0]
    for m in range(NARROW):
        out[n ^ m] = dot_nt(grad_pre[m], weight[...]) + grad[m]


def last_weight(hidden, grad_pre, *refs):
    acc = refs[-1]
    for m in range(NARROW):
        product = dot_tn(hidden[m], grad_pre[m])
        if m == 0:
            acc[...] = product
        else:
            acc[...] += product
    hand_out(acc, refs[:-1])


def hand_out(acc, outs):
    if len(outs) == 1:
        outs[0][...] = acc[...]
        return
    _, z, y = position()
    own, away = outs
    rows = acc.shape[0] // 8
    for j in range(4):
        place = pl.ds(j * rows, rows)
        for ref, dy in ((own, 0), (away, 1)):
            top = ((z ^ j) * 2 + (y ^ dy)) * rows
            ref[place, :] = acc[pl.ds(pl.multiple_of(top, rows), rows), :].astype(ref.dtype)


def middle_weight(hidden, q0, q1, far, last, pre, sum0, sum1, sum2, sum3, norm, params, mask, to_canvas,
                  level_sum, tilt_sum, *refs):
    outs, (acc, shifted, canvases) = refs[:-3], refs[-3:]
    n = position()[0]
    places = to_canvas.shape[0]
    img = places // (SIDE * PITCH)
    margin = img * (PITCH + 1)
    norms = total_of(norm, n)
    blocks = (sum0[...], sum1[...], sum2[...], sum3[...])
    every = blocks[0] + blocks[1] + blocks[2] + blocks[3]
    level_sum[...] = row_of(every, 0, n)
    tilt_sum[...] = row_of(every, NARROW, n)
    for m, piece in enumerate((q0[...], q1[...], far[0], last[1])):
        b = n ^ m
        inverse = inverse_count(params, b, 128)
        mean, scale, slope, _ = coefficients(
            norms[2 * m : 2 * m + 1], norms[2 * m + 1 : 2 * m + 2], inverse, params[n, 2:3, :], params[n, 3:4, :]
        )
        block = blocks[m]
        level = row_of(block, 0, n) * inverse
        tilt = row_of(block, NARROW, n) * inverse
        level, tilt = level - mean * scale * tilt, scale * tilt
        away = mask[b] * (level + pre[m].astype(F32) * tilt)
        grad_pre = (slope * (piece.astype(F32) - away)).astype(BF)
        canvas = canvases.at[m]
        canvas[0:margin, :] = jnp.zeros((margin, 128), F32)
        canvas[margin + places :, :] = jnp.zeros((margin, 128), F32)
        canvas[margin : margin + places, :] = dot(to_canvas[...], grad_pre)
        for tap in range(TAPS):
            start = margin - ((tap // 3 - 1) * PITCH + tap % 3 - 1) * img
            here = slice(m * places, (m + 1) * places)
            shifted[here, 128 * tap : 128 * tap + 128] = canvas[start : start + places, :].astype(BF)
    acc[...] = dot_tn(hidden[...].reshape(NARROW * places, hidden.shape[2]), shifted[...])
    hand_out(acc, outs)


def gather_middle(near, far, out):
    _, z, y = position()
    rows = out.shape[0] // 8
    for dy, stack in enumerate((near, far)):
        for j in range(4):
            here = pl.ds(pl.multiple_of(((z ^ j) * 2 + (y ^ dy)) * rows, rows), rows)
            for tap in range(TAPS):
                top = (j * TAPS + tap) * rows
                out[here, 128 * tap : 128 * tap + 128] = stack[top : top + rows, :]


def gather_last(near, far, out):
    _, z, y = position()
    rows = out.shape[0] // 8
    for dy, stack in enumerate((near, far)):
        for j in range(4):
            here = pl.ds(pl.multiple_of(((z ^ j) * 2 + (y ^ dy)) * rows, rows), rows)
            out[here, :] = stack[j * rows : (j + 1) * rows, :]


def merge_first(own, away, *sends):
    for j, send in enumerate(sends):
        here = slice(128 * j, 128 * j + 128)
        send[...] = (own[:, here] + away[:, here].astype(F32)).astype(BF)


def add_tiles(*refs):
    total = refs[0][...]
    for ref in refs[1:-1]:
        total = total + ref[...]
    refs[-1][...] = total


def add_parts(parts, out):
    out[...] = sum_parts(parts)


def merge_wide(own, away, own_last, away_last, keep, keep_last, *sends):
    rows, middle = keep.shape
    keep[...] = own[0:rows, :] + away[0:rows, :].astype(F32)
    keep_last[...] = own_last[0:rows, :] + away_last[0:rows, :].astype(F32)
    for j, send in enumerate(sends):
        here = slice((j + 1) * rows, (j + 2) * rows)
        send[:, 0:middle] = (own[here, :] + away[here, :].astype(F32)).astype(BF)
        send[:, middle:] = (own_last[here, :] + away_last[here, :].astype(F32)).astype(BF)


def finish_wide(keep, keep_last, p1, p2, p3, out, out_last):
    middle = keep.shape[1]
    for tap in range(TAPS):
        here = slice(128 * tap, 128 * tap + 128)
        out[tap] = keep[:, here] + p1[:, here].astype(F32) + p2[:, here].astype(F32) + p3[:, here].astype(F32)
    out_last[...] = (
        keep_last[...] + p1[:, middle:].astype(F32) + p2[:, middle:].astype(F32) + p3[:, middle:].astype(F32)
    )


def exchange(message):
    return lax.all_to_all(message, ("wide", "narrow"), 0, 0, tiled=True)


def swap_core(values):
    return lax.ppermute(values, "narrow", [(i, i ^ 1) for i in range(NARROW)])


def swap_chip(values):
    return lax.ppermute(values, "narrow", [(i, i ^ 2) for i in range(NARROW)])


def swap_wide(values, step, wide):
    return lax.ppermute(values, "wide", [(i, i ^ step) for i in range(wide)])


def after(value, *others):
    return lax.optimization_barrier((value, *others))[0]


def from_all(values, *others):
    far = swap_chip(values)
    if others:
        return values, swap_core(after(values, *others)), far, swap_core(after(far, *others))
    return values, swap_core(values), far, swap_core(far)


def add(*tiles):
    return run(add_tiles, tiles, [arr(tiles[0].shape, F32)])[0]


def sum_wide(values, wide, beside=(), late=()):
    if wide == 8:
        values = add(after(values, *beside) if beside else values, swap_wide(values, 1, wide))
        parts = [swap_wide(values, step, wide) for step in (2, 4, 6)]
        total = add(after(values, *late) if late else values, *parts)
        return values, total
    step = 1
    while step < wide:
        values = add(values, swap_wide(values, step, wide))
        step *= 2
    return values, values


def reduce_narrow(send_far, own_far, send_near, own_near, *others):
    got_far = swap_core(send_far)
    got_near = swap_core(send_near)
    joined = (own_far + got_far.astype(F32)).astype(BF)
    if others:
        joined = after(joined, *others)
    return (own_near, got_near, swap_chip(joined)), joined


def transposed_steps():
    steps = []
    for j in range(NARROW):
        pairs = []
        for k in range(NARROW):
            for z in range(4):
                for y in range(2):
                    pairs.append((k * 8 + 2 * z + y, z * 8 + 2 * ((k + j) % 4) + y))
        steps.append(pairs)
    return steps


def on_device(inputs, sides, w_first, w_middle, w_last, gain_first, shift_first, gain_middle, shift_middle,
              gain_last, shift_last, cotangent, *, wide):
    micro, rows, low = inputs.shape
    img = sides.shape[1]
    mid = w_last.shape[0] * wide
    cols = w_first.shape[1]
    places = img * SIDE * PITCH
    direct = wide == 8
    n = lax.axis_index("narrow")
    w = lax.axis_index("wide")

    spots = jnp.arange(rows, dtype=jnp.int32)
    spot_y, spot_x, spot_img = spots % 49 // 7, spots % 7, spots // 49

    def mask_of(limits):
        limits = jnp.repeat(limits, 49, axis=1)
        return ((spot_y[None] < limits) & (spot_x[None] < limits)).astype(F32)[:, :, None]

    place = (spot_y * PITCH + spot_x) * img + spot_img
    to_canvas = (jnp.arange(places, dtype=jnp.int32)[:, None] == place[None, :]).astype(BF)
    to_rows = (place[:, None] == jnp.arange(places, dtype=jnp.int32)[None, :]).astype(BF)

    if direct:
        steps = transposed_steps()
        share = w_last.shape[0]
        packed = w_middle.reshape(TAPS * share, 128)
        middle_near = [packed] + [swap_wide(packed, 2 * j, wide) for j in range(1, 4)]
        first_pieces = [lax.ppermute(w_first, MESH, pairs) for pairs in steps]
        first_half = run(place_columns, first_pieces, [arr((w_first.shape[0], mid), BF)])[0]
        first_pieces = [first_half, swap_wide(first_half, 1, wide)]
    else:
        first_all = lax.all_gather(lax.all_gather(w_first, "narrow", axis=1, tiled=True), "wide", axis=0, tiled=True)
        first_pieces = [lax.dynamic_slice_in_dim(first_all, n * low, low, 0)]
        middle_slice = lax.all_gather(w_middle, "wide", axis=2, tiled=True)
        middle_slice = middle_slice.reshape(TAPS, mid, 128).transpose(1, 0, 2).reshape(mid, TAPS * 128)
        last_slice = lax.all_gather(w_last, "wide", axis=0, tiled=True)

    counts = jnp.sum((sides * sides).astype(F32), axis=1)
    small = jnp.concatenate(
        [jnp.stack([gain_first, shift_first, gain_middle, shift_middle]) * (1.0 / wide),
         jnp.broadcast_to(counts[:, None], (micro, 128))], axis=0
    )

    tile = arr((8, 128), F32)
    across = arr((wide, 8, low), F32)
    flat = arr((rows, mid), BF)
    flat32 = arr((rows, mid), F32)

    w_rows, send_far, own_far, send_near, own_near = run(
        first_product, (inputs, *first_pieces),
        [arr((low, mid), BF), flat, flat32, flat, flat32], flops=2 * micro * rows * low * mid,
    )
    joined, begun = reduce_narrow(send_far, own_far, send_near, own_near, *(middle_near[:2] if direct else ()))
    if direct:
        middle_near = jnp.concatenate([after(middle_near[0], begun)] + middle_near[1:], axis=0)
        middle_far = swap_wide(middle_near, 1, wide)
    mask = mask_of(after(sides, begun))
    beside = ()
    if direct:
        held = after(w_last, middle_near)
        last_near = jnp.concatenate([held] + [swap_wide(held, 2 * j, wide) for j in range(1, 4)], axis=0)
        beside = (middle_far, last_near)
    pre_one, message = run(first_join, (*joined, mask, small), [flat, arr((16, 128), F32)])
    begun, total = sum_wide(message, wide, beside=beside)
    if direct:
        last_far = swap_wide(after(last_near, begun), 1, wide)
    pre_ones = from_all(pre_one, total)
    sums_one = from_all(total)
    if direct:
        middle_slice = run(gather_middle, (middle_near, middle_far), [arr((mid, TAPS * 128), BF)])[0]
        middle_slice = after(middle_slice, last_far)

    hidden_one, pre_two, coef_one, message, params = run(
        middle_forward, (*pre_ones, *sums_one, mask, to_canvas, to_rows, middle_slice),
        [arr((micro, places, mid), BF), arr((micro, rows, 128), BF), arr((micro, 8, mid), F32), arr((wide * NARROW, 8, 128), F32), arr((NARROW, 8, 128), F32)],
        [pltpu.VMEM((rows, mid), BF), pltpu.VMEM((places + 2 * img * (PITCH + 1), TAPS * 128), F32), pltpu.VMEM((places, 128), BF)],
        flops=2 * micro * places * mid * TAPS * 128,
    )
    if direct:
        last_slice = run(gather_last, (last_near, last_far), [arr((mid, low), BF)])[0]
    parts_two = exchange(message)
    pre_twos = from_all(pre_two, parts_two)
    held = after(middle_slice, pre_twos[3], parts_two)
    middle_away = swap_chip(held)

    hidden_two, own_two, coef_two, pre_three, message = run(
        last_forward, (*pre_twos, parts_two, params, mask, last_slice),
        [arr((micro, rows, mid), BF), flat, arr((8, mid), F32), arr((micro, rows, low), F32), across],
        flops=2 * micro * rows * low * mid,
    )
    parts_three = lax.all_to_all(message, "wide", 0, 0, tiled=True)
    block_out, grad_sum, coef_three, message = run(
        block_output,
        (pre_three, inputs, cotangent, parts_three, params, gain_last[None], shift_last[None], mask),
        [arr(inputs.shape, BF), arr((micro, rows, low), F32), arr((micro, 8, low), F32), across],
    )
    parts_four = lax.all_to_all(message, "wide", 0, 0, tiled=True)

    grad_three, send_far, own_far, send_near, own_near, level_three, tilt_three = run(
        last_backward, (pre_three, grad_sum, parts_four, params, coef_three, mask, last_slice),
        [arr((micro, rows, low), BF), flat, flat32, flat, flat32, arr((1, low), F32), arr((1, low), F32)],
        flops=2 * micro * rows * low * mid,
    )
    joined, begun = reduce_narrow(send_far, own_far, send_near, own_near, middle_away)
    grad_three = after(grad_three, begun)

    def handed(channels):
        if direct:
            return [arr((mid // 2, channels), F32), arr((mid // 2, channels), BF)]
        return [arr((mid, channels), F32)]

    last_sum = run(
        last_weight, (hidden_two, grad_three), handed(low), [pltpu.VMEM((mid, low), F32)],
        flops=2 * micro * rows * low * mid,
    )
    slim = arr((rows, 128), BF)
    row = arr((1, 128), F32)
    if direct:
        got_last_sum = swap_wide(last_sum[1], 1, wide)
        joined = (after(joined[0], got_last_sum), *joined[1:])
    grad_two, own_q, near_q, far_q, message = run(
        middle_join, (*joined, own_two, coef_two, mask), [flat32, slim, slim, arr((2, rows, 128), BF), arr((wide, 8, 128), F32)]
    )
    got_far = swap_chip(far_q)
    middle_slices = (middle_slice, swap_core(held), middle_away, swap_core(middle_away))
    parts_five = lax.all_to_all(after(message, *middle_slices), "wide", 0, 0, tiled=True)
    total_five = run(add_parts, (parts_five,), [tile])[0]
    near_q, got_far = lax.optimization_barrier((near_q, got_far, parts_five))[:2]
    got_near, got_last = swap_core(near_q), swap_core(got_far)
    sums_five = from_all(total_five)

    grad_one, message = run(
        middle_backward,
        (grad_two, own_two, parts_five, params, coef_two, mask, pre_one, coef_one, to_canvas, to_rows, *middle_slices),
        [flat, tile],
        [pltpu.VMEM((rows, mid), BF), pltpu.VMEM((TAPS, mid, mid), BF),
         pltpu.VMEM((places + 2 * img * (PITCH + 1), mid), F32), pltpu.VMEM((places, mid), F32)],
        flops=2 * places * mid * TAPS * mid,
    )
    level_two, tilt_two, *middle_sum = run(
        middle_weight,
        (hidden_one, own_q, got_near, got_far, got_last, pre_two, *sums_five, parts_two, params, mask, to_canvas),
        [row, row, *handed(TAPS * 128)],
        [pltpu.VMEM((mid, TAPS * 128), F32), pltpu.VMEM((micro * places, TAPS * 128), BF),
         pltpu.VMEM((micro, places + 2 * img * (PITCH + 1), 128), F32)],
        flops=2 * micro * places * mid * TAPS * 128,
    )
    begun, total = sum_wide(message, wide, beside=middle_sum)
    grad_ones = from_all(after(grad_one, sums_five[2]), total)
    sums_six = from_all(total)
    if direct:
        got_middle = swap_wide(after(middle_sum[1], begun), 1, wide)

    out_first = [arr((low // 2, mid), F32), arr((low // 2, mid), BF)] if direct else [arr((low, mid), F32)]
    level_one, tilt_one, grad_pre_one, *first_sum = run(
        first_weight,
        (*grad_ones, *pre_ones, *sums_six, after(params, got_middle) if direct else params, coef_one, mask, inputs),
        [row, row, arr((micro, rows, mid), BF), *out_first], [pltpu.VMEM((low, mid), F32)],
        flops=2 * micro * rows * low * mid,
    )
    input_grad = run(
        input_gradient, (grad_pre_one, w_rows, grad_sum), [arr((micro, rows, low), F32)],
        flops=2 * micro * rows * low * mid,
    )[0]

    if direct:
        got_first = swap_wide(first_sum[1], 1, wide)
        channels = TAPS * 128
        keep, keep_last, *sends = run(
            merge_wide, (middle_sum[0], after(got_middle, first_sum[1]), last_sum[0], got_last_sum),
            [arr((share, channels), F32), arr((share, low), F32)] + [arr((share, channels + low), BF)] * 3,
        )
        parts = [swap_wide(send, 2 * j + 2, wide) for j, send in enumerate(sends)]
        sends = run(merge_first, (first_sum[0], after(got_first, *parts[0:2])), [arr((low // 2, cols), BF)] * NARROW)
        arrived = [
            lax.ppermute(send, MESH, [(dst, src) for src, dst in pairs]) for send, pairs in zip(sends, steps)
        ]
        grad_middle, grad_last = run(
            finish_wide, (after(keep, arrived[0]), keep_last, *parts),
            [arr((TAPS, share, 128), F32), arr((share, low), F32)],
        )
        grad_middle = grad_middle.reshape(3, 3, share, 128)
        grad_first = arrived[0].astype(F32)
        for piece in arrived[1:]:
            grad_first = grad_first + piece.astype(F32)
    else:
        grad_last = lax.psum_scatter(last_sum[0], "wide", scatter_dimension=0, tiled=True)
        grad_middle = lax.psum_scatter(middle_sum[0], "wide", scatter_dimension=0, tiled=True)
        share = grad_middle.shape[0]
        grad_middle = grad_middle.reshape(share, TAPS, 128).transpose(1, 0, 2).reshape(3, 3, share, 128)
        whole = lax.psum(first_sum[0], "wide")
        whole = lax.all_gather(whole, "narrow", axis=0, tiled=True)
        share = whole.shape[0] // wide
        grad_first = lax.dynamic_slice(whole, (w * share, n * cols), (share, cols))
    return (
        block_out, input_grad, grad_first, grad_middle, grad_last,
        tilt_one[0], level_one[0], tilt_two[0], level_two[0], tilt_three[0], level_three[0],
    )


def solution(mesh):
    wide = mesh.shape["wide"]
    placed = (
        P(None, "wide", "narrow"),
        P(None, "wide"),
        P("wide", "narrow"),
        P(None, None, "wide", "narrow"),
        P("wide", "narrow"),
        P("narrow"),
        P("narrow"),
        P("narrow"),
        P("narrow"),
        P("narrow"),
        P("narrow"),
        P(None, "wide", "narrow"),
    )
    return jax.shard_map(
        lambda *arrays: on_device(*arrays, wide=wide),
        mesh=mesh,
        in_specs=placed,
        out_specs=(
            P(None, "wide", "narrow"),
            P(None, "wide", "narrow"),
            P("wide", "narrow"),
            P(None, None, "wide", "narrow"),
            P("wide", "narrow"),
            P("narrow"),
            P("narrow"),
            P("narrow"),
            P("narrow"),
            P("narrow"),
            P("narrow"),
        ),
        check_vma=False,
    )
```

```python
import jax
import jax.numpy as jnp
from jax import lax
from jax.experimental import pallas as pl
from jax.experimental.pallas import tpu as pltpu
from jax.sharding import PartitionSpec as P


F32 = jnp.float32
BF = jnp.bfloat16
EPS = 1e-05
SIDE = 7
PITCH = 8
TAPS = 9
NARROW = 4
MESH = ("narrow", "wide")
VMEM_BYTES = 20 * 2**20


def dot(left, right):
    return jnp.dot(left, right, preferred_element_type=F32)


def dot_nt(left, right):
    return lax.dot_general(left, right, (((1,), (1,)), ((), ())), preferred_element_type=F32)


def dot_tn(left, right):
    return lax.dot_general(left, right, (((0,), (0,)), ((), ())), preferred_element_type=F32)


def position():
    n, w = lax.axis_index("narrow"), lax.axis_index("wide")
    return n, w // 2, w % 2


def run(kernel, operands, outs, scratch=(), flops=0):
    moved = sum(o.size * o.dtype.itemsize for o in (*operands, *outs))
    return pl.pallas_call(
        kernel,
        out_shape=outs,
        name=kernel.__name__,
        in_specs=[pl.BlockSpec(memory_space=pltpu.VMEM)] * len(operands),
        out_specs=[pl.BlockSpec(memory_space=pltpu.VMEM)] * len(outs),
        scratch_shapes=list(scratch),
        cost_estimate=pl.CostEstimate(flops=flops, bytes_accessed=moved, transcendentals=0),
        compiler_params=pltpu.CompilerParams(vmem_limit_bytes=VMEM_BYTES),
    )(*operands)


def arr(shape, dtype):
    return jax.ShapeDtypeStruct(shape, dtype)


def by_rows(rows, body, carry):
    return body(pl.ds(0, rows), carry)


def fold(values):
    total = values[0:8]
    for start in range(8, values.shape[0], 8):
        total = total + values[start : start + 8]
    return total


def zeros_acc(channels):
    return (jnp.zeros((8, channels), F32), jnp.zeros((8, channels), F32))


def column_sum(acc):
    return jnp.sum(acc, axis=0, keepdims=True)


def sigmoid(values):
    return 0.5 * jnp.tanh(0.5 * values) + 0.5


def coefficients(total, squares, inverse, gain, shift):
    mean = total * inverse
    spread = squares * inverse - mean * mean
    scale = lax.rsqrt(spread + EPS)
    slope = gain * scale
    return mean, scale, slope, shift - mean * slope


def wide_row(block, first, count=NARROW):
    return jnp.concatenate([block[first + k : first + k + 1] for k in range(count)], axis=1)


def row_of(block, first, index):
    rows = [jnp.where(index == k, block[first + k : first + k + 1], 0.0) for k in range(NARROW)]
    return rows[0] + rows[1] + rows[2] + rows[3]


def inverse_count(params, b, channels):
    row = params[b, 4:5, :]
    return row if channels == 128 else jnp.concatenate([row] * (channels // 128), axis=1)


def lane_block(index):
    return pl.ds(pl.multiple_of(index * 128, 128), 128)


def send_stats(message, first, second):
    for k in range(NARROW):
        message[k : k + 1, :] = first[:, 128 * k : 128 * k + 128]
        message[NARROW + k : NARROW + k + 1, :] = second[:, 128 * k : 128 * k + 128]


def repeat_first(message):
    block = message[0]
    for place in range(1, message.shape[0]):
        message[place] = block


def total_of(parts, index):
    total = parts[index]
    for place in range(NARROW, parts.shape[0], NARROW):
        total = total + parts[place + index]
    return total


def sum_parts(parts):
    total = parts[0]
    for place in range(1, parts.shape[0]):
        total = total + parts[place]
    return total


def place_columns(p0, p1, p2, p3, out):
    z = position()[1]
    for j, piece in enumerate((p0, p1, p2, p3)):
        out[:, lane_block((z - j) & 3)] = piece[...]


def first_product(x, *refs):
    pieces, (w_first, send_far, own_far, send_near, own_near) = refs[:-5], refs[-5:]
    n, z, y = position()
    if len(pieces) == 1:
        w_first[...] = pieces[0][...]
    else:
        rows = pieces[0].shape[0]
        for dy, piece in enumerate(pieces):
            w_first[pl.ds(pl.multiple_of((y ^ dy) * rows, rows), rows), :] = piece[...]
    for ref, m in ((send_far, 3), (own_far, 2), (send_near, 1), (own_near, 0)):
        ref[...] = dot(x[n ^ m], w_first[...]).astype(ref.dtype)


def first_join(own, near, far, mask, small, pre, message):
    b = position()[0]

    def body(ds, acc):
        values = own[ds, :] + near[ds, :].astype(F32) + far[ds, :].astype(F32)
        pre[ds, :] = values.astype(BF)
        kept = mask[b, ds, :] * values
        return acc[0] + fold(kept), acc[1] + fold(kept * values)

    sums = by_rows(own.shape[0], body, zeros_acc(own.shape[1]))
    send_stats(message, column_sum(sums[0]), column_sum(sums[1]))
    message[8:16, :] = small[...]


def middle_forward(pre0, pre1, pre2, pre3, sum0, sum1, sum2, sum3, mask, to_canvas, to_rows, weight,
                   hidden, pre, coef, message, params, active, spread, joined):
    n = position()[0]
    blocks = (sum0[...], sum1[...], sum2[...], sum3[...])
    for m, block in enumerate(blocks):
        params[n ^ m, 0:4, :] = block[8:12]
    for b in range(NARROW):
        params[b, 4:5, :] = 1.0 / blocks[0][12 + b : 13 + b]
        params[b, 5:8, :] = jnp.zeros((3, 128), F32)
    rows, places = pre0.shape[0], to_canvas.shape[0]
    img = places // (SIDE * PITCH)
    margin = img * (PITCH + 1)
    gain = jnp.concatenate([params[k, 0:1, :] for k in range(NARROW)], axis=1)
    shift = jnp.concatenate([params[k, 1:2, :] for k in range(NARROW)], axis=1)
    spread[0:margin, :] = jnp.zeros((margin, spread.shape[1]), F32)
    spread[margin + places :, :] = jnp.zeros((margin, spread.shape[1]), F32)
    line = img * PITCH
    for m, source in enumerate((pre0, pre1, pre2, pre3)):
        b = n ^ m
        block = blocks[m]
        mean, scale, slope, offset = coefficients(
            wide_row(block, 0), wide_row(block, NARROW), inverse_count(params, b, gain.shape[1]), gain, shift
        )
        for k, row in enumerate((mean, scale, slope, offset)):
            coef[m, k : k + 1, :] = row

        def activate(ds, carry):
            act = source[ds, :].astype(F32) * slope + offset
            active[ds, :] = (mask[b, ds, :] * act * sigmoid(act)).astype(BF)
            return carry

        by_rows(rows, activate, 0)
        hidden[m] = dot(to_canvas[...], active[...]).astype(BF)
        spread[margin : margin + places, :] = dot(hidden[m], weight[...])
        for top in range(SIDE):
            acc = None
            for tap in range(TAPS):
                start = margin + top * line + ((tap // 3 - 1) * PITCH + tap % 3 - 1) * img
                part = spread[start : start + line, 128 * tap : 128 * tap + 128]
                acc = part if acc is None else acc + part
            joined[top * line : (top + 1) * line, :] = acc.astype(BF)
        pre[m] = dot(to_rows[...], joined[...]).astype(BF)

        def collect(ds, acc):
            values = pre[m, ds, :].astype(F32)
            kept = mask[b, ds, :] * values
            return acc[0] + fold(kept), acc[1] + fold(kept * values)

        sums = by_rows(rows, collect, zeros_acc(128))
        message[0, 2 * m : 2 * m + 1, :] = column_sum(sums[0])
        message[0, 2 * m + 1 : 2 * m + 2, :] = column_sum(sums[1])
    repeat_first(message)


def last_forward(src0, src1, src2, src3, parts, params, mask, weight,
                 hidden, own, coef, pre, message):
    n = position()[0]
    rows = own.shape[0]
    sources = (src0, src1, src2, src3)
    blocks = [total_of(parts, n ^ i) for i in range(NARROW)]
    for m in range(NARROW):
        b = n ^ m
        for i in range(NARROW):
            j = m ^ i
            here = lane_block(n ^ i)
            mean, scale, slope, offset = coefficients(
                blocks[i][2 * j : 2 * j + 1], blocks[i][2 * j + 1 : 2 * j + 2], inverse_count(params, b, 128),
                params[n ^ i, 2:3, :], params[n ^ i, 3:4, :],
            )
            if m == 0:
                own[:, here] = sources[i][j]
                for k, row in enumerate((mean, scale, slope, offset)):
                    coef[k : k + 1, here] = row

            def activate(ds, carry):
                act = sources[i][j, ds, :].astype(F32) * slope + offset
                hidden[m, ds, here] = (mask[b, ds, :] * act * sigmoid(act)).astype(BF)
                return carry

            by_rows(rows, activate, 0)
        pre[m] = dot(hidden[m], weight[...])

        def collect(ds, acc):
            values = pre[m, ds, :]
            kept = mask[b, ds, :] * values
            return acc[0] + fold(kept), acc[1] + fold(kept * values)

        sums = by_rows(rows, collect, zeros_acc(pre.shape[2]))
        message[0, 2 * m : 2 * m + 1, :] = column_sum(sums[0])
        message[0, 2 * m + 1 : 2 * m + 2, :] = column_sum(sums[1])
    repeat_first(message)


def block_output(pre, x, cotangent, parts, params, gain, shift, mask, out, grad, coef, message):
    n = position()[0]
    rows, channels = pre.shape[1:]
    block = sum_parts(parts)
    for m in range(NARROW):
        b = n ^ m
        mean, scale, slope, offset = coefficients(
            block[2 * m : 2 * m + 1], block[2 * m + 1 : 2 * m + 2], inverse_count(params, b, channels), gain[...], shift[...]
        )
        for k, row in enumerate((mean, scale, slope, offset)):
            coef[m, k : k + 1, :] = row

        def body(ds, acc):
            values = pre[m, ds, :]
            inside = mask[b, ds, :]
            summed = values * slope + offset + x[b, ds, :].astype(F32)
            gate = sigmoid(summed)
            value = summed * gate
            out[b, ds, :] = (inside * value).astype(BF)
            local = inside * cotangent[b, ds, :].astype(F32) * (gate + value * (1.0 - gate))
            grad[m, ds, :] = local
            return acc[0] + fold(local), acc[1] + fold(local * values)

        sums = by_rows(rows, body, zeros_acc(channels))
        first, second = column_sum(sums[0]), column_sum(sums[1])
        message[0, 2 * m : 2 * m + 1, :] = first
        message[0, 2 * m + 1 : 2 * m + 2, :] = scale * (second - mean * first)
    repeat_first(message)


def last_backward(pre, grad, parts, params, coef, mask, weight,
                  grad_pre, send_far, own_far, send_near, own_near, level_sum, tilt_sum):
    n = position()[0]
    rows = pre.shape[1]
    block = sum_parts(parts)
    for s, ref in enumerate((level_sum, tilt_sum)):
        acc = block[s : s + 1]
        for m in range(1, NARROW):
            acc = acc + block[2 * m + s : 2 * m + s + 1]
        ref[...] = acc
    for m, ref in ((3, send_far), (2, own_far), (1, send_near), (0, own_near)):
        b = n ^ m
        mean, scale, slope = (coef[m, k : k + 1, :] for k in range(3))
        inverse = inverse_count(params, b, block.shape[1])
        level = block[2 * m : 2 * m + 1] * inverse
        tilt = block[2 * m + 1 : 2 * m + 2] * inverse
        level, tilt = level - mean * scale * tilt, scale * tilt

        def body(ds, carry):
            away = mask[b, ds, :] * (level + pre[m, ds, :] * tilt)
            grad_pre[m, ds, :] = (slope * (grad[m, ds, :] - away)).astype(BF)
            return carry

        by_rows(rows, body, 0)
        ref[...] = dot_nt(grad_pre[m], weight[...]).astype(ref.dtype)


def middle_join(own, near, far, pre, coef, mask, grad, own_q, near_q, far_q, message):
    b = position()[0]
    mean, scale, slope, offset = (coef[k : k + 1, :] for k in range(4))
    back = mean * scale

    def body(ds, acc):
        values = pre[ds, :].astype(F32)
        act = values * slope + offset
        gate = sigmoid(act)
        total = own[ds, :] + near[ds, :].astype(F32) + far[ds, :].astype(F32)
        local = total * mask[b, ds, :] * (gate * (1.0 + act * (1.0 - gate)))
        grad[ds, :] = local
        return acc[0] + fold(local), acc[1] + fold(local * (values * scale - back))

    sums = by_rows(own.shape[0], body, zeros_acc(own.shape[1]))
    send_stats(message.at[0], column_sum(sums[0]), column_sum(sums[1]))
    repeat_first(message)
    own_q[...] = grad[:, lane_block(b)].astype(BF)
    near_q[...] = grad[:, lane_block(b ^ 1)].astype(BF)
    far_q[0] = grad[:, lane_block(b ^ 2)].astype(BF)
    far_q[1] = grad[:, lane_block(b ^ 3)].astype(BF)


def middle_backward(grad, pre, parts, params, coef, mask, first_pre, first_coef, to_canvas, to_rows,
                    w0, w1, w2, w3, grad_first, message,
                    grad_pre, weight, gathered, canvas):
    n = position()[0]
    rows, places = grad.shape[0], to_canvas.shape[0]
    img = places // (SIDE * PITCH)
    margin = img * (PITCH + 1)
    block = sum_parts(parts)
    mean, scale, slope = (coef[k : k + 1, :] for k in range(3))
    inverse = inverse_count(params, n, grad.shape[1])
    level = wide_row(block, 0) * inverse
    tilt = wide_row(block, NARROW) * inverse
    level, tilt = level - mean * scale * tilt, scale * tilt

    def body(ds, carry):
        away = mask[n, ds, :] * (level + pre[ds, :].astype(F32) * tilt)
        grad_pre[ds, :] = (slope * (grad[ds, :] - away)).astype(BF)
        return carry

    by_rows(rows, body, 0)
    for j, piece in enumerate((w0, w1, w2, w3)):
        for tap in range(TAPS):
            weight[tap, :, lane_block(n ^ j)] = piece[:, 128 * tap : 128 * tap + 128]
    canvas[...] = dot(to_canvas[...], grad_pre[...]).astype(BF).astype(F32)
    gathered[...] = jnp.zeros_like(gathered)
    for tap in range(TAPS):
        start = margin + ((tap // 3 - 1) * PITCH + tap % 3 - 1) * img
        gathered[start : start + places, :] += dot_nt(canvas[...].astype(BF), weight[tap])
    canvas[...] = gathered[margin : margin + places, :]
    grad_pre[...] = dot(to_rows[...], canvas[...].astype(BF)).astype(BF)
    mean, scale, slope, offset = (first_coef[0, k : k + 1, :] for k in range(4))
    back = mean * scale

    def finish(ds, acc):
        values = first_pre[ds, :].astype(F32)
        act = values * slope + offset
        gate = sigmoid(act)
        local = grad_pre[ds, :].astype(F32) * mask[n, ds, :] * (gate * (1.0 + act * (1.0 - gate)))
        grad_first[ds, :] = local.astype(BF)
        return acc[0] + fold(local), acc[1] + fold(local * (values * scale - back))

    sums2 = by_rows(rows, finish, zeros_acc(grad.shape[1]))
    send_stats(message, column_sum(sums2[0]), column_sum(sums2[1]))


def first_weight(g0, g1, g2, g3, p0, p1, p2, p3, sum0, sum1, sum2, sum3, params, coef, mask, x,
                 level_sum, tilt_sum, grad_pre, *refs):
    outs, acc = refs[:-1], refs[-1]
    n, z, y = position()
    rows, channels = g0.shape
    blocks = (sum0[...], sum1[...], sum2[...], sum3[...])
    every = blocks[0] + blocks[1] + blocks[2] + blocks[3]
    for m, (g, pre) in enumerate(((g0, p0), (g1, p1), (g2, p2), (g3, p3))):
        b = n ^ m
        block = blocks[m]
        mean, scale, slope = (coef[m, k : k + 1, :] for k in range(3))
        inverse = inverse_count(params, b, channels)
        level = wide_row(block, 0) * inverse
        tilt = wide_row(block, NARROW) * inverse
        level, tilt = level - mean * scale * tilt, scale * tilt
        away = mask[b] * (level + pre[...].astype(F32) * tilt)
        grad_pre[m] = (slope * (g[...].astype(F32) - away)).astype(BF)
    total = dot_tn(x[n], grad_pre[0])
    for m in range(1, NARROW):
        total = total + dot_tn(x[n ^ m], grad_pre[m])
    acc[...] = total
    if len(outs) == 1:
        outs[0][...] = acc[...]
    else:
        half = acc.shape[0] // 2
        for ref, h in zip(outs, (y, 1 - y)):
            top = pl.multiple_of(h * half, half)
            for j in range(NARROW):
                block = acc[pl.ds(top, half), lane_block(n ^ j)]
                ref[:, 128 * j : 128 * j + 128] = block.astype(ref.dtype)
    level_sum[...] = row_of(every, 0, n)
    tilt_sum[...] = row_of(every, NARROW, n)


def input_gradient(grad_pre, weight, grad, out):
    n = position()[0]
    for m in range(NARROW):
        out[n ^ m] = dot_nt(grad_pre[m], weight[...]) + grad[m]


def last_weight(hidden, grad_pre, *refs):
    acc = refs[-1]
    for m in range(NARROW):
        product = dot_tn(hidden[m], grad_pre[m])
        if m == 0:
            acc[...] = product
        else:
            acc[...] += product
    hand_out(acc, refs[:-1])


def hand_out(acc, outs):
    if len(outs) == 1:
        outs[0][...] = acc[...]
        return
    _, z, y = position()
    own, away = outs
    rows = acc.shape[0] // 8
    for j in range(4):
        place = pl.ds(j * rows, rows)
        for ref, dy in ((own, 0), (away, 1)):
            top = ((z ^ j) * 2 + (y ^ dy)) * rows
            ref[place, :] = acc[pl.ds(pl.multiple_of(top, rows), rows), :].astype(ref.dtype)


def middle_weight(hidden, q0, q1, far, last, pre, sum0, sum1, sum2, sum3, norm, params, mask, to_canvas,
                  level_sum, tilt_sum, *refs):
    outs, (acc, shifted, canvases) = refs[:-3], refs[-3:]
    n = position()[0]
    places = to_canvas.shape[0]
    img = places // (SIDE * PITCH)
    margin = img * (PITCH + 1)
    norms = total_of(norm, n)
    blocks = (sum0[...], sum1[...], sum2[...], sum3[...])
    every = blocks[0] + blocks[1] + blocks[2] + blocks[3]
    level_sum[...] = row_of(every, 0, n)
    tilt_sum[...] = row_of(every, NARROW, n)
    for m, piece in enumerate((q0[...], q1[...], far[0], last[1])):
        b = n ^ m
        inverse = inverse_count(params, b, 128)
        mean, scale, slope, _ = coefficients(
            norms[2 * m : 2 * m + 1], norms[2 * m + 1 : 2 * m + 2], inverse, params[n, 2:3, :], params[n, 3:4, :]
        )
        block = blocks[m]
        level = row_of(block, 0, n) * inverse
        tilt = row_of(block, NARROW, n) * inverse
        level, tilt = level - mean * scale * tilt, scale * tilt
        away = mask[b] * (level + pre[m].astype(F32) * tilt)
        grad_pre = (slope * (piece.astype(F32) - away)).astype(BF)
        canvas = canvases.at[m]
        canvas[0:margin, :] = jnp.zeros((margin, 128), F32)
        canvas[margin + places :, :] = jnp.zeros((margin, 128), F32)
        canvas[margin : margin + places, :] = dot(to_canvas[...], grad_pre)
        for tap in range(TAPS):
            start = margin - ((tap // 3 - 1) * PITCH + tap % 3 - 1) * img
            here = slice(m * places, (m + 1) * places)
            shifted[here, 128 * tap : 128 * tap + 128] = canvas[start : start + places, :].astype(BF)
    acc[...] = dot_tn(hidden[...].reshape(NARROW * places, hidden.shape[2]), shifted[...])
    hand_out(acc, outs)


def gather_middle(near, far, out):
    _, z, y = position()
    rows = out.shape[0] // 8
    for dy, stack in enumerate((near, far)):
        for j in range(4):
            here = pl.ds(pl.multiple_of(((z ^ j) * 2 + (y ^ dy)) * rows, rows), rows)
            for tap in range(TAPS):
                top = (j * TAPS + tap) * rows
                out[here, 128 * tap : 128 * tap + 128] = stack[top : top + rows, :]


def gather_last(near, far, out):
    _, z, y = position()
    rows = out.shape[0] // 8
    for dy, stack in enumerate((near, far)):
        for j in range(4):
            here = pl.ds(pl.multiple_of(((z ^ j) * 2 + (y ^ dy)) * rows, rows), rows)
            out[here, :] = stack[j * rows : (j + 1) * rows, :]


def merge_first(own, away, keep, near, far):
    parts = [own[:, 128 * i : 128 * i + 128] + away[:, 128 * i : 128 * i + 128].astype(F32) for i in range(NARROW)]
    keep[...] = parts[0]
    near[...] = parts[1].astype(BF)
    far[0] = parts[2].astype(BF)
    far[1] = parts[3].astype(BF)


def sort_first(own, near, far, last, keep, *refs):
    sends, pieces = refs[:-1], refs[-1]
    n, z, _ = position()
    for i, piece in enumerate((own[...], near[...], far[0], last[1])):
        pieces[i] = piece.astype(F32)
    keep[...] = pieces[n ^ z]
    for j, send in enumerate(sends):
        send[...] = pieces[n ^ z ^ (j + 1)].astype(BF)


def finish_first(keep, p1, p2, p3, out):
    out[...] = keep[...] + p1[...].astype(F32) + p2[...].astype(F32) + p3[...].astype(F32)


def add_tiles(*refs):
    total = refs[0][...]
    for ref in refs[1:-1]:
        total = total + ref[...]
    refs[-1][...] = total


def add_parts(parts, out):
    out[...] = sum_parts(parts)


def merge_wide(own, away, own_last, away_last, keep, keep_last, *sends):
    rows, middle = keep.shape
    keep[...] = own[0:rows, :] + away[0:rows, :].astype(F32)
    keep_last[...] = own_last[0:rows, :] + away_last[0:rows, :].astype(F32)
    for j, send in enumerate(sends):
        here = slice((j + 1) * rows, (j + 2) * rows)
        send[:, 0:middle] = (own[here, :] + away[here, :].astype(F32)).astype(BF)
        send[:, middle:] = (own_last[here, :] + away_last[here, :].astype(F32)).astype(BF)


def finish_wide(keep, keep_last, p1, p2, p3, out, out_last):
    middle = keep.shape[1]
    for tap in range(TAPS):
        here = slice(128 * tap, 128 * tap + 128)
        out[tap] = keep[:, here] + p1[:, here].astype(F32) + p2[:, here].astype(F32) + p3[:, here].astype(F32)
    out_last[...] = (
        keep_last[...] + p1[:, middle:].astype(F32) + p2[:, middle:].astype(F32) + p3[:, middle:].astype(F32)
    )


def exchange(message):
    return lax.all_to_all(message, ("wide", "narrow"), 0, 0, tiled=True)


def swap_core(values):
    return lax.ppermute(values, "narrow", [(i, i ^ 1) for i in range(NARROW)])


def swap_chip(values):
    return lax.ppermute(values, "narrow", [(i, i ^ 2) for i in range(NARROW)])


def swap_wide(values, step, wide):
    return lax.ppermute(values, "wide", [(i, i ^ step) for i in range(wide)])


def after(value, *others):
    return lax.optimization_barrier((value, *others))[0]


def from_all(values, *others):
    far = swap_chip(values)
    if others:
        return values, swap_core(after(values, *others)), far, swap_core(after(far, *others))
    return values, swap_core(values), far, swap_core(far)


def add(*tiles):
    return run(add_tiles, tiles, [arr(tiles[0].shape, F32)])[0]


def sum_wide(values, wide, beside=(), late=()):
    if wide == 8:
        values = add(after(values, *beside) if beside else values, swap_wide(values, 1, wide))
        parts = [swap_wide(values, step, wide) for step in (2, 4, 6)]
        total = add(after(values, *late) if late else values, *parts)
        return values, total
    step = 1
    while step < wide:
        values = add(values, swap_wide(values, step, wide))
        step *= 2
    return values, values


def reduce_narrow(send_far, own_far, send_near, own_near, *others):
    got_far = swap_core(send_far)
    got_near = swap_core(send_near)
    joined = (own_far + got_far.astype(F32)).astype(BF)
    if others:
        joined = after(joined, *others)
    return (own_near, got_near, swap_chip(joined)), joined


def transposed_steps():
    steps = []
    for j in range(NARROW):
        pairs = []
        for k in range(NARROW):
            for z in range(4):
                for y in range(2):
                    pairs.append((k * 8 + 2 * z + y, z * 8 + 2 * ((k + j) % 4) + y))
        steps.append(pairs)
    return steps


def on_device(inputs, sides, w_first, w_middle, w_last, gain_first, shift_first, gain_middle, shift_middle,
              gain_last, shift_last, cotangent, *, wide):
    micro, rows, low = inputs.shape
    img = sides.shape[1]
    mid = w_last.shape[0] * wide
    cols = w_first.shape[1]
    places = img * SIDE * PITCH
    direct = wide == 8
    n = lax.axis_index("narrow")
    w = lax.axis_index("wide")

    spots = jnp.arange(rows, dtype=jnp.int32)
    spot_y, spot_x, spot_img = spots % 49 // 7, spots % 7, spots // 49

    def mask_of(limits):
        limits = jnp.repeat(limits, 49, axis=1)
        return ((spot_y[None] < limits) & (spot_x[None] < limits)).astype(F32)[:, :, None]

    place = (spot_y * PITCH + spot_x) * img + spot_img
    to_canvas = (jnp.arange(places, dtype=jnp.int32)[:, None] == place[None, :]).astype(BF)
    to_rows = (place[:, None] == jnp.arange(places, dtype=jnp.int32)[None, :]).astype(BF)

    if direct:
        steps = transposed_steps()
        share = w_last.shape[0]
        packed = w_middle.reshape(TAPS * share, 128)
        middle_near = [packed] + [swap_wide(packed, 2 * j, wide) for j in range(1, 4)]
        first_pieces = [lax.ppermute(w_first, MESH, pairs) for pairs in steps]
        first_half = run(place_columns, first_pieces, [arr((w_first.shape[0], mid), BF)])[0]
        first_pieces = [first_half, swap_wide(first_half, 1, wide)]
    else:
        first_all = lax.all_gather(lax.all_gather(w_first, "narrow", axis=1, tiled=True), "wide", axis=0, tiled=True)
        first_pieces = [lax.dynamic_slice_in_dim(first_all, n * low, low, 0)]
        middle_slice = lax.all_gather(w_middle, "wide", axis=2, tiled=True)
        middle_slice = middle_slice.reshape(TAPS, mid, 128).transpose(1, 0, 2).reshape(mid, TAPS * 128)
        last_slice = lax.all_gather(w_last, "wide", axis=0, tiled=True)

    counts = jnp.sum((sides * sides).astype(F32), axis=1)
    small = jnp.concatenate(
        [jnp.stack([gain_first, shift_first, gain_middle, shift_middle]) * (1.0 / wide),
         jnp.broadcast_to(counts[:, None], (micro, 128))], axis=0
    )

    tile = arr((8, 128), F32)
    across = arr((wide, 8, low), F32)
    flat = arr((rows, mid), BF)
    flat32 = arr((rows, mid), F32)

    w_rows, send_far, own_far, send_near, own_near = run(
        first_product, (inputs, *first_pieces),
        [arr((low, mid), BF), flat, flat32, flat, flat32], flops=2 * micro * rows * low * mid,
    )
    joined, begun = reduce_narrow(send_far, own_far, send_near, own_near, *(middle_near[:2] if direct else ()))
    if direct:
        middle_near = jnp.concatenate([after(middle_near[0], begun)] + middle_near[1:], axis=0)
        middle_far = swap_wide(middle_near, 1, wide)
    mask = mask_of(after(sides, begun))
    beside = ()
    if direct:
        held = after(w_last, middle_near)
        last_near = jnp.concatenate([held] + [swap_wide(held, 2 * j, wide) for j in range(1, 4)], axis=0)
        beside = (middle_far, last_near)
    pre_one, message = run(first_join, (*joined, mask, small), [flat, arr((16, 128), F32)])
    begun, total = sum_wide(message, wide, beside=beside)
    if direct:
        last_far = swap_wide(after(last_near, begun), 1, wide)
    pre_ones = from_all(pre_one, total)
    sums_one = from_all(total)
    if direct:
        middle_slice = run(gather_middle, (middle_near, middle_far), [arr((mid, TAPS * 128), BF)])[0]
        middle_slice = after(middle_slice, last_far)

    hidden_one, pre_two, coef_one, message, params = run(
        middle_forward, (*pre_ones, *sums_one, mask, to_canvas, to_rows, middle_slice),
        [arr((micro, places, mid), BF), arr((micro, rows, 128), BF), arr((micro, 8, mid), F32), arr((wide * NARROW, 8, 128), F32), arr((NARROW, 8, 128), F32)],
        [pltpu.VMEM((rows, mid), BF), pltpu.VMEM((places + 2 * img * (PITCH + 1), TAPS * 128), F32), pltpu.VMEM((places, 128), BF)],
        flops=2 * micro * places * mid * TAPS * 128,
    )
    if direct:
        last_slice = run(gather_last, (last_near, last_far), [arr((mid, low), BF)])[0]
    parts_two = exchange(message)
    pre_twos = from_all(pre_two, parts_two)
    held = after(middle_slice, pre_twos[3], parts_two)
    middle_away = swap_chip(held)

    hidden_two, own_two, coef_two, pre_three, message = run(
        last_forward, (*pre_twos, parts_two, params, mask, last_slice),
        [arr((micro, rows, mid), BF), flat, arr((8, mid), F32), arr((micro, rows, low), F32), across],
        flops=2 * micro * rows * low * mid,
    )
    parts_three = lax.all_to_all(message, "wide", 0, 0, tiled=True)
    block_out, grad_sum, coef_three, message = run(
        block_output,
        (pre_three, inputs, cotangent, parts_three, params, gain_last[None], shift_last[None], mask),
        [arr(inputs.shape, BF), arr((micro, rows, low), F32), arr((micro, 8, low), F32), across],
    )
    parts_four = lax.all_to_all(message, "wide", 0, 0, tiled=True)

    grad_three, send_far, own_far, send_near, own_near, level_three, tilt_three = run(
        last_backward, (pre_three, grad_sum, parts_four, params, coef_three, mask, last_slice),
        [arr((micro, rows, low), BF), flat, flat32, flat, flat32, arr((1, low), F32), arr((1, low), F32)],
        flops=2 * micro * rows * low * mid,
    )
    joined, begun = reduce_narrow(send_far, own_far, send_near, own_near, middle_away)
    grad_three = after(grad_three, begun)

    def handed(channels):
        if direct:
            return [arr((mid // 2, channels), F32), arr((mid // 2, channels), BF)]
        return [arr((mid, channels), F32)]

    last_sum = run(
        last_weight, (hidden_two, grad_three), handed(low), [pltpu.VMEM((mid, low), F32)],
        flops=2 * micro * rows * low * mid,
    )
    slim = arr((rows, 128), BF)
    row = arr((1, 128), F32)
    if direct:
        got_last_sum = swap_wide(last_sum[1], 1, wide)
        joined = (after(joined[0], got_last_sum), *joined[1:])
    grad_two, own_q, near_q, far_q, message = run(
        middle_join, (*joined, own_two, coef_two, mask), [flat32, slim, slim, arr((2, rows, 128), BF), arr((wide, 8, 128), F32)]
    )
    got_far = swap_chip(far_q)
    middle_slices = (middle_slice, swap_core(held), middle_away, swap_core(middle_away))
    parts_five = lax.all_to_all(after(message, *middle_slices), "wide", 0, 0, tiled=True)
    total_five = run(add_parts, (parts_five,), [tile])[0]
    near_q, got_far = lax.optimization_barrier((near_q, got_far, parts_five))[:2]
    got_near, got_last = swap_core(near_q), swap_core(got_far)
    sums_five = from_all(total_five)

    grad_one, message = run(
        middle_backward,
        (grad_two, own_two, parts_five, params, coef_two, mask, pre_one, coef_one, to_canvas, to_rows, *middle_slices),
        [flat, tile],
        [pltpu.VMEM((rows, mid), BF), pltpu.VMEM((TAPS, mid, mid), BF),
         pltpu.VMEM((places + 2 * img * (PITCH + 1), mid), F32), pltpu.VMEM((places, mid), F32)],
        flops=2 * places * mid * TAPS * mid,
    )
    level_two, tilt_two, *middle_sum = run(
        middle_weight,
        (hidden_one, own_q, got_near, got_far, got_last, pre_two, *sums_five, parts_two, params, mask, to_canvas),
        [row, row, *handed(TAPS * 128)],
        [pltpu.VMEM((mid, TAPS * 128), F32), pltpu.VMEM((micro * places, TAPS * 128), BF),
         pltpu.VMEM((micro, places + 2 * img * (PITCH + 1), 128), F32)],
        flops=2 * micro * places * mid * TAPS * 128,
    )
    begun, total = sum_wide(message, wide, beside=middle_sum)
    grad_ones = from_all(after(grad_one, sums_five[2]), total)
    sums_six = from_all(total)
    if direct:
        got_middle = swap_wide(after(middle_sum[1], begun), 1, wide)

    out_first = [arr((low // 2, mid), F32), arr((low // 2, mid), BF)] if direct else [arr((low, mid), F32)]
    level_one, tilt_one, grad_pre_one, *first_sum = run(
        first_weight,
        (*grad_ones, *pre_ones, *sums_six, params, coef_one, mask, inputs),
        [row, row, arr((micro, rows, mid), BF), *out_first], [pltpu.VMEM((low, mid), F32)],
        flops=2 * micro * rows * low * mid,
    )
    input_grad = run(
        input_gradient, (grad_pre_one, w_rows, grad_sum), [arr((micro, rows, low), F32)],
        flops=2 * micro * rows * low * mid,
    )[0]

    if direct:
        got_first = swap_wide(after(first_sum[1], got_middle), 1, wide)
        channels = TAPS * 128
        keep, keep_last, *sends = run(
            merge_wide, (middle_sum[0], after(got_middle, first_sum[1]), last_sum[0], got_last_sum),
            [arr((share, channels), F32), arr((share, low), F32)] + [arr((share, channels + low), BF)] * 3,
        )
        parts = [swap_wide(send, 2 * j + 2, wide) for j, send in enumerate(sends)]
        piece, half = arr((low // 2, cols), BF), arr((low // 2, cols), F32)
        keep_first, near, far = run(merge_first, (first_sum[0], after(got_first, parts[0])), [half, piece, arr((2, low // 2, cols), BF)])
        far = after(swap_chip(far), *parts[0:2])
        keep_first, *sends = run(
            sort_first, (keep_first, swap_core(near), far, swap_core(far)), [half, piece, piece, piece],
            [pltpu.VMEM((NARROW, low // 2, cols), F32)],
        )
        arrived = [swap_wide(send, 2 * j + 2, wide) for j, send in enumerate(sends)]
        grad_first = run(finish_first, (keep_first, *arrived), [half])[0]
        grad_middle, grad_last = run(
            finish_wide, (keep, keep_last, *parts),
            [arr((TAPS, share, 128), F32), arr((share, low), F32)],
        )
        grad_middle = grad_middle.reshape(3, 3, share, 128)
    else:
        grad_last = lax.psum_scatter(last_sum[0], "wide", scatter_dimension=0, tiled=True)
        grad_middle = lax.psum_scatter(middle_sum[0], "wide", scatter_dimension=0, tiled=True)
        share = grad_middle.shape[0]
        grad_middle = grad_middle.reshape(share, TAPS, 128).transpose(1, 0, 2).reshape(3, 3, share, 128)
        whole = lax.psum(first_sum[0], "wide")
        whole = lax.all_gather(whole, "narrow", axis=0, tiled=True)
        share = whole.shape[0] // wide
        grad_first = lax.dynamic_slice(whole, (w * share, n * cols), (share, cols))
    return (
        block_out, input_grad, grad_first, grad_middle, grad_last,
        tilt_one[0], level_one[0], tilt_two[0], level_two[0], tilt_three[0], level_three[0],
    )


def solution(mesh):
    wide = mesh.shape["wide"]
    placed = (
        P(None, "wide", "narrow"),
        P(None, "wide"),
        P("wide", "narrow"),
        P(None, None, "wide", "narrow"),
        P("wide", "narrow"),
        P("narrow"),
        P("narrow"),
        P("narrow"),
        P("narrow"),
        P("narrow"),
        P("narrow"),
        P(None, "wide", "narrow"),
    )
    return jax.shard_map(
        lambda *arrays: on_device(*arrays, wide=wide),
        mesh=mesh,
        in_specs=placed,
        out_specs=(
            P(None, "wide", "narrow"),
            P(None, "wide", "narrow"),
            P("wide", "narrow"),
            P(None, None, "wide", "narrow"),
            P("wide", "narrow"),
            P("narrow"),
            P("narrow"),
            P("narrow"),
            P("narrow"),
            P("narrow"),
            P("narrow"),
        ),
        check_vma=False,
    )
```

```python
import jax
import jax.numpy as jnp
from jax import lax
from jax.experimental import pallas as pl
from jax.experimental.pallas import tpu as pltpu
from jax.sharding import PartitionSpec as P


F32 = jnp.float32
BF = jnp.bfloat16
EPS = 1e-05
SIDE = 7
PITCH = 8
TAPS = 9
NARROW = 4
MESH = ("narrow", "wide")
VMEM_BYTES = 20 * 2**20


def dot(left, right):
    return jnp.dot(left, right, preferred_element_type=F32)


def dot_nt(left, right):
    return lax.dot_general(left, right, (((1,), (1,)), ((), ())), preferred_element_type=F32)


def dot_tn(left, right):
    return lax.dot_general(left, right, (((0,), (0,)), ((), ())), preferred_element_type=F32)


def position():
    n, w = lax.axis_index("narrow"), lax.axis_index("wide")
    return n, w // 2, w % 2


def run(kernel, operands, outs, scratch=(), flops=0):
    moved = sum(o.size * o.dtype.itemsize for o in (*operands, *outs))
    return pl.pallas_call(
        kernel,
        out_shape=outs,
        name=kernel.__name__,
        in_specs=[pl.BlockSpec(memory_space=pltpu.VMEM)] * len(operands),
        out_specs=[pl.BlockSpec(memory_space=pltpu.VMEM)] * len(outs),
        scratch_shapes=list(scratch),
        cost_estimate=pl.CostEstimate(flops=flops, bytes_accessed=moved, transcendentals=0),
        compiler_params=pltpu.CompilerParams(vmem_limit_bytes=VMEM_BYTES),
    )(*operands)


def arr(shape, dtype):
    return jax.ShapeDtypeStruct(shape, dtype)


def by_rows(rows, body, carry):
    return body(pl.ds(0, rows), carry)


def fold(values):
    total = values[0:8]
    for start in range(8, values.shape[0], 8):
        total = total + values[start : start + 8]
    return total


def zeros_acc(channels):
    return (jnp.zeros((8, channels), F32), jnp.zeros((8, channels), F32))


def column_sum(acc):
    return jnp.sum(acc, axis=0, keepdims=True)


def sigmoid(values):
    return 0.5 * jnp.tanh(0.5 * values) + 0.5


def coefficients(total, squares, inverse, gain, shift):
    mean = total * inverse
    spread = squares * inverse - mean * mean
    scale = lax.rsqrt(spread + EPS)
    slope = gain * scale
    return mean, scale, slope, shift - mean * slope


def wide_row(block, first, count=NARROW):
    return jnp.concatenate([block[first + k : first + k + 1] for k in range(count)], axis=1)


def row_of(block, first, index):
    rows = [jnp.where(index == k, block[first + k : first + k + 1], 0.0) for k in range(NARROW)]
    return rows[0] + rows[1] + rows[2] + rows[3]


def inverse_count(params, b, channels):
    row = params[b, 4:5, :]
    return row if channels == 128 else jnp.concatenate([row] * (channels // 128), axis=1)


def lane_block(index):
    return pl.ds(pl.multiple_of(index * 128, 128), 128)


def send_stats(message, first, second):
    for k in range(NARROW):
        message[k : k + 1, :] = first[:, 128 * k : 128 * k + 128]
        message[NARROW + k : NARROW + k + 1, :] = second[:, 128 * k : 128 * k + 128]


def repeat_first(message):
    block = message[0]
    for place in range(1, message.shape[0]):
        message[place] = block


def total_of(parts, index):
    total = parts[index]
    for place in range(NARROW, parts.shape[0], NARROW):
        total = total + parts[place + index]
    return total


def sum_parts(parts):
    total = parts[0]
    for place in range(1, parts.shape[0]):
        total = total + parts[place]
    return total


def place_columns(p0, p1, p2, p3, out):
    z = position()[1]
    for j, piece in enumerate((p0, p1, p2, p3)):
        out[:, lane_block((z - j) & 3)] = piece[...]


def first_product(x, *refs):
    pieces, (w_first, send_far, own_far, send_near, own_near) = refs[:-5], refs[-5:]
    n, z, y = position()
    if len(pieces) == 1:
        w_first[...] = pieces[0][...]
    else:
        rows = pieces[0].shape[0]
        for dy, piece in enumerate(pieces):
            w_first[pl.ds(pl.multiple_of((y ^ dy) * rows, rows), rows), :] = piece[...]
    for ref, m in ((send_far, 3), (own_far, 2), (send_near, 1), (own_near, 0)):
        ref[...] = dot(x[n ^ m], w_first[...]).astype(ref.dtype)


def first_join(own, near, far, mask, small, pre, message):
    b = position()[0]

    def body(ds, acc):
        values = own[ds, :] + near[ds, :].astype(F32) + far[ds, :].astype(F32)
        pre[ds, :] = values.astype(BF)
        kept = mask[b, ds, :] * values
        return acc[0] + fold(kept), acc[1] + fold(kept * values)

    sums = by_rows(own.shape[0], body, zeros_acc(own.shape[1]))
    send_stats(message, column_sum(sums[0]), column_sum(sums[1]))
    message[8:16, :] = small[...]


def middle_forward(pre0, pre1, pre2, pre3, sum0, sum1, sum2, sum3, mask, to_canvas, to_rows, weight,
                   hidden, pre, coef, message, params, active, spread, joined):
    n = position()[0]
    blocks = (sum0[...], sum1[...], sum2[...], sum3[...])
    for m, block in enumerate(blocks):
        params[n ^ m, 0:4, :] = block[8:12]
    for b in range(NARROW):
        params[b, 4:5, :] = 1.0 / blocks[0][12 + b : 13 + b]
        params[b, 5:8, :] = jnp.zeros((3, 128), F32)
    rows, places = pre0.shape[0], to_canvas.shape[0]
    img = places // (SIDE * PITCH)
    margin = img * (PITCH + 1)
    gain = jnp.concatenate([params[k, 0:1, :] for k in range(NARROW)], axis=1)
    shift = jnp.concatenate([params[k, 1:2, :] for k in range(NARROW)], axis=1)
    spread[0:margin, :] = jnp.zeros((margin, spread.shape[1]), F32)
    spread[margin + places :, :] = jnp.zeros((margin, spread.shape[1]), F32)
    line = img * PITCH
    for m, source in enumerate((pre0, pre1, pre2, pre3)):
        b = n ^ m
        block = blocks[m]
        mean, scale, slope, offset = coefficients(
            wide_row(block, 0), wide_row(block, NARROW), inverse_count(params, b, gain.shape[1]), gain, shift
        )
        for k, row in enumerate((mean, scale, slope, offset)):
            coef[m, k : k + 1, :] = row

        def activate(ds, carry):
            act = source[ds, :].astype(F32) * slope + offset
            active[ds, :] = (mask[b, ds, :] * act * sigmoid(act)).astype(BF)
            return carry

        by_rows(rows, activate, 0)
        hidden[m] = dot(to_canvas[...], active[...]).astype(BF)
        spread[margin : margin + places, :] = dot(hidden[m], weight[...])
        for top in range(SIDE):
            acc = None
            for tap in range(TAPS):
                start = margin + top * line + ((tap // 3 - 1) * PITCH + tap % 3 - 1) * img
                part = spread[start : start + line, 128 * tap : 128 * tap + 128]
                acc = part if acc is None else acc + part
            joined[top * line : (top + 1) * line, :] = acc.astype(BF)
        pre[m] = dot(to_rows[...], joined[...]).astype(BF)

        def collect(ds, acc):
            values = pre[m, ds, :].astype(F32)
            kept = mask[b, ds, :] * values
            return acc[0] + fold(kept), acc[1] + fold(kept * values)

        sums = by_rows(rows, collect, zeros_acc(128))
        message[0, 2 * m : 2 * m + 1, :] = column_sum(sums[0])
        message[0, 2 * m + 1 : 2 * m + 2, :] = column_sum(sums[1])
    repeat_first(message)


def last_forward(src0, src1, src2, src3, parts, params, mask, weight,
                 hidden, own, coef, pre, message):
    n = position()[0]
    rows = own.shape[0]
    sources = (src0, src1, src2, src3)
    blocks = [total_of(parts, n ^ i) for i in range(NARROW)]
    for m in range(NARROW):
        b = n ^ m
        for i in range(NARROW):
            j = m ^ i
            here = lane_block(n ^ i)
            mean, scale, slope, offset = coefficients(
                blocks[i][2 * j : 2 * j + 1], blocks[i][2 * j + 1 : 2 * j + 2], inverse_count(params, b, 128),
                params[n ^ i, 2:3, :], params[n ^ i, 3:4, :],
            )
            if m == 0:
                own[:, here] = sources[i][j]
                for k, row in enumerate((mean, scale, slope, offset)):
                    coef[k : k + 1, here] = row

            def activate(ds, carry):
                act = sources[i][j, ds, :].astype(F32) * slope + offset
                hidden[m, ds, here] = (mask[b, ds, :] * act * sigmoid(act)).astype(BF)
                return carry

            by_rows(rows, activate, 0)
        pre[m] = dot(hidden[m], weight[...])

        def collect(ds, acc):
            values = pre[m, ds, :]
            kept = mask[b, ds, :] * values
            return acc[0] + fold(kept), acc[1] + fold(kept * values)

        sums = by_rows(rows, collect, zeros_acc(pre.shape[2]))
        message[0, 2 * m : 2 * m + 1, :] = column_sum(sums[0])
        message[0, 2 * m + 1 : 2 * m + 2, :] = column_sum(sums[1])
    repeat_first(message)


def block_output(pre, x, cotangent, parts, params, gain, shift, mask, out, grad, coef, message):
    n = position()[0]
    rows, channels = pre.shape[1:]
    block = sum_parts(parts)
    for m in range(NARROW):
        b = n ^ m
        mean, scale, slope, offset = coefficients(
            block[2 * m : 2 * m + 1], block[2 * m + 1 : 2 * m + 2], inverse_count(params, b, channels), gain[...], shift[...]
        )
        for k, row in enumerate((mean, scale, slope, offset)):
            coef[m, k : k + 1, :] = row

        def body(ds, acc):
            values = pre[m, ds, :]
            inside = mask[b, ds, :]
            summed = values * slope + offset + x[b, ds, :].astype(F32)
            gate = sigmoid(summed)
            value = summed * gate
            out[b, ds, :] = (inside * value).astype(BF)
            local = inside * cotangent[b, ds, :].astype(F32) * (gate + value * (1.0 - gate))
            grad[m, ds, :] = local
            return acc[0] + fold(local), acc[1] + fold(local * values)

        sums = by_rows(rows, body, zeros_acc(channels))
        first, second = column_sum(sums[0]), column_sum(sums[1])
        message[0, 2 * m : 2 * m + 1, :] = first
        message[0, 2 * m + 1 : 2 * m + 2, :] = scale * (second - mean * first)
    repeat_first(message)


def last_backward(pre, grad, parts, params, coef, mask, weight,
                  grad_pre, send_far, own_far, send_near, own_near, level_sum, tilt_sum):
    n = position()[0]
    rows = pre.shape[1]
    block = sum_parts(parts)
    for s, ref in enumerate((level_sum, tilt_sum)):
        acc = block[s : s + 1]
        for m in range(1, NARROW):
            acc = acc + block[2 * m + s : 2 * m + s + 1]
        ref[...] = acc
    for m, ref in ((3, send_far), (2, own_far), (1, send_near), (0, own_near)):
        b = n ^ m
        mean, scale, slope = (coef[m, k : k + 1, :] for k in range(3))
        inverse = inverse_count(params, b, block.shape[1])
        level = block[2 * m : 2 * m + 1] * inverse
        tilt = block[2 * m + 1 : 2 * m + 2] * inverse
        level, tilt = level - mean * scale * tilt, scale * tilt

        def body(ds, carry):
            away = mask[b, ds, :] * (level + pre[m, ds, :] * tilt)
            grad_pre[m, ds, :] = (slope * (grad[m, ds, :] - away)).astype(BF)
            return carry

        by_rows(rows, body, 0)
        ref[...] = dot_nt(grad_pre[m], weight[...]).astype(ref.dtype)


def middle_join(own, near, far, pre, coef, mask, grad, own_q, near_q, far_q, message):
    b = position()[0]
    mean, scale, slope, offset = (coef[k : k + 1, :] for k in range(4))
    back = mean * scale

    def body(ds, acc):
        values = pre[ds, :].astype(F32)
        act = values * slope + offset
        gate = sigmoid(act)
        total = own[ds, :] + near[ds, :].astype(F32) + far[ds, :].astype(F32)
        local = total * mask[b, ds, :] * (gate * (1.0 + act * (1.0 - gate)))
        grad[ds, :] = local
        return acc[0] + fold(local), acc[1] + fold(local * (values * scale - back))

    sums = by_rows(own.shape[0], body, zeros_acc(own.shape[1]))
    send_stats(message.at[0], column_sum(sums[0]), column_sum(sums[1]))
    repeat_first(message)
    own_q[...] = grad[:, lane_block(b)].astype(BF)
    near_q[...] = grad[:, lane_block(b ^ 1)].astype(BF)
    far_q[0] = grad[:, lane_block(b ^ 2)].astype(BF)
    far_q[1] = grad[:, lane_block(b ^ 3)].astype(BF)


def middle_backward(grad, pre, parts, params, coef, mask, first_pre, first_coef, to_canvas, to_rows,
                    w0, w1, w2, w3, grad_first, message,
                    grad_pre, weight, gathered, canvas):
    n = position()[0]
    rows, places = grad.shape[0], to_canvas.shape[0]
    img = places // (SIDE * PITCH)
    margin = img * (PITCH + 1)
    block = sum_parts(parts)
    mean, scale, slope = (coef[k : k + 1, :] for k in range(3))
    inverse = inverse_count(params, n, grad.shape[1])
    level = wide_row(block, 0) * inverse
    tilt = wide_row(block, NARROW) * inverse
    level, tilt = level - mean * scale * tilt, scale * tilt

    def body(ds, carry):
        away = mask[n, ds, :] * (level + pre[ds, :].astype(F32) * tilt)
        grad_pre[ds, :] = (slope * (grad[ds, :] - away)).astype(BF)
        return carry

    by_rows(rows, body, 0)
    for j, piece in enumerate((w0, w1, w2, w3)):
        for tap in range(TAPS):
            weight[tap, :, lane_block(n ^ j)] = piece[:, 128 * tap : 128 * tap + 128]
    canvas[...] = dot(to_canvas[...], grad_pre[...]).astype(BF).astype(F32)
    gathered[...] = jnp.zeros_like(gathered)
    for tap in range(TAPS):
        start = margin + ((tap // 3 - 1) * PITCH + tap % 3 - 1) * img
        gathered[start : start + places, :] += dot_nt(canvas[...].astype(BF), weight[tap])
    canvas[...] = gathered[margin : margin + places, :]
    grad_pre[...] = dot(to_rows[...], canvas[...].astype(BF)).astype(BF)
    mean, scale, slope, offset = (first_coef[0, k : k + 1, :] for k in range(4))
    back = mean * scale

    def finish(ds, acc):
        values = first_pre[ds, :].astype(F32)
        act = values * slope + offset
        gate = sigmoid(act)
        local = grad_pre[ds, :].astype(F32) * mask[n, ds, :] * (gate * (1.0 + act * (1.0 - gate)))
        grad_first[ds, :] = local.astype(BF)
        return acc[0] + fold(local), acc[1] + fold(local * (values * scale - back))

    sums2 = by_rows(rows, finish, zeros_acc(grad.shape[1]))
    send_stats(message, column_sum(sums2[0]), column_sum(sums2[1]))


def first_weight(g0, g1, g2, g3, p0, p1, p2, p3, sum0, sum1, sum2, sum3, params, coef, mask, x,
                 level_sum, tilt_sum, grad_pre, *refs):
    outs, acc = refs[:-1], refs[-1]
    n, z, y = position()
    rows, channels = g0.shape
    blocks = (sum0[...], sum1[...], sum2[...], sum3[...])
    every = blocks[0] + blocks[1] + blocks[2] + blocks[3]
    for m, (g, pre) in enumerate(((g0, p0), (g1, p1), (g2, p2), (g3, p3))):
        b = n ^ m
        block = blocks[m]
        mean, scale, slope = (coef[m, k : k + 1, :] for k in range(3))
        inverse = inverse_count(params, b, channels)
        level = wide_row(block, 0) * inverse
        tilt = wide_row(block, NARROW) * inverse
        level, tilt = level - mean * scale * tilt, scale * tilt
        away = mask[b] * (level + pre[...].astype(F32) * tilt)
        grad_pre[m] = (slope * (g[...].astype(F32) - away)).astype(BF)
    total = dot_tn(x[n], grad_pre[0])
    for m in range(1, NARROW):
        total = total + dot_tn(x[n ^ m], grad_pre[m])
    acc[...] = total
    if len(outs) == 1:
        outs[0][...] = acc[...]
    else:
        half = acc.shape[0] // 2
        for ref, h in zip(outs, (y, 1 - y)):
            top = pl.multiple_of(h * half, half)
            for j in range(NARROW):
                block = acc[pl.ds(top, half), lane_block(n ^ j)]
                ref[:, 128 * j : 128 * j + 128] = block.astype(ref.dtype)
    level_sum[...] = row_of(every, 0, n)
    tilt_sum[...] = row_of(every, NARROW, n)


def input_gradient(grad_pre, weight, grad, out):
    n = position()[0]
    for m in range(NARROW):
        out[n ^ m] = dot_nt(grad_pre[m], weight[...]) + grad[m]


def last_weight(hidden, grad_pre, *refs):
    acc = refs[-1]
    for m in range(NARROW):
        product = dot_tn(hidden[m], grad_pre[m])
        if m == 0:
            acc[...] = product
        else:
            acc[...] += product
    hand_out(acc, refs[:-1])


def hand_out(acc, outs):
    if len(outs) == 1:
        outs[0][...] = acc[...]
        return
    _, z, y = position()
    own, away = outs
    rows = acc.shape[0] // 8
    for j in range(4):
        place = pl.ds(j * rows, rows)
        for ref, dy in ((own, 0), (away, 1)):
            top = ((z ^ j) * 2 + (y ^ dy)) * rows
            ref[place, :] = acc[pl.ds(pl.multiple_of(top, rows), rows), :].astype(ref.dtype)


def middle_weight(hidden, q0, q1, far, last, pre, sum0, sum1, sum2, sum3, norm, params, mask, to_canvas,
                  level_sum, tilt_sum, *refs):
    outs, (acc, shifted, canvases) = refs[:-3], refs[-3:]
    n = position()[0]
    places = to_canvas.shape[0]
    img = places // (SIDE * PITCH)
    margin = img * (PITCH + 1)
    norms = total_of(norm, n)
    blocks = (sum0[...], sum1[...], sum2[...], sum3[...])
    every = blocks[0] + blocks[1] + blocks[2] + blocks[3]
    level_sum[...] = row_of(every, 0, n)
    tilt_sum[...] = row_of(every, NARROW, n)
    for m, piece in enumerate((q0[...], q1[...], far[0], last[1])):
        b = n ^ m
        inverse = inverse_count(params, b, 128)
        mean, scale, slope, _ = coefficients(
            norms[2 * m : 2 * m + 1], norms[2 * m + 1 : 2 * m + 2], inverse, params[n, 2:3, :], params[n, 3:4, :]
        )
        block = blocks[m]
        level = row_of(block, 0, n) * inverse
        tilt = row_of(block, NARROW, n) * inverse
        level, tilt = level - mean * scale * tilt, scale * tilt
        away = mask[b] * (level + pre[m].astype(F32) * tilt)
        grad_pre = (slope * (piece.astype(F32) - away)).astype(BF)
        canvas = canvases.at[m]
        canvas[0:margin, :] = jnp.zeros((margin, 128), F32)
        canvas[margin + places :, :] = jnp.zeros((margin, 128), F32)
        canvas[margin : margin + places, :] = dot(to_canvas[...], grad_pre)
        for tap in range(TAPS):
            start = margin - ((tap // 3 - 1) * PITCH + tap % 3 - 1) * img
            here = slice(m * places, (m + 1) * places)
            shifted[here, 128 * tap : 128 * tap + 128] = canvas[start : start + places, :].astype(BF)
    acc[...] = dot_tn(hidden[...].reshape(NARROW * places, hidden.shape[2]), shifted[...])
    hand_out(acc, outs)


def gather_middle(near, far, out):
    _, z, y = position()
    rows = out.shape[0] // 8
    for dy, stack in enumerate((near, far)):
        for j in range(4):
            here = pl.ds(pl.multiple_of(((z ^ j) * 2 + (y ^ dy)) * rows, rows), rows)
            for tap in range(TAPS):
                top = (j * TAPS + tap) * rows
                out[here, 128 * tap : 128 * tap + 128] = stack[top : top + rows, :]


def gather_last(near, far, out):
    _, z, y = position()
    rows = out.shape[0] // 8
    for dy, stack in enumerate((near, far)):
        for j in range(4):
            here = pl.ds(pl.multiple_of(((z ^ j) * 2 + (y ^ dy)) * rows, rows), rows)
            out[here, :] = stack[j * rows : (j + 1) * rows, :]


def merge_first(own, away, keep, near, far):
    parts = [own[:, 128 * i : 128 * i + 128] + away[:, 128 * i : 128 * i + 128].astype(F32) for i in range(NARROW)]
    keep[...] = parts[0]
    near[...] = parts[1].astype(BF)
    far[0] = parts[2].astype(BF)
    far[1] = parts[3].astype(BF)


def sort_first(own, near, far, last, keep, *refs):
    sends, pieces = refs[:-1], refs[-1]
    n, z, _ = position()
    for i, piece in enumerate((own[...], near[...], far[0], last[1])):
        pieces[i] = piece.astype(F32)
    keep[...] = pieces[n ^ z]
    for j, send in enumerate(sends):
        send[...] = pieces[n ^ z ^ (j + 1)].astype(BF)


def finish_first(keep, p1, p2, p3, out):
    out[...] = keep[...] + p1[...].astype(F32) + p2[...].astype(F32) + p3[...].astype(F32)


def add_tiles(*refs):
    total = refs[0][...]
    for ref in refs[1:-1]:
        total = total + ref[...]
    refs[-1][...] = total


def add_parts(parts, out):
    out[...] = sum_parts(parts)


def merge_wide(own, away, own_last, away_last, keep, keep_last, *sends):
    rows, middle = keep.shape
    keep[...] = own[0:rows, :] + away[0:rows, :].astype(F32)
    keep_last[...] = own_last[0:rows, :] + away_last[0:rows, :].astype(F32)
    for j, send in enumerate(sends):
        here = slice((j + 1) * rows, (j + 2) * rows)
        send[:, 0:middle] = (own[here, :] + away[here, :].astype(F32)).astype(BF)
        send[:, middle:] = (own_last[here, :] + away_last[here, :].astype(F32)).astype(BF)


def finish_wide(keep, keep_last, p1, p2, p3, out, out_last):
    middle = keep.shape[1]
    for tap in range(TAPS):
        here = slice(128 * tap, 128 * tap + 128)
        out[tap] = keep[:, here] + p1[:, here].astype(F32) + p2[:, here].astype(F32) + p3[:, here].astype(F32)
    out_last[...] = (
        keep_last[...] + p1[:, middle:].astype(F32) + p2[:, middle:].astype(F32) + p3[:, middle:].astype(F32)
    )


def exchange(message):
    return lax.all_to_all(message, ("wide", "narrow"), 0, 0, tiled=True)


def swap_core(values):
    return lax.ppermute(values, "narrow", [(i, i ^ 1) for i in range(NARROW)])


def swap_chip(values):
    return lax.ppermute(values, "narrow", [(i, i ^ 2) for i in range(NARROW)])


def swap_wide(values, step, wide):
    return lax.ppermute(values, "wide", [(i, i ^ step) for i in range(wide)])


def after(value, *others):
    return lax.optimization_barrier((value, *others))[0]


def from_all(values, *others):
    far = swap_chip(values)
    if others:
        return values, swap_core(after(values, *others)), far, swap_core(after(far, *others))
    return values, swap_core(values), far, swap_core(far)


def add(*tiles):
    return run(add_tiles, tiles, [arr(tiles[0].shape, F32)])[0]


def sum_wide(values, wide, beside=(), late=()):
    if wide == 8:
        values = add(after(values, *beside) if beside else values, swap_wide(values, 1, wide))
        parts = [swap_wide(values, step, wide) for step in (2, 4, 6)]
        total = add(after(values, *late) if late else values, *parts)
        return values, total
    step = 1
    while step < wide:
        values = add(values, swap_wide(values, step, wide))
        step *= 2
    return values, values


def reduce_narrow(send_far, own_far, send_near, own_near, *others):
    got_far = swap_core(send_far)
    got_near = swap_core(send_near)
    joined = (own_far + got_far.astype(F32)).astype(BF)
    if others:
        joined = after(joined, *others)
    return (own_near, got_near, swap_chip(joined)), joined


def transposed_steps():
    steps = []
    for j in range(NARROW):
        pairs = []
        for k in range(NARROW):
            for z in range(4):
                for y in range(2):
                    pairs.append((k * 8 + 2 * z + y, z * 8 + 2 * ((k + j) % 4) + y))
        steps.append(pairs)
    return steps


def on_device(inputs, sides, w_first, w_middle, w_last, gain_first, shift_first, gain_middle, shift_middle,
              gain_last, shift_last, cotangent, *, wide):
    micro, rows, low = inputs.shape
    img = sides.shape[1]
    mid = w_last.shape[0] * wide
    cols = w_first.shape[1]
    places = img * SIDE * PITCH
    direct = wide == 8
    n = lax.axis_index("narrow")
    w = lax.axis_index("wide")

    spots = jnp.arange(rows, dtype=jnp.int32)
    spot_y, spot_x, spot_img = spots % 49 // 7, spots % 7, spots // 49

    def mask_of(limits):
        limits = jnp.repeat(limits, 49, axis=1)
        return ((spot_y[None] < limits) & (spot_x[None] < limits)).astype(F32)[:, :, None]

    place = (spot_y * PITCH + spot_x) * img + spot_img
    to_canvas = (jnp.arange(places, dtype=jnp.int32)[:, None] == place[None, :]).astype(BF)
    to_rows = (place[:, None] == jnp.arange(places, dtype=jnp.int32)[None, :]).astype(BF)

    if direct:
        steps = transposed_steps()
        share = w_last.shape[0]
        packed = w_middle.reshape(TAPS * share, 128)
        middle_near = [packed] + [swap_wide(packed, 2 * j, wide) for j in range(1, 4)]
        first_pieces = [lax.ppermute(w_first, MESH, pairs) for pairs in steps]
        first_half = run(place_columns, first_pieces, [arr((w_first.shape[0], mid), BF)])[0]
        first_pieces = [first_half, swap_wide(first_half, 1, wide)]
    else:
        first_all = lax.all_gather(lax.all_gather(w_first, "narrow", axis=1, tiled=True), "wide", axis=0, tiled=True)
        first_pieces = [lax.dynamic_slice_in_dim(first_all, n * low, low, 0)]
        middle_slice = lax.all_gather(w_middle, "wide", axis=2, tiled=True)
        middle_slice = middle_slice.reshape(TAPS, mid, 128).transpose(1, 0, 2).reshape(mid, TAPS * 128)
        last_slice = lax.all_gather(w_last, "wide", axis=0, tiled=True)

    counts = jnp.sum((sides * sides).astype(F32), axis=1)
    small = jnp.concatenate(
        [jnp.stack([gain_first, shift_first, gain_middle, shift_middle]) * (1.0 / wide),
         jnp.broadcast_to(counts[:, None], (micro, 128))], axis=0
    )

    tile = arr((8, 128), F32)
    across = arr((wide, 8, low), F32)
    flat = arr((rows, mid), BF)
    flat32 = arr((rows, mid), F32)

    w_rows, send_far, own_far, send_near, own_near = run(
        first_product, (inputs, *first_pieces),
        [arr((low, mid), BF), flat, flat32, flat, flat32], flops=2 * micro * rows * low * mid,
    )
    joined, begun = reduce_narrow(send_far, own_far, send_near, own_near, *(middle_near[:2] if direct else ()))
    if direct:
        middle_near = jnp.concatenate([after(middle_near[0], begun)] + middle_near[1:], axis=0)
        middle_far = swap_wide(middle_near, 1, wide)
    mask = mask_of(after(sides, begun))
    beside = ()
    if direct:
        held = after(w_last, middle_near)
        last_near = jnp.concatenate([held] + [swap_wide(held, 2 * j, wide) for j in range(1, 4)], axis=0)
        beside = (middle_far, last_near)
    pre_one, message = run(first_join, (*joined, mask, small), [flat, arr((16, 128), F32)])
    begun, total = sum_wide(message, wide, beside=beside)
    if direct:
        last_far = swap_wide(after(last_near, total), 1, wide)
    pre_ones = from_all(pre_one, total)
    sums_one = from_all(total)
    if direct:
        middle_slice = run(gather_middle, (middle_near, middle_far), [arr((mid, TAPS * 128), BF)])[0]

    hidden_one, pre_two, coef_one, message, params = run(
        middle_forward, (*pre_ones, *sums_one, mask, to_canvas, to_rows, middle_slice),
        [arr((micro, places, mid), BF), arr((micro, rows, 128), BF), arr((micro, 8, mid), F32), arr((wide * NARROW, 8, 128), F32), arr((NARROW, 8, 128), F32)],
        [pltpu.VMEM((rows, mid), BF), pltpu.VMEM((places + 2 * img * (PITCH + 1), TAPS * 128), F32), pltpu.VMEM((places, 128), BF)],
        flops=2 * micro * places * mid * TAPS * 128,
    )
    if direct:
        last_slice = run(gather_last, (last_near, last_far), [arr((mid, low), BF)])[0]
    if direct:
        message = after(message, last_far)
    parts_two = exchange(message)
    pre_twos = from_all(pre_two, parts_two)
    held = after(middle_slice, pre_twos[3], parts_two)
    middle_away = swap_chip(held)

    hidden_two, own_two, coef_two, pre_three, message = run(
        last_forward, (*pre_twos, parts_two, params, mask, last_slice),
        [arr((micro, rows, mid), BF), flat, arr((8, mid), F32), arr((micro, rows, low), F32), across],
        flops=2 * micro * rows * low * mid,
    )
    parts_three = lax.all_to_all(message, "wide", 0, 0, tiled=True)
    block_out, grad_sum, coef_three, message = run(
        block_output,
        (pre_three, inputs, cotangent, parts_three, params, gain_last[None], shift_last[None], mask),
        [arr(inputs.shape, BF), arr((micro, rows, low), F32), arr((micro, 8, low), F32), across],
    )
    parts_four = lax.all_to_all(message, "wide", 0, 0, tiled=True)

    grad_three, send_far, own_far, send_near, own_near, level_three, tilt_three = run(
        last_backward, (pre_three, grad_sum, parts_four, params, coef_three, mask, last_slice),
        [arr((micro, rows, low), BF), flat, flat32, flat, flat32, arr((1, low), F32), arr((1, low), F32)],
        flops=2 * micro * rows * low * mid,
    )
    joined, begun = reduce_narrow(send_far, own_far, send_near, own_near, middle_away)
    grad_three = after(grad_three, begun)

    def handed(channels):
        if direct:
            return [arr((mid // 2, channels), F32), arr((mid // 2, channels), BF)]
        return [arr((mid, channels), F32)]

    last_sum = run(
        last_weight, (hidden_two, grad_three), handed(low), [pltpu.VMEM((mid, low), F32)],
        flops=2 * micro * rows * low * mid,
    )
    slim = arr((rows, 128), BF)
    row = arr((1, 128), F32)
    if direct:
        got_last_sum = swap_wide(last_sum[1], 1, wide)
        joined = (after(joined[0], got_last_sum), *joined[1:])
    grad_two, own_q, near_q, far_q, message = run(
        middle_join, (*joined, own_two, coef_two, mask), [flat32, slim, slim, arr((2, rows, 128), BF), arr((wide, 8, 128), F32)]
    )
    got_far = swap_chip(far_q)
    middle_slices = (middle_slice, swap_core(held), middle_away, swap_core(middle_away))
    parts_five = lax.all_to_all(after(message, *middle_slices), "wide", 0, 0, tiled=True)
    total_five = run(add_parts, (parts_five,), [tile])[0]
    near_q, got_far = lax.optimization_barrier((near_q, got_far, parts_five))[:2]
    got_near, got_last = swap_core(near_q), swap_core(got_far)
    sums_five = from_all(total_five)

    grad_one, message = run(
        middle_backward,
        (grad_two, own_two, parts_five, params, coef_two, mask, pre_one, coef_one, to_canvas, to_rows, *middle_slices),
        [flat, tile],
        [pltpu.VMEM((rows, mid), BF), pltpu.VMEM((TAPS, mid, mid), BF),
         pltpu.VMEM((places + 2 * img * (PITCH + 1), mid), F32), pltpu.VMEM((places, mid), F32)],
        flops=2 * places * mid * TAPS * mid,
    )
    level_two, tilt_two, *middle_sum = run(
        middle_weight,
        (hidden_one, own_q, got_near, got_far, got_last, pre_two, *sums_five, parts_two, params, mask, to_canvas),
        [row, row, *handed(TAPS * 128)],
        [pltpu.VMEM((mid, TAPS * 128), F32), pltpu.VMEM((micro * places, TAPS * 128), BF),
         pltpu.VMEM((micro, places + 2 * img * (PITCH + 1), 128), F32)],
        flops=2 * micro * places * mid * TAPS * 128,
    )
    begun, total = sum_wide(message, wide, beside=middle_sum)
    grad_ones = from_all(after(grad_one, sums_five[2]), total)
    sums_six = from_all(total)
    if direct:
        got_middle = swap_wide(after(middle_sum[1], begun), 1, wide)

    out_first = [arr((low // 2, mid), F32), arr((low // 2, mid), BF)] if direct else [arr((low, mid), F32)]
    level_one, tilt_one, grad_pre_one, *first_sum = run(
        first_weight,
        (*grad_ones, *pre_ones, *sums_six, params, coef_one, mask, inputs),
        [row, row, arr((micro, rows, mid), BF), *out_first], [pltpu.VMEM((low, mid), F32)],
        flops=2 * micro * rows * low * mid,
    )
    input_grad = run(
        input_gradient, (grad_pre_one, w_rows, grad_sum), [arr((micro, rows, low), F32)],
        flops=2 * micro * rows * low * mid,
    )[0]

    if direct:
        got_first = swap_wide(after(first_sum[1], got_middle), 1, wide)
        channels = TAPS * 128
        keep, keep_last, *sends = run(
            merge_wide, (middle_sum[0], after(got_middle, first_sum[1]), last_sum[0], got_last_sum),
            [arr((share, channels), F32), arr((share, low), F32)] + [arr((share, channels + low), BF)] * 3,
        )
        parts = [swap_wide(send, 2 * j + 2, wide) for j, send in enumerate(sends)]
        piece, half = arr((low // 2, cols), BF), arr((low // 2, cols), F32)
        keep_first, near, far = run(merge_first, (first_sum[0], after(got_first, parts[0])), [half, piece, arr((2, low // 2, cols), BF)])
        far = after(swap_chip(far), *parts[0:2])
        keep_first, *sends = run(
            sort_first, (keep_first, swap_core(near), far, swap_core(far)), [half, piece, piece, piece],
            [pltpu.VMEM((NARROW, low // 2, cols), F32)],
        )
        arrived = [swap_wide(send, 2 * j + 2, wide) for j, send in enumerate(sends)]
        grad_first = run(finish_first, (keep_first, *arrived), [half])[0]
        grad_middle, grad_last = run(
            finish_wide, (keep, keep_last, *parts),
            [arr((TAPS, share, 128), F32), arr((share, low), F32)],
        )
        grad_middle = grad_middle.reshape(3, 3, share, 128)
    else:
        grad_last = lax.psum_scatter(last_sum[0], "wide", scatter_dimension=0, tiled=True)
        grad_middle = lax.psum_scatter(middle_sum[0], "wide", scatter_dimension=0, tiled=True)
        share = grad_middle.shape[0]
        grad_middle = grad_middle.reshape(share, TAPS, 128).transpose(1, 0, 2).reshape(3, 3, share, 128)
        whole = lax.psum(first_sum[0], "wide")
        whole = lax.all_gather(whole, "narrow", axis=0, tiled=True)
        share = whole.shape[0] // wide
        grad_first = lax.dynamic_slice(whole, (w * share, n * cols), (share, cols))
    return (
        block_out, input_grad, grad_first, grad_middle, grad_last,
        tilt_one[0], level_one[0], tilt_two[0], level_two[0], tilt_three[0], level_three[0],
    )


def solution(mesh):
    wide = mesh.shape["wide"]
    placed = (
        P(None, "wide", "narrow"),
        P(None, "wide"),
        P("wide", "narrow"),
        P(None, None, "wide", "narrow"),
        P("wide", "narrow"),
        P("narrow"),
        P("narrow"),
        P("narrow"),
        P("narrow"),
        P("narrow"),
        P("narrow"),
        P(None, "wide", "narrow"),
    )
    return jax.shard_map(
        lambda *arrays: on_device(*arrays, wide=wide),
        mesh=mesh,
        in_specs=placed,
        out_specs=(
            P(None, "wide", "narrow"),
            P(None, "wide", "narrow"),
            P("wide", "narrow"),
            P(None, None, "wide", "narrow"),
            P("wide", "narrow"),
            P("narrow"),
            P("narrow"),
            P("narrow"),
            P("narrow"),
            P("narrow"),
            P("narrow"),
        ),
        check_vma=False,
    )
```

```python
import jax
import jax.numpy as jnp
from jax import lax
from jax.experimental import pallas as pl
from jax.experimental.pallas import tpu as pltpu
from jax.sharding import PartitionSpec as P


F32 = jnp.float32
BF = jnp.bfloat16
EPS = 1e-05
SIDE = 7
PITCH = 8
TAPS = 9
NARROW = 4
MESH = ("narrow", "wide")
VMEM_BYTES = 20 * 2**20


def dot(left, right):
    return jnp.dot(left, right, preferred_element_type=F32)


def dot_nt(left, right):
    return lax.dot_general(left, right, (((1,), (1,)), ((), ())), preferred_element_type=F32)


def dot_tn(left, right):
    return lax.dot_general(left, right, (((0,), (0,)), ((), ())), preferred_element_type=F32)


def position():
    n, w = lax.axis_index("narrow"), lax.axis_index("wide")
    return n, w // 2, w % 2


def run(kernel, operands, outs, scratch=(), flops=0):
    moved = sum(o.size * o.dtype.itemsize for o in (*operands, *outs))
    return pl.pallas_call(
        kernel,
        out_shape=outs,
        name=kernel.__name__,
        in_specs=[pl.BlockSpec(memory_space=pltpu.VMEM)] * len(operands),
        out_specs=[pl.BlockSpec(memory_space=pltpu.VMEM)] * len(outs),
        scratch_shapes=list(scratch),
        cost_estimate=pl.CostEstimate(flops=flops, bytes_accessed=moved, transcendentals=0),
        compiler_params=pltpu.CompilerParams(vmem_limit_bytes=VMEM_BYTES),
    )(*operands)


def arr(shape, dtype):
    return jax.ShapeDtypeStruct(shape, dtype)


def by_rows(rows, body, carry):
    return body(pl.ds(0, rows), carry)


def fold(values):
    total = values[0:8]
    for start in range(8, values.shape[0], 8):
        total = total + values[start : start + 8]
    return total


def zeros_acc(channels):
    return (jnp.zeros((8, channels), F32), jnp.zeros((8, channels), F32))


def column_sum(acc):
    return jnp.sum(acc, axis=0, keepdims=True)


def sigmoid(values):
    return 0.5 * jnp.tanh(0.5 * values) + 0.5


def coefficients(total, squares, inverse, gain, shift):
    mean = total * inverse
    spread = squares * inverse - mean * mean
    scale = lax.rsqrt(spread + EPS)
    slope = gain * scale
    return mean, scale, slope, shift - mean * slope


def wide_row(block, first, count=NARROW):
    return jnp.concatenate([block[first + k : first + k + 1] for k in range(count)], axis=1)


def row_of(block, first, index):
    rows = [jnp.where(index == k, block[first + k : first + k + 1], 0.0) for k in range(NARROW)]
    return rows[0] + rows[1] + rows[2] + rows[3]


def inverse_count(params, b, channels):
    row = params[b, 4:5, :]
    return row if channels == 128 else jnp.concatenate([row] * (channels // 128), axis=1)


def lane_block(index):
    return pl.ds(pl.multiple_of(index * 128, 128), 128)


def send_stats(message, first, second):
    for k in range(NARROW):
        message[k : k + 1, :] = first[:, 128 * k : 128 * k + 128]
        message[NARROW + k : NARROW + k + 1, :] = second[:, 128 * k : 128 * k + 128]


def repeat_first(message):
    block = message[0]
    for place in range(1, message.shape[0]):
        message[place] = block


def total_of(parts, index):
    total = parts[index]
    for place in range(NARROW, parts.shape[0], NARROW):
        total = total + parts[place + index]
    return total


def sum_parts(parts):
    total = parts[0]
    for place in range(1, parts.shape[0]):
        total = total + parts[place]
    return total


def place_columns(p0, p1, p2, p3, out):
    z = position()[1]
    for j, piece in enumerate((p0, p1, p2, p3)):
        out[:, lane_block((z - j) & 3)] = piece[...]


def first_product(x, *refs):
    pieces, (w_first, send_far, own_far, send_near, own_near) = refs[:-5], refs[-5:]
    n, z, y = position()
    if len(pieces) == 1:
        w_first[...] = pieces[0][...]
    else:
        rows = pieces[0].shape[0]
        for dy, piece in enumerate(pieces):
            w_first[pl.ds(pl.multiple_of((y ^ dy) * rows, rows), rows), :] = piece[...]
    for ref, m in ((send_far, 3), (own_far, 2), (send_near, 1), (own_near, 0)):
        ref[...] = dot(x[n ^ m], w_first[...]).astype(ref.dtype)


def first_join(own, near, far, mask, small, pre, message):
    b = position()[0]

    def body(ds, acc):
        values = own[ds, :] + near[ds, :].astype(F32) + far[ds, :].astype(F32)
        pre[ds, :] = values.astype(BF)
        kept = mask[b, ds, :] * values
        return acc[0] + fold(kept), acc[1] + fold(kept * values)

    sums = by_rows(own.shape[0], body, zeros_acc(own.shape[1]))
    send_stats(message, column_sum(sums[0]), column_sum(sums[1]))
    message[8:16, :] = small[...]


def middle_forward(pre0, pre1, pre2, pre3, sum0, sum1, sum2, sum3, mask, to_canvas, to_rows, weight,
                   hidden, pre, coef, message, params, active, spread, joined):
    n = position()[0]
    blocks = (sum0[...], sum1[...], sum2[...], sum3[...])
    for m, block in enumerate(blocks):
        params[n ^ m, 0:4, :] = block[8:12]
    for b in range(NARROW):
        params[b, 4:5, :] = 1.0 / blocks[0][12 + b : 13 + b]
        params[b, 5:8, :] = jnp.zeros((3, 128), F32)
    rows, places = pre0.shape[0], to_canvas.shape[0]
    img = places // (SIDE * PITCH)
    margin = img * (PITCH + 1)
    gain = jnp.concatenate([params[k, 0:1, :] for k in range(NARROW)], axis=1)
    shift = jnp.concatenate([params[k, 1:2, :] for k in range(NARROW)], axis=1)
    spread[0:margin, :] = jnp.zeros((margin, spread.shape[1]), F32)
    spread[margin + places :, :] = jnp.zeros((margin, spread.shape[1]), F32)
    line = img * PITCH
    for m, source in enumerate((pre0, pre1, pre2, pre3)):
        b = n ^ m
        block = blocks[m]
        mean, scale, slope, offset = coefficients(
            wide_row(block, 0), wide_row(block, NARROW), inverse_count(params, b, gain.shape[1]), gain, shift
        )
        for k, row in enumerate((mean, scale, slope, offset)):
            coef[m, k : k + 1, :] = row

        def activate(ds, carry):
            act = source[ds, :].astype(F32) * slope + offset
            active[ds, :] = (mask[b, ds, :] * act * sigmoid(act)).astype(BF)
            return carry

        by_rows(rows, activate, 0)
        hidden[m] = dot(to_canvas[...], active[...]).astype(BF)
        spread[margin : margin + places, :] = dot(hidden[m], weight[...])
        for top in range(SIDE):
            acc = None
            for tap in range(TAPS):
                start = margin + top * line + ((tap // 3 - 1) * PITCH + tap % 3 - 1) * img
                part = spread[start : start + line, 128 * tap : 128 * tap + 128]
                acc = part if acc is None else acc + part
            joined[top * line : (top + 1) * line, :] = acc.astype(BF)
        pre[m] = dot(to_rows[...], joined[...]).astype(BF)

        def collect(ds, acc):
            values = pre[m, ds, :].astype(F32)
            kept = mask[b, ds, :] * values
            return acc[0] + fold(kept), acc[1] + fold(kept * values)

        sums = by_rows(rows, collect, zeros_acc(128))
        message[0, 2 * m : 2 * m + 1, :] = column_sum(sums[0])
        message[0, 2 * m + 1 : 2 * m + 2, :] = column_sum(sums[1])
    repeat_first(message)


def last_forward(src0, src1, src2, src3, parts, params, mask, weight,
                 hidden, own, coef, pre, message):
    n = position()[0]
    rows = own.shape[0]
    sources = (src0, src1, src2, src3)
    blocks = [total_of(parts, n ^ i) for i in range(NARROW)]
    for m in range(NARROW):
        b = n ^ m
        for i in range(NARROW):
            j = m ^ i
            here = lane_block(n ^ i)
            mean, scale, slope, offset = coefficients(
                blocks[i][2 * j : 2 * j + 1], blocks[i][2 * j + 1 : 2 * j + 2], inverse_count(params, b, 128),
                params[n ^ i, 2:3, :], params[n ^ i, 3:4, :],
            )
            if m == 0:
                own[:, here] = sources[i][j]
                for k, row in enumerate((mean, scale, slope, offset)):
                    coef[k : k + 1, here] = row

            def activate(ds, carry):
                act = sources[i][j, ds, :].astype(F32) * slope + offset
                hidden[m, ds, here] = (mask[b, ds, :] * act * sigmoid(act)).astype(BF)
                return carry

            by_rows(rows, activate, 0)
        pre[m] = dot(hidden[m], weight[...])

        def collect(ds, acc):
            values = pre[m, ds, :]
            kept = mask[b, ds, :] * values
            return acc[0] + fold(kept), acc[1] + fold(kept * values)

        sums = by_rows(rows, collect, zeros_acc(pre.shape[2]))
        message[0, 2 * m : 2 * m + 1, :] = column_sum(sums[0])
        message[0, 2 * m + 1 : 2 * m + 2, :] = column_sum(sums[1])
    repeat_first(message)


def block_output(pre, x, cotangent, parts, params, gain, shift, mask, out, grad, coef, message):
    n = position()[0]
    rows, channels = pre.shape[1:]
    block = sum_parts(parts)
    for m in range(NARROW):
        b = n ^ m
        mean, scale, slope, offset = coefficients(
            block[2 * m : 2 * m + 1], block[2 * m + 1 : 2 * m + 2], inverse_count(params, b, channels), gain[...], shift[...]
        )
        for k, row in enumerate((mean, scale, slope, offset)):
            coef[m, k : k + 1, :] = row

        def body(ds, acc):
            values = pre[m, ds, :]
            inside = mask[b, ds, :]
            summed = values * slope + offset + x[b, ds, :].astype(F32)
            gate = sigmoid(summed)
            value = summed * gate
            out[b, ds, :] = (inside * value).astype(BF)
            local = inside * cotangent[b, ds, :].astype(F32) * (gate + value * (1.0 - gate))
            grad[m, ds, :] = local
            return acc[0] + fold(local), acc[1] + fold(local * values)

        sums = by_rows(rows, body, zeros_acc(channels))
        first, second = column_sum(sums[0]), column_sum(sums[1])
        message[0, 2 * m : 2 * m + 1, :] = first
        message[0, 2 * m + 1 : 2 * m + 2, :] = scale * (second - mean * first)
    repeat_first(message)


def last_backward(pre, grad, parts, params, coef, mask, weight,
                  grad_pre, send_far, own_far, send_near, own_near, level_sum, tilt_sum):
    n = position()[0]
    rows = pre.shape[1]
    block = sum_parts(parts)
    for s, ref in enumerate((level_sum, tilt_sum)):
        acc = block[s : s + 1]
        for m in range(1, NARROW):
            acc = acc + block[2 * m + s : 2 * m + s + 1]
        ref[...] = acc
    for m, ref in ((3, send_far), (2, own_far), (1, send_near), (0, own_near)):
        b = n ^ m
        mean, scale, slope = (coef[m, k : k + 1, :] for k in range(3))
        inverse = inverse_count(params, b, block.shape[1])
        level = block[2 * m : 2 * m + 1] * inverse
        tilt = block[2 * m + 1 : 2 * m + 2] * inverse
        level, tilt = level - mean * scale * tilt, scale * tilt

        def body(ds, carry):
            away = mask[b, ds, :] * (level + pre[m, ds, :] * tilt)
            grad_pre[m, ds, :] = (slope * (grad[m, ds, :] - away)).astype(BF)
            return carry

        by_rows(rows, body, 0)
        ref[...] = dot_nt(grad_pre[m], weight[...]).astype(ref.dtype)


def middle_join(own, near, far, pre, coef, mask, grad, own_q, near_q, far_q, message):
    b = position()[0]
    mean, scale, slope, offset = (coef[k : k + 1, :] for k in range(4))
    back = mean * scale

    def body(ds, acc):
        values = pre[ds, :].astype(F32)
        act = values * slope + offset
        gate = sigmoid(act)
        total = own[ds, :] + near[ds, :].astype(F32) + far[ds, :].astype(F32)
        local = total * mask[b, ds, :] * (gate * (1.0 + act * (1.0 - gate)))
        grad[ds, :] = local
        return acc[0] + fold(local), acc[1] + fold(local * (values * scale - back))

    sums = by_rows(own.shape[0], body, zeros_acc(own.shape[1]))
    send_stats(message.at[0], column_sum(sums[0]), column_sum(sums[1]))
    repeat_first(message)
    own_q[...] = grad[:, lane_block(b)].astype(BF)
    near_q[...] = grad[:, lane_block(b ^ 1)].astype(BF)
    far_q[0] = grad[:, lane_block(b ^ 2)].astype(BF)
    far_q[1] = grad[:, lane_block(b ^ 3)].astype(BF)


def middle_backward(grad, pre, parts, params, coef, mask, first_pre, first_coef, to_canvas, to_rows,
                    w0, w1, w2, w3, grad_first, message,
                    grad_pre, weight, gathered, canvas):
    n = position()[0]
    rows, places = grad.shape[0], to_canvas.shape[0]
    img = places // (SIDE * PITCH)
    margin = img * (PITCH + 1)
    block = sum_parts(parts)
    mean, scale, slope = (coef[k : k + 1, :] for k in range(3))
    inverse = inverse_count(params, n, grad.shape[1])
    level = wide_row(block, 0) * inverse
    tilt = wide_row(block, NARROW) * inverse
    level, tilt = level - mean * scale * tilt, scale * tilt

    def body(ds, carry):
        away = mask[n, ds, :] * (level + pre[ds, :].astype(F32) * tilt)
        grad_pre[ds, :] = (slope * (grad[ds, :] - away)).astype(BF)
        return carry

    by_rows(rows, body, 0)
    for j, piece in enumerate((w0, w1, w2, w3)):
        for tap in range(TAPS):
            weight[tap, :, lane_block(n ^ j)] = piece[:, 128 * tap : 128 * tap + 128]
    canvas[...] = dot(to_canvas[...], grad_pre[...]).astype(BF).astype(F32)
    gathered[...] = jnp.zeros_like(gathered)
    for tap in range(TAPS):
        start = margin + ((tap // 3 - 1) * PITCH + tap % 3 - 1) * img
        gathered[start : start + places, :] += dot_nt(canvas[...].astype(BF), weight[tap])
    canvas[...] = gathered[margin : margin + places, :]
    grad_pre[...] = dot(to_rows[...], canvas[...].astype(BF)).astype(BF)
    mean, scale, slope, offset = (first_coef[0, k : k + 1, :] for k in range(4))
    back = mean * scale

    def finish(ds, acc):
        values = first_pre[ds, :].astype(F32)
        act = values * slope + offset
        gate = sigmoid(act)
        local = grad_pre[ds, :].astype(F32) * mask[n, ds, :] * (gate * (1.0 + act * (1.0 - gate)))
        grad_first[ds, :] = local.astype(BF)
        return acc[0] + fold(local), acc[1] + fold(local * (values * scale - back))

    sums2 = by_rows(rows, finish, zeros_acc(grad.shape[1]))
    send_stats(message, column_sum(sums2[0]), column_sum(sums2[1]))


def first_weight(g0, g1, g2, g3, p0, p1, p2, p3, sum0, sum1, sum2, sum3, params, coef, mask, x,
                 level_sum, tilt_sum, grad_pre, *refs):
    outs, acc = refs[:-1], refs[-1]
    n, z, y = position()
    rows, channels = g0.shape
    blocks = (sum0[...], sum1[...], sum2[...], sum3[...])
    every = blocks[0] + blocks[1] + blocks[2] + blocks[3]
    for m, (g, pre) in enumerate(((g0, p0), (g1, p1), (g2, p2), (g3, p3))):
        b = n ^ m
        block = blocks[m]
        mean, scale, slope = (coef[m, k : k + 1, :] for k in range(3))
        inverse = inverse_count(params, b, channels)
        level = wide_row(block, 0) * inverse
        tilt = wide_row(block, NARROW) * inverse
        level, tilt = level - mean * scale * tilt, scale * tilt
        away = mask[b] * (level + pre[...].astype(F32) * tilt)
        grad_pre[m] = (slope * (g[...].astype(F32) - away)).astype(BF)
    total = dot_tn(x[n], grad_pre[0])
    for m in range(1, NARROW):
        total = total + dot_tn(x[n ^ m], grad_pre[m])
    acc[...] = total
    if len(outs) == 1:
        outs[0][...] = acc[...]
    else:
        half = acc.shape[0] // 2
        for ref, h in zip(outs, (y, 1 - y)):
            top = pl.multiple_of(h * half, half)
            for j in range(NARROW):
                block = acc[pl.ds(top, half), lane_block(n ^ j)]
                ref[:, 128 * j : 128 * j + 128] = block.astype(ref.dtype)
    level_sum[...] = row_of(every, 0, n)
    tilt_sum[...] = row_of(every, NARROW, n)


def input_gradient(grad_pre, weight, grad, out):
    n = position()[0]
    for m in range(NARROW):
        out[n ^ m] = dot_nt(grad_pre[m], weight[...]) + grad[m]


def last_weight(hidden, grad_pre, *refs):
    acc = refs[-1]
    for m in range(NARROW):
        product = dot_tn(hidden[m], grad_pre[m])
        if m == 0:
            acc[...] = product
        else:
            acc[...] += product
    hand_out(acc, refs[:-1])


def hand_out(acc, outs):
    if len(outs) == 1:
        outs[0][...] = acc[...]
        return
    _, z, y = position()
    own, away = outs
    rows = acc.shape[0] // 8
    for j in range(4):
        place = pl.ds(j * rows, rows)
        for ref, dy in ((own, 0), (away, 1)):
            top = ((z ^ j) * 2 + (y ^ dy)) * rows
            ref[place, :] = acc[pl.ds(pl.multiple_of(top, rows), rows), :].astype(ref.dtype)


def middle_weight(hidden, q0, q1, far, last, pre, sum0, sum1, sum2, sum3, norm, params, mask, to_canvas,
                  level_sum, tilt_sum, *refs):
    outs, (acc, shifted, canvases) = refs[:-3], refs[-3:]
    n = position()[0]
    places = to_canvas.shape[0]
    img = places // (SIDE * PITCH)
    margin = img * (PITCH + 1)
    norms = total_of(norm, n)
    blocks = (sum0[...], sum1[...], sum2[...], sum3[...])
    every = blocks[0] + blocks[1] + blocks[2] + blocks[3]
    level_sum[...] = row_of(every, 0, n)
    tilt_sum[...] = row_of(every, NARROW, n)
    for m, piece in enumerate((q0[...], q1[...], far[0], last[1])):
        b = n ^ m
        inverse = inverse_count(params, b, 128)
        mean, scale, slope, _ = coefficients(
            norms[2 * m : 2 * m + 1], norms[2 * m + 1 : 2 * m + 2], inverse, params[n, 2:3, :], params[n, 3:4, :]
        )
        block = blocks[m]
        level = row_of(block, 0, n) * inverse
        tilt = row_of(block, NARROW, n) * inverse
        level, tilt = level - mean * scale * tilt, scale * tilt
        away = mask[b] * (level + pre[m].astype(F32) * tilt)
        grad_pre = (slope * (piece.astype(F32) - away)).astype(BF)
        canvas = canvases.at[m]
        canvas[0:margin, :] = jnp.zeros((margin, 128), F32)
        canvas[margin + places :, :] = jnp.zeros((margin, 128), F32)
        canvas[margin : margin + places, :] = dot(to_canvas[...], grad_pre)
        for tap in range(TAPS):
            start = margin - ((tap // 3 - 1) * PITCH + tap % 3 - 1) * img
            here = slice(m * places, (m + 1) * places)
            shifted[here, 128 * tap : 128 * tap + 128] = canvas[start : start + places, :].astype(BF)
    acc[...] = dot_tn(hidden[...].reshape(NARROW * places, hidden.shape[2]), shifted[...])
    hand_out(acc, outs)


def gather_middle(near, far, out):
    _, z, y = position()
    rows = out.shape[0] // 8
    for dy, stack in enumerate((near, far)):
        for j in range(4):
            here = pl.ds(pl.multiple_of(((z ^ j) * 2 + (y ^ dy)) * rows, rows), rows)
            for tap in range(TAPS):
                top = (j * TAPS + tap) * rows
                out[here, 128 * tap : 128 * tap + 128] = stack[top : top + rows, :]


def gather_last(near, far, out):
    _, z, y = position()
    rows = out.shape[0] // 8
    for dy, stack in enumerate((near, far)):
        for j in range(4):
            here = pl.ds(pl.multiple_of(((z ^ j) * 2 + (y ^ dy)) * rows, rows), rows)
            out[here, :] = stack[j * rows : (j + 1) * rows, :]


def merge_first(own, away, keep, near, far):
    parts = [own[:, 128 * i : 128 * i + 128] + away[:, 128 * i : 128 * i + 128].astype(F32) for i in range(NARROW)]
    keep[...] = parts[0]
    near[...] = parts[1].astype(BF)
    far[0] = parts[2].astype(BF)
    far[1] = parts[3].astype(BF)


def sort_first(own, near, far, last, keep, *refs):
    sends, pieces = refs[:-1], refs[-1]
    n, z, _ = position()
    for i, piece in enumerate((own[...], near[...], far[0], last[1])):
        pieces[i] = piece.astype(F32)
    keep[...] = pieces[n ^ z]
    for j, send in enumerate(sends):
        send[...] = pieces[n ^ z ^ (j + 1)].astype(BF)


def finish_first(keep, p1, p2, p3, out):
    out[...] = keep[...] + p1[...].astype(F32) + p2[...].astype(F32) + p3[...].astype(F32)


def add_tiles(*refs):
    total = refs[0][...]
    for ref in refs[1:-1]:
        total = total + ref[...]
    refs[-1][...] = total


def add_parts(parts, out):
    out[...] = sum_parts(parts)


def merge_wide(own, away, own_last, away_last, keep, keep_last, *sends):
    rows, middle = keep.shape
    keep[...] = own[0:rows, :] + away[0:rows, :].astype(F32)
    keep_last[...] = own_last[0:rows, :] + away_last[0:rows, :].astype(F32)
    for j, send in enumerate(sends):
        here = slice((j + 1) * rows, (j + 2) * rows)
        send[:, 0:middle] = (own[here, :] + away[here, :].astype(F32)).astype(BF)
        send[:, middle:] = (own_last[here, :] + away_last[here, :].astype(F32)).astype(BF)


def finish_wide(keep, keep_last, p1, p2, p3, out, out_last):
    middle = keep.shape[1]
    for tap in range(TAPS):
        here = slice(128 * tap, 128 * tap + 128)
        out[tap] = keep[:, here] + p1[:, here].astype(F32) + p2[:, here].astype(F32) + p3[:, here].astype(F32)
    out_last[...] = (
        keep_last[...] + p1[:, middle:].astype(F32) + p2[:, middle:].astype(F32) + p3[:, middle:].astype(F32)
    )


def exchange(message):
    return lax.all_to_all(message, ("wide", "narrow"), 0, 0, tiled=True)


def swap_core(values):
    return lax.ppermute(values, "narrow", [(i, i ^ 1) for i in range(NARROW)])


def swap_chip(values):
    return lax.ppermute(values, "narrow", [(i, i ^ 2) for i in range(NARROW)])


def swap_wide(values, step, wide):
    return lax.ppermute(values, "wide", [(i, i ^ step) for i in range(wide)])


def after(value, *others):
    return lax.optimization_barrier((value, *others))[0]


def from_all(values, *others):
    far = swap_chip(values)
    if others:
        return values, swap_core(values), far, swap_core(after(far, *others))
    return values, swap_core(values), far, swap_core(far)


def add(*tiles):
    return run(add_tiles, tiles, [arr(tiles[0].shape, F32)])[0]


def sum_wide(values, wide, beside=(), late=()):
    if wide == 8:
        values = add(after(values, *beside) if beside else values, swap_wide(values, 1, wide))
        parts = [swap_wide(values, step, wide) for step in (2, 4, 6)]
        total = add(after(values, *late) if late else values, *parts)
        return values, total
    step = 1
    while step < wide:
        values = add(values, swap_wide(values, step, wide))
        step *= 2
    return values, values


def reduce_narrow(send_far, own_far, send_near, own_near, *others):
    got_far = swap_core(send_far)
    got_near = swap_core(send_near)
    joined = (own_far + got_far.astype(F32)).astype(BF)
    if others:
        joined = after(joined, *others)
    return (own_near, got_near, swap_chip(joined)), joined


def transposed_steps():
    steps = []
    for j in range(NARROW):
        pairs = []
        for k in range(NARROW):
            for z in range(4):
                for y in range(2):
                    pairs.append((k * 8 + 2 * z + y, z * 8 + 2 * ((k + j) % 4) + y))
        steps.append(pairs)
    return steps


def on_device(inputs, sides, w_first, w_middle, w_last, gain_first, shift_first, gain_middle, shift_middle,
              gain_last, shift_last, cotangent, *, wide):
    micro, rows, low = inputs.shape
    img = sides.shape[1]
    mid = w_last.shape[0] * wide
    cols = w_first.shape[1]
    places = img * SIDE * PITCH
    direct = wide == 8
    n = lax.axis_index("narrow")
    w = lax.axis_index("wide")

    spots = jnp.arange(rows, dtype=jnp.int32)
    spot_y, spot_x, spot_img = spots % 49 // 7, spots % 7, spots // 49

    def mask_of(limits):
        limits = jnp.repeat(limits, 49, axis=1)
        return ((spot_y[None] < limits) & (spot_x[None] < limits)).astype(F32)[:, :, None]

    place = (spot_y * PITCH + spot_x) * img + spot_img
    to_canvas = (jnp.arange(places, dtype=jnp.int32)[:, None] == place[None, :]).astype(BF)
    to_rows = (place[:, None] == jnp.arange(places, dtype=jnp.int32)[None, :]).astype(BF)

    if direct:
        steps = transposed_steps()
        share = w_last.shape[0]
        packed = w_middle.reshape(TAPS * share, 128)
        middle_near = [packed] + [swap_wide(packed, 2 * j, wide) for j in range(1, 4)]
        first_pieces = [lax.ppermute(w_first, MESH, pairs) for pairs in steps]
        first_half = run(place_columns, first_pieces, [arr((w_first.shape[0], mid), BF)])[0]
        first_pieces = [first_half, swap_wide(first_half, 1, wide)]
    else:
        first_all = lax.all_gather(lax.all_gather(w_first, "narrow", axis=1, tiled=True), "wide", axis=0, tiled=True)
        first_pieces = [lax.dynamic_slice_in_dim(first_all, n * low, low, 0)]
        middle_slice = lax.all_gather(w_middle, "wide", axis=2, tiled=True)
        middle_slice = middle_slice.reshape(TAPS, mid, 128).transpose(1, 0, 2).reshape(mid, TAPS * 128)
        last_slice = lax.all_gather(w_last, "wide", axis=0, tiled=True)

    counts = jnp.sum((sides * sides).astype(F32), axis=1)
    small = jnp.concatenate(
        [jnp.stack([gain_first, shift_first, gain_middle, shift_middle]) * (1.0 / wide),
         jnp.broadcast_to(counts[:, None], (micro, 128))], axis=0
    )

    tile = arr((8, 128), F32)
    across = arr((wide, 8, low), F32)
    flat = arr((rows, mid), BF)
    flat32 = arr((rows, mid), F32)

    w_rows, send_far, own_far, send_near, own_near = run(
        first_product, (inputs, *first_pieces),
        [arr((low, mid), BF), flat, flat32, flat, flat32], flops=2 * micro * rows * low * mid,
    )
    joined, begun = reduce_narrow(send_far, own_far, send_near, own_near, *(middle_near[:2] if direct else ()))
    if direct:
        middle_near = jnp.concatenate([after(middle_near[0], begun)] + middle_near[1:], axis=0)
        middle_far = swap_wide(middle_near, 1, wide)
    mask = mask_of(after(sides, begun))
    beside = ()
    if direct:
        held = after(w_last, middle_near)
        last_near = jnp.concatenate([held] + [swap_wide(held, 2 * j, wide) for j in range(1, 4)], axis=0)
        beside = (middle_far, last_near)
    pre_one, message = run(first_join, (*joined, mask, small), [flat, arr((16, 128), F32)])
    begun, total = sum_wide(message, wide, beside=beside)
    if direct:
        last_far = swap_wide(after(last_near, total), 1, wide)
    pre_ones = from_all(pre_one, total)
    sums_one = from_all(total)
    if direct:
        middle_slice = run(gather_middle, (middle_near, middle_far), [arr((mid, TAPS * 128), BF)])[0]

    hidden_one, pre_two, coef_one, message, params = run(
        middle_forward, (*pre_ones, *sums_one, mask, to_canvas, to_rows, middle_slice),
        [arr((micro, places, mid), BF), arr((micro, rows, 128), BF), arr((micro, 8, mid), F32), arr((wide * NARROW, 8, 128), F32), arr((NARROW, 8, 128), F32)],
        [pltpu.VMEM((rows, mid), BF), pltpu.VMEM((places + 2 * img * (PITCH + 1), TAPS * 128), F32), pltpu.VMEM((places, 128), BF)],
        flops=2 * micro * places * mid * TAPS * 128,
    )
    if direct:
        last_slice = run(gather_last, (last_near, last_far), [arr((mid, low), BF)])[0]
    if direct:
        message = after(message, last_far)
    parts_two = exchange(message)
    pre_twos = from_all(pre_two, parts_two)
    held = after(middle_slice, pre_twos[3], parts_two)
    middle_away = swap_chip(held)

    hidden_two, own_two, coef_two, pre_three, message = run(
        last_forward, (*pre_twos, parts_two, params, mask, last_slice),
        [arr((micro, rows, mid), BF), flat, arr((8, mid), F32), arr((micro, rows, low), F32), across],
        flops=2 * micro * rows * low * mid,
    )
    parts_three = lax.all_to_all(message, "wide", 0, 0, tiled=True)
    block_out, grad_sum, coef_three, message = run(
        block_output,
        (pre_three, inputs, cotangent, parts_three, params, gain_last[None], shift_last[None], mask),
        [arr(inputs.shape, BF), arr((micro, rows, low), F32), arr((micro, 8, low), F32), across],
    )
    parts_four = lax.all_to_all(message, "wide", 0, 0, tiled=True)

    grad_three, send_far, own_far, send_near, own_near, level_three, tilt_three = run(
        last_backward, (pre_three, grad_sum, parts_four, params, coef_three, mask, last_slice),
        [arr((micro, rows, low), BF), flat, flat32, flat, flat32, arr((1, low), F32), arr((1, low), F32)],
        flops=2 * micro * rows * low * mid,
    )
    joined, begun = reduce_narrow(send_far, own_far, send_near, own_near, middle_away)
    grad_three = after(grad_three, begun)

    def handed(channels):
        if direct:
            return [arr((mid // 2, channels), F32), arr((mid // 2, channels), BF)]
        return [arr((mid, channels), F32)]

    last_sum = run(
        last_weight, (hidden_two, grad_three), handed(low), [pltpu.VMEM((mid, low), F32)],
        flops=2 * micro * rows * low * mid,
    )
    slim = arr((rows, 128), BF)
    row = arr((1, 128), F32)
    if direct:
        got_last_sum = swap_wide(last_sum[1], 1, wide)
        joined = (after(joined[0], got_last_sum), *joined[1:])
    grad_two, own_q, near_q, far_q, message = run(
        middle_join, (*joined, own_two, coef_two, mask), [flat32, slim, slim, arr((2, rows, 128), BF), arr((wide, 8, 128), F32)]
    )
    got_far = swap_chip(far_q)
    middle_slices = (middle_slice, swap_core(held), middle_away, swap_core(middle_away))
    parts_five = lax.all_to_all(after(message, *middle_slices), "wide", 0, 0, tiled=True)
    total_five = run(add_parts, (parts_five,), [tile])[0]
    near_q, got_far = lax.optimization_barrier((near_q, got_far, parts_five))[:2]
    got_near, got_last = swap_core(near_q), swap_core(got_far)
    sums_five = from_all(total_five)

    grad_one, message = run(
        middle_backward,
        (grad_two, own_two, parts_five, params, coef_two, mask, pre_one, coef_one, to_canvas, to_rows, *middle_slices),
        [flat, tile],
        [pltpu.VMEM((rows, mid), BF), pltpu.VMEM((TAPS, mid, mid), BF),
         pltpu.VMEM((places + 2 * img * (PITCH + 1), mid), F32), pltpu.VMEM((places, mid), F32)],
        flops=2 * places * mid * TAPS * mid,
    )
    level_two, tilt_two, *middle_sum = run(
        middle_weight,
        (hidden_one, own_q, got_near, got_far, got_last, pre_two, *sums_five, parts_two, params, mask, to_canvas),
        [row, row, *handed(TAPS * 128)],
        [pltpu.VMEM((mid, TAPS * 128), F32), pltpu.VMEM((micro * places, TAPS * 128), BF),
         pltpu.VMEM((micro, places + 2 * img * (PITCH + 1), 128), F32)],
        flops=2 * micro * places * mid * TAPS * 128,
    )
    begun, total = sum_wide(message, wide, beside=middle_sum)
    grad_ones = from_all(after(grad_one, sums_five[2]), total)
    sums_six = from_all(total)
    if direct:
        got_middle = swap_wide(after(middle_sum[1], begun), 1, wide)

    out_first = [arr((low // 2, mid), F32), arr((low // 2, mid), BF)] if direct else [arr((low, mid), F32)]
    level_one, tilt_one, grad_pre_one, *first_sum = run(
        first_weight,
        (*grad_ones, *pre_ones, *sums_six, params, coef_one, mask, inputs),
        [row, row, arr((micro, rows, mid), BF), *out_first], [pltpu.VMEM((low, mid), F32)],
        flops=2 * micro * rows * low * mid,
    )
    input_grad = run(
        input_gradient, (grad_pre_one, w_rows, grad_sum), [arr((micro, rows, low), F32)],
        flops=2 * micro * rows * low * mid,
    )[0]

    if direct:
        got_first = swap_wide(after(first_sum[1], got_middle), 1, wide)
        channels = TAPS * 128
        keep, keep_last, *sends = run(
            merge_wide, (middle_sum[0], after(got_middle, first_sum[1]), last_sum[0], got_last_sum),
            [arr((share, channels), F32), arr((share, low), F32)] + [arr((share, channels + low), BF)] * 3,
        )
        parts = [swap_wide(send, 2 * j + 2, wide) for j, send in enumerate(sends)]
        piece, half = arr((low // 2, cols), BF), arr((low // 2, cols), F32)
        keep_first, near, far = run(merge_first, (first_sum[0], after(got_first, parts[0])), [half, piece, arr((2, low // 2, cols), BF)])
        far = after(swap_chip(far), *parts[0:2])
        keep_first, *sends = run(
            sort_first, (keep_first, swap_core(near), far, swap_core(far)), [half, piece, piece, piece],
            [pltpu.VMEM((NARROW, low // 2, cols), F32)],
        )
        arrived = [swap_wide(send, 2 * j + 2, wide) for j, send in enumerate(sends)]
        grad_first = run(finish_first, (keep_first, *arrived), [half])[0]
        grad_middle, grad_last = run(
            finish_wide, (keep, keep_last, *parts),
            [arr((TAPS, share, 128), F32), arr((share, low), F32)],
        )
        grad_middle = grad_middle.reshape(3, 3, share, 128)
    else:
        grad_last = lax.psum_scatter(last_sum[0], "wide", scatter_dimension=0, tiled=True)
        grad_middle = lax.psum_scatter(middle_sum[0], "wide", scatter_dimension=0, tiled=True)
        share = grad_middle.shape[0]
        grad_middle = grad_middle.reshape(share, TAPS, 128).transpose(1, 0, 2).reshape(3, 3, share, 128)
        whole = lax.psum(first_sum[0], "wide")
        whole = lax.all_gather(whole, "narrow", axis=0, tiled=True)
        share = whole.shape[0] // wide
        grad_first = lax.dynamic_slice(whole, (w * share, n * cols), (share, cols))
    return (
        block_out, input_grad, grad_first, grad_middle, grad_last,
        tilt_one[0], level_one[0], tilt_two[0], level_two[0], tilt_three[0], level_three[0],
    )


def solution(mesh):
    wide = mesh.shape["wide"]
    placed = (
        P(None, "wide", "narrow"),
        P(None, "wide"),
        P("wide", "narrow"),
        P(None, None, "wide", "narrow"),
        P("wide", "narrow"),
        P("narrow"),
        P("narrow"),
        P("narrow"),
        P("narrow"),
        P("narrow"),
        P("narrow"),
        P(None, "wide", "narrow"),
    )
    return jax.shard_map(
        lambda *arrays: on_device(*arrays, wide=wide),
        mesh=mesh,
        in_specs=placed,
        out_specs=(
            P(None, "wide", "narrow"),
            P(None, "wide", "narrow"),
            P("wide", "narrow"),
            P(None, None, "wide", "narrow"),
            P("wide", "narrow"),
            P("narrow"),
            P("narrow"),
            P("narrow"),
            P("narrow"),
            P("narrow"),
            P("narrow"),
        ),
        check_vma=False,
    )
```
